128 devices in a mesh: gx: 8 (over x, core), gy: 16 (over y, z).
Axes of the slice: x: 4, y: 4, z: 4, core: 2. Of those that a mesh axis runs over, the one named last changes fastest.
Arguments:
- concentration: float32 [768, 5, 32768], P(('gx', 'gy')), may hold values from 0.05 to 3
- neighbours: int32 [768, 6], P(('gx', 'gy')), may hold values from -1 to 767, as said below
- source_slot: int32 [768], P(('gx', 'gy')), may hold values from -1 to 767, as said below
- mobility: float32 [5], replicated, may hold values from 0.3 to 2
- fermi_gain: float32 [5], replicated, may hold values from 0.3 to 3
- rates: float32 [5], replicated, may hold values from 0.05 to 0.5
Outputs:
- moved: float32 [768, 5, 32768], P(('gx', 'gy'))
The draws below stay inside these ranges and needn't reach their ends.
Inputs may be any that keep to these rules, and one draw needn't show every extreme that they name: neighbours: each entry is -1 or a slot on the same device or on a device next to it along gx or along gy (same index on the other axis); every slot that source_slot names has neighbours that name only such slots that source_slot names too or -1. source_slot: each entry is -1 or a slot on the same device or on a device next to it along gx or along gy; no slot is named twice; only slots below 2 of a device are other than -1; at most 1 slots of one device name slots of one other device, and some device names exactly 1 of a neighbour's.
All inputs are finite; a program needn't handle non-finite values.
Results may differ from the reference program's by a relative error of at most 0.0003.
Values sent between devices are 32-bit elements; how exact they have to be, the bound alone decides.
A program may use at most 192 MiB of HBM per device.

```python
import math
import jax
import jax.numpy as jnp
from jax import lax

B = 32
SPECIES = 5
SWEEPS = 3
KEEP = 2
MOVE = 1
CAP = 6
PATCHES = 768
CELLS = 32768
N_GX = 8
N_GY = 16


DIRECTIONS = ((-1, 0), (1, 0), (0, -1), (0, 1))


def plan_layout(key):
    layout_key = jax.random.fold_in(key, 4099)
    shift_key, light_key, order_key = jax.random.split(layout_key, 3)
    device_count = N_GX * N_GY
    device_ids = jnp.arange(device_count, dtype=jnp.int32)
    column_index = device_ids // N_GY
    row_index = device_ids % N_GY
    offset = jax.random.randint(shift_key, (), 0, 5)
    crowded = (column_index + 2 * row_index + offset) % 5 == 0
    present = jnp.stack([(column_index + step_x >= 0) & (column_index + step_x < N_GX) & (row_index + step_y >= 0) & (row_index + step_y < N_GY) for step_x, step_y in DIRECTIONS], axis=1)
    neighbour_ids = jnp.stack([jnp.clip(column_index + step_x, 0, N_GX - 1) * N_GY + jnp.clip(row_index + step_y, 0, N_GY - 1) for step_x, step_y in DIRECTIONS], axis=1).astype(jnp.int32)
    light_live = jax.random.randint(light_key, (device_count,), 1, KEEP)
    live = jnp.where(crowded, KEEP + MOVE * jnp.sum(present.astype(jnp.int32), axis=1), light_live).astype(jnp.int32)

    def shuffle(device_key):
        return jax.random.permutation(device_key, CAP)
    home = jax.vmap(shuffle)(jax.random.split(order_key, device_count)).astype(jnp.int32)
    return (device_ids, crowded, present, neighbour_ids, live, home)


def draw_source_slot(key, part):
    device_ids, crowded, present, neighbour_ids, live, home = plan_layout(key)
    slots = jnp.arange(CAP, dtype=jnp.int32)
    kept = jnp.where(crowded, KEEP, live)
    result = jnp.where(slots[None, :] < kept[:, None], device_ids[:, None] * CAP + home, -1)
    for direction in range(4):
        helper_device = neighbour_ids[:, direction]
        receives = present[:, direction] & crowded[helper_device] & jnp.logical_not(crowded)
        backward = direction ^ 1
        rank = jnp.sum(present[helper_device][:, :backward].astype(jnp.int32), axis=1)
        logical = KEEP + rank[:, None] * MOVE + (slots[None, :] - live[:, None])
        within = receives[:, None] & (slots[None, :] >= live[:, None]) & (slots[None, :] < live[:, None] + MOVE)
        position = jnp.take_along_axis(home[helper_device], jnp.clip(logical, 0, CAP - 1), axis=1)
        result = jnp.where(within, helper_device[:, None] * CAP + position, result)
    return result.reshape(-1).astype(jnp.int32)


def draw_neighbours(key, part):
    device_ids, crowded, present, neighbour_ids, live, home = plan_layout(key)
    device_count = N_GX * N_GY
    face_key = jax.random.fold_in(key, 8191)
    heading_key, slot_key = jax.random.split(face_key, 2)
    heading = jax.random.randint(heading_key, (device_count, CAP * 6), 0, 6)
    candidates = jnp.concatenate([device_ids[:, None], neighbour_ids], axis=1)
    exists = jnp.concatenate([jnp.ones((device_count, 1), dtype=bool), present], axis=1)
    clipped = jnp.minimum(heading, 4)
    target = jnp.take_along_axis(candidates, clipped, axis=1)
    valid = (heading < 5) & jnp.take_along_axis(exists, clipped, axis=1)
    raw = jax.random.randint(slot_key, (device_count, CAP * 6), 0, 1 << 20)
    logical = raw % live[target]
    position = home[target, logical]
    result = jnp.where(valid, target * CAP + position, -1)
    return result.reshape(device_count * CAP, 6).astype(jnp.int32)


def steps_of(rng, shape, cuts, smallest, high):
    gain, own = 1.0, jax.random.fold_in(rng, 6)
    for dim, shards_of in cuts:
        draws = jnp.exp(jax.random.uniform(jax.random.fold_in(own, dim), (shards_of,), jnp.float32, smallest / len(cuts), high / len(cuts)))
        gain = gain * jnp.repeat(draws, shape[dim] // shards_of).reshape([-1 if axis == dim else 1 for axis in range(len(shape))])
    return gain


def setup_inputs(seed: int = 0) -> dict:
    key_of = jax.random.split(jax.random.key(seed), 7)
    return {
        "concentration": jnp.clip(jnp.exp(math.log(3.0) - 4.0943445 * jax.random.uniform(key_of[0], (PATCHES, SPECIES, CELLS), jnp.float32) ** steps_of(key_of[0], (PATCHES, SPECIES, CELLS), ((0, 128),), -0.2, 0.2)), 0.05, 3.0),
        "neighbours": draw_neighbours(jax.random.fold_in(key_of[6], 71), 0),
        "source_slot": draw_source_slot(jax.random.fold_in(key_of[6], 71), 0),
        "mobility": jnp.clip(jnp.exp(jax.random.uniform(key_of[3], (SPECIES,), jnp.float32, math.log(0.3), math.log(2.0))), 0.3, 2.0),
        "fermi_gain": jnp.clip(jnp.exp(jax.random.uniform(key_of[4], (SPECIES,), jnp.float32, math.log(0.3), math.log(3.0))), 0.3, 3.0),
        "rates": jnp.clip(jnp.exp(jax.random.uniform(key_of[5], (5,), jnp.float32, math.log(0.05), math.log(0.5))), 0.05, 0.5),
    }


OPPOSITE = (1, 0, 3, 2, 5, 4)

def faces_of(blocks):
    last = blocks.shape[-1] - 1
    return jnp.stack([blocks[..., 0, :, :], blocks[..., last, :, :], blocks[..., :, 0, :], blocks[..., :, last, :], blocks[..., :, :, 0], blocks[..., :, :, last]], axis=-4)

def neighbour_sum(iterate, ghosts):
    lower_x = jnp.concatenate([ghosts[0][:, None], iterate[:, :-1]], axis=1)
    upper_x = jnp.concatenate([iterate[:, 1:], ghosts[1][:, None]], axis=1)
    lower_y = jnp.concatenate([ghosts[2][:, :, None], iterate[:, :, :-1]], axis=2)
    upper_y = jnp.concatenate([iterate[:, :, 1:], ghosts[3][:, :, None]], axis=2)
    lower_z = jnp.concatenate([ghosts[4][..., None], iterate[..., :-1]], axis=3)
    upper_z = jnp.concatenate([iterate[..., 1:], ghosts[5][..., None]], axis=3)
    return lower_x + upper_x + lower_y + upper_y + lower_z + upper_z

def smooth(current, ghosts, mobility, fermi_gain, rates):
    dopant_sum = current[0] + current[3] + current[4]
    half_total = 0.5 * dopant_sum
    electrons = half_total + jnp.sqrt(half_total * half_total + 1.0)
    gain_column = fermi_gain[:, None, None, None]
    spread = mobility[:, None, None, None] * (1.0 + gain_column * electrons[None]) / (1.0 + gain_column)
    dopant, interstitial, vacancy, pair_inter, pair_vacancy = (current[0], current[1], current[2], current[3], current[4])
    forming_ai = rates[0] * dopant * interstitial - rates[1] * pair_inter
    forming_av = rates[2] * dopant * vacancy - rates[3] * pair_vacancy
    recombine = rates[4] * (interstitial * vacancy - 1.0)
    source = jnp.stack([dopant - forming_ai - forming_av, interstitial - forming_ai - recombine, vacancy - forming_av - recombine, pair_inter + forming_ai, pair_vacancy + forming_av], axis=0)
    diagonal = 1.0 + 6.0 * spread
    iterate = current
    for repeat in range(SWEEPS):
        iterate = (source + spread * neighbour_sum(iterate, ghosts)) / diagonal
    return iterate

def reference(concentration, neighbours, source_slot, mobility, fermi_gain, rates):
    patches = concentration.shape[0]
    blocks = concentration.reshape(patches, SPECIES, B, B, B)
    face_table = faces_of(blocks)
    opposite = jnp.array(OPPOSITE, jnp.int32)
    face_ids = jnp.arange(6, dtype=jnp.int32)

    def one_slot(source):
        patch_index = jnp.maximum(source, 0)
        neighbour_row = neighbours[patch_index]
        remote = face_table[jnp.maximum(neighbour_row, 0), opposite]
        own_layers = face_table[patch_index, face_ids]
        ghosts = jnp.where((neighbour_row >= 0)[:, None, None, None], remote, own_layers)
        swept = smooth(blocks[patch_index], ghosts, mobility, fermi_gain, rates)
        swept = jnp.where(source >= 0, swept, jnp.zeros_like(swept))
        return swept.reshape(SPECIES, B * B * B)
    return lax.map(one_slot, source_slot)
```

```python
import functools

import jax
import jax.numpy as jnp
from jax import lax
from jax.experimental import pallas as pl
from jax.experimental.pallas import tpu as pltpu
from jax.sharding import PartitionSpec as P

B = 32
SPECIES = 5
SWEEPS = 3
KEEP = 2
MOVE = 1
CAP = 6
ROWS = 256
ROOM = 6
MESH = pl.DeviceIdType.MESH

NEAR = ((-1, 0), (1, 0), (0, -1), (0, 1))
FAR = ((-2, 0), (2, 0), (0, -2), (0, 2), (-1, -1), (-1, 1), (1, -1), (1, 1))
AROUND = NEAR + FAR
ORDER = (2, 3, 0, 1)
PLACE = {(0, 0): 0, **{step: i + 1 for i, step in enumerate(AROUND)}}


def iota(shape, dim):
    return lax.broadcasted_iota(jnp.int32, shape, dim)


def exchange_kernel(
    nx, ny,
    conc, nbr_s, src_s, nbr_v, src_v,
    landp, landg, ghost_out, flag_out,
    raw, dense, own_faces, meta, table, table_s, sendp, sendf, landf, sendg, flags,
    in_sem, meta_ss, meta_rs, tab_sem, p_ss, p_rs, f_ss, f_rs, g_ss, g_rs, fl_ss, fl_rs,
):
    gx, gy = lax.axis_index("gx"), lax.axis_index("gy")
    me = gx * ny + gy

    def inside(step):
        x, y = gx + step[0], gy + step[1]
        return (x >= 0) & (x < nx) & (y >= 0) & (y < ny)

    def at(step):
        return (gx + step[0], gy + step[1])

    load = pltpu.make_async_copy(conc, raw, in_sem)
    load.start()

    row, col = gy // 4, gy % 4
    ring = (
        [((gx + k) % nx, gy) for k in range(1, nx)],
        [(gx, ((row + k) % 4) * 4 + col) for k in range(1, 4)],
        [(gx, row * 4 + (col + k) % 4) for k in range(1, 4)],
    )

    meta[...] = jnp.full(meta.shape, -1, jnp.int32)
    meta[0, 0:CAP, 0:6] = nbr_v[...]
    meta[0, CAP:CAP + 1, 0:CAP] = src_v[...]

    barrier = pltpu.get_barrier_semaphore()
    expected = nx - 1 + 6
    for step in AROUND:
        there = inside(step)
        expected = expected + there.astype(jnp.int32)

        @pl.when(there)
        def _():
            pl.semaphore_signal(barrier, inc=1, device_id=at(step), device_id_type=MESH)
    for group in ring:
        for target in group:
            pl.semaphore_signal(barrier, inc=1, device_id=target, device_id_type=MESH)
    load.wait()

    def spread_out(k, carry):
        s, x = k // B, k % B
        planes = raw[s, :, pl.ds(pl.multiple_of(x * 1024, 1024), 1024)].reshape(CAP, 8, 128)
        for q in range(CAP):
            dense[q, s, pl.ds(pl.multiple_of(x * 8, 8), 8), :] = planes[q]
        return carry

    lax.fori_loop(0, SPECIES * B, spread_out, 0)

    pl.semaphore_wait(barrier, expected)

    def opposite(i):
        return AROUND.index((-AROUND[i][0], -AROUND[i][1]))

    def meta_send(i):
        return pltpu.make_async_remote_copy(
            src_ref=meta.at[0], dst_ref=meta.at[1 + opposite(i)],
            send_sem=meta_ss.at[i], recv_sem=meta_rs.at[opposite(i)], device_id=at(AROUND[i]), device_id_type=MESH)

    for i, step in enumerate(AROUND):
        @pl.when(inside(step))
        def _():
            meta_send(i).start()

    lane8 = iota((8, 128), 1)

    def faces(k, carry):
        q, s = k // SPECIES, k % SPECIES
        own_faces[q * 6 + 0, s] = dense[q, s, 0:8, :]
        own_faces[q * 6 + 1, s] = dense[q, s, ROWS - 8:ROWS, :]
        low = jnp.zeros((8, 128), jnp.float32)
        high = jnp.zeros((8, 128), jnp.float32)
        for b in range(4):
            first = dense[q, s, pl.ds(64 * b, 8, stride=8), :]
            final = dense[q, s, pl.ds(64 * b + 7, 8, stride=8), :]
            here = lane8 // 32 == b
            low = jnp.where(here, pltpu.roll(first, 32 * b, 1) if b else first, low)
            high = jnp.where(here, pltpu.roll(final, 32 * (b + 1), 1) if b < 3 else final, high)
        own_faces[q * 6 + 2, s] = low
        own_faces[q * 6 + 3, s] = high
        low = jnp.zeros((8, 128), jnp.float32)
        high = jnp.zeros((8, 128), jnp.float32)
        for x in range(B):
            turned = pltpu.roll(dense[q, s, 8 * x:8 * x + 8, :], x + 1, 1)
            high = jnp.where(lane8 % 32 == x, turned, high)
            low = jnp.where(lane8 % 32 == (x + 1) % 32, turned, low)
        own_faces[q * 6 + 4, s] = pltpu.roll(low, 127, 1)
        own_faces[q * 6 + 5, s] = pltpu.roll(high, 96, 1)
        return carry

    lax.fori_loop(0, CAP * SPECIES, faces, 0)

    for i, step in enumerate(AROUND):
        @pl.when(inside(step))
        def _():
            meta_send(i).wait_send()
            pltpu.make_async_remote_copy(
                src_ref=meta.at[0], dst_ref=meta.at[1 + i], send_sem=meta_ss.at[i], recv_sem=meta_rs.at[i],
                device_id=at(step), device_id_type=MESH).wait_recv()

    def device(step):
        return me + step[0] * ny + step[1]

    def sources(step):
        return meta[PLACE[step], CAP:CAP + 1, :]

    taken = []
    for d, step in enumerate(NEAR):
        rel = sources(step) - me * CAP
        slot = jnp.max(jnp.where((rel >= 0) & (rel < CAP), rel, -1))
        taken.append(slot)
    safe = [jnp.maximum(slot, 0) for slot in taken]

    def patch_send(d, s):
        return pltpu.make_async_remote_copy(
            src_ref=sendp.at[d, s], dst_ref=landp.at[d ^ 1, s], send_sem=p_ss.at[d, s], recv_sem=p_rs.at[d ^ 1, s],
            device_id=at(NEAR[d]), device_id_type=MESH)

    def patch_wait(d, s):
        return pltpu.make_async_remote_copy(
            src_ref=sendp.at[d, s], dst_ref=landp.at[d, s], send_sem=p_ss.at[d, s], recv_sem=p_rs.at[d, s],
            device_id=at(NEAR[d]), device_id_type=MESH)

    def patches(some):
        for d in ORDER:
            @pl.when(inside(NEAR[d]))
            def _():
                for s in some:
                    def stage(r, carry):
                        part = pl.ds(pl.multiple_of(r * 64, 64), 64)
                        sendp[d, s, part, :] = dense[safe[d], s, part, :]
                        return carry
                    lax.fori_loop(0, 4, stage, 0)
                    patch_send(d, s).start()

    patches((0,))

    def face_send(d):
        return pltpu.make_async_remote_copy(
            src_ref=sendf.at[d], dst_ref=landf.at[d ^ 1], send_sem=f_ss.at[d], recv_sem=f_rs.at[d ^ 1],
            device_id=at(NEAR[d]), device_id_type=MESH)

    def face_wait(d):
        return pltpu.make_async_remote_copy(
            src_ref=sendf.at[d], dst_ref=landf.at[d], send_sem=f_ss.at[d], recv_sem=f_rs.at[d],
            device_id=at(NEAR[d]), device_id_type=MESH)

    def ghost_send(d):
        return pltpu.make_async_remote_copy(
            src_ref=sendg.at[d], dst_ref=landg.at[d ^ 1], send_sem=g_ss.at[d], recv_sem=g_rs.at[d ^ 1],
            device_id=at(NEAR[d]), device_id_type=MESH)

    def ghost_wait(d):
        return pltpu.make_async_remote_copy(
            src_ref=sendg.at[d], dst_ref=landg.at[d], send_sem=g_ss.at[d], recv_sem=g_rs.at[d],
            device_id=at(NEAR[d]), device_id_type=MESH)

    side = iota((8, 128), 1)
    far_side = side + 1 - 2 * (side % 2)
    slot_row = iota((8, 128), 0)
    lane1 = iota((1, 128), 1)

    def named(step):
        owner = device(step)
        hit = jnp.zeros((8, 128), jnp.bool_)
        for extra in ((0, 0),) + NEAR:
            hit = hit | (sources((step[0] + extra[0], step[1] + extra[1])) == owner * CAP + slot_row)
        return jnp.max(hit.astype(jnp.int32), axis=1, keepdims=True) > 0

    def wanted(step, of, names):
        rel = meta[PLACE[step]] - device(of) * CAP
        good = names & (rel >= 0) & (rel < CAP) & (slot_row < CAP) & (side < 6)
        code = jnp.where(good, rel * 6 + far_side, 127)
        hit = jnp.zeros((8, 128), jnp.bool_)
        for f in range(6):
            hit = hit | (code[:, f:f + 1] == side)
        mask = jnp.max(hit.astype(jnp.int32), axis=0, keepdims=True)
        mask = jnp.where(lane1 < 36, mask, 0)
        total = mask
        for k in (1, 2, 4, 8, 16, 32):
            total = total + jnp.where(lane1 >= k, pltpu.roll(total, k, 1), 0)
        return mask, total - mask

    mine = named((0, 0))
    over = jnp.zeros((8, 128), jnp.int32)
    for d, step in enumerate(NEAR):
        mask, rank = wanted(step, (0, 0), named(step))
        over = jnp.maximum(over, jnp.where((mask > 0) & (rank >= ROOM), 1, 0))
        chosen = jnp.where((mask > 0) & (rank == slot_row), side, 0)
        table[d] = jnp.broadcast_to(jnp.max(chosen, axis=1, keepdims=True), (8, 128))
        _, rank = wanted((0, 0), step, mine)
        table[4, d:d + 1, :] = rank
    over = jnp.broadcast_to(jnp.max(jnp.max(over, axis=1, keepdims=True), axis=0, keepdims=True), (8, 128))
    flags[0] = over
    to_scalars = pltpu.make_async_copy(table, table_s, tab_sem)
    to_scalars.start()

    to_scalars.wait()
    for d in ORDER:
        @pl.when(inside(NEAR[d]))
        def _():
            def stage(p, carry):
                sendf[d, p] = own_faces[table_s[d, p, 0]]
                return carry
            lax.fori_loop(0, ROOM, stage, 0)
            face_send(d).start()

    def flag_copy(base, k, target, held):
        return pltpu.make_async_remote_copy(
            src_ref=flags.at[held], dst_ref=flags.at[base + k], send_sem=fl_ss.at[base + k],
            recv_sem=fl_rs.at[base + k], device_id=target, device_id_type=MESH)

    bases = (3, 3 + nx - 1, 3 + nx - 1 + 3)
    for k, target in enumerate(ring[0]):
        flag_copy(bases[0], k, target, 0).start()
    patches((1, 2, 3, 4))

    for d, step in enumerate(NEAR):
        @pl.when(inside(step))
        def _():
            face_wait(d).wait_recv()

    def ghost_place(slot, f):
        nb = nbr_s[slot, f]
        rel = nb - me * CAP
        here = (rel >= 0) & (rel < CAP)
        opposite_f = f + 1 - 2 * (f % 2)
        own = jnp.where(here, rel * 6 + opposite_f, slot * 6 + f)
        own = jnp.where((nb < 0) | here, own, 0)
        away = jnp.int32(-1)
        for d, step in enumerate(NEAR):
            rel = nb - device(step) * CAP
            there = (nb >= 0) & (rel >= 0) & (rel < CAP)
            code = jnp.where(there, rel * 6 + opposite_f, 0)
            away = jnp.where(there, d * ROOM + jnp.minimum(table_s[4, d, code], ROOM - 1), away)
        return own, away

    def ghost_value(slot, f):
        own, away = ghost_place(slot, f)
        other = jnp.maximum(away, 0)
        return jnp.where(away >= 0, landf[other // ROOM, other % ROOM], own_faces[own])

    for d, step in enumerate(NEAR):
        @pl.when(inside(step))
        def _():
            def stage(f, carry):
                sendg[d, f] = ghost_value(safe[d], f)
                return carry
            lax.fori_loop(0, 6, stage, 0)
            ghost_send(d).start()

    def flag_round(n, held, following):
        for k, target in enumerate(ring[n]):
            copy = flag_copy(bases[n], k, target, held)
            copy.wait()
        total = flags[held]
        for k in range(len(ring[n])):
            total = jnp.maximum(total, flags[bases[n] + k])
        if following is None:
            flag_out[...] = total
        else:
            flags[following] = total
            for k, target in enumerate(ring[n + 1]):
                flag_copy(bases[n + 1], k, target, following).start()

    flag_round(0, 0, 1)

    for t in range(KEEP):
        rel = src_s[0, t] - me * CAP
        slot = jnp.where((rel >= 0) & (rel < CAP), rel, 0)

        def layer(f, carry):
            ghost_out[t, f] = ghost_value(slot, f)
            return carry
        lax.fori_loop(0, 6, layer, 0)

    flag_round(1, 1, 2)
    flag_round(2, 2, None)

    for d, step in enumerate(NEAR):
        @pl.when(inside(step))
        def _():
            face_send(d).wait_send()
            ghost_send(d).wait_send()
            for s in range(SPECIES):
                patch_send(d, s).wait_send()
                patch_wait(d, s).wait_recv()
            ghost_wait(d).wait_recv()


def smooth_kernel(
    nx, ny,
    src_s, mobility, fermi_gain, rates, conc, landp, landg, ghost_own,
    out,
    cur, ghost, coef, base, ping, pong, blank, cur_sem, ghost_sem, out_sem, zero_sem,
):
    gx, gy = lax.axis_index("gx"), lax.axis_index("gy")
    me = gx * ny + gy
    whence = []
    for t in range(KEEP):
        source = src_s[0, t]
        rel = source - me * CAP
        own = (rel >= 0) & (rel < CAP)
        came = jnp.int32(0)
        for d, step in enumerate(NEAR):
            away = source - (me + step[0] * ny + step[1]) * CAP
            came = jnp.where((away >= 0) & (away < CAP), d, came)
        whence.append((source, own, jnp.where(own, rel, 0), came))

    def fetch_own(t):
        return (
            pltpu.make_async_copy(
                conc.at[:, pl.ds(whence[t][2], 1), :], cur.at[t].reshape(SPECIES, 1, B**3), cur_sem.at[t]),
            pltpu.make_async_copy(ghost_own.at[t], ghost.at[t], ghost_sem.at[t]),
        )

    def fetch_moved(t):
        return (
            pltpu.make_async_copy(landp.at[whence[t][3]], cur.at[t], cur_sem.at[t]),
            pltpu.make_async_copy(landg.at[whence[t][3]], ghost.at[t], ghost_sem.at[t]),
        )

    for t in range(KEEP):
        source, own, slot, came = whence[t]

        @pl.when((source >= 0) & own)
        def _():
            for copy in fetch_own(t):
                copy.start()

        @pl.when((source >= 0) & jnp.logical_not(own))
        def _():
            for copy in fetch_moved(t):
                copy.start()

    blank[...] = jnp.zeros(blank.shape, jnp.float32)
    zeros = [
        pltpu.make_async_copy(blank, out.at[pl.ds(s, 1), pl.ds(KEEP, CAP - KEEP), :], zero_sem.at[s])
        for s in range(SPECIES)
    ]
    for copy in zeros:
        copy.start()
    lane = iota((8, 128), 1)
    sub = iota((8, 128), 0)
    z = lane % 32
    first_y = (sub == 0) & (lane < 32)
    last_y = (sub == 7) & (lane >= 96)

    def patch(t):
        for copy in fetch_moved(t):
            copy.wait()

        def prepare(xo, carry):
            for xi in range(8):
                x = xo * 8 + xi
                plane = pl.ds(pl.multiple_of(x * 8, 8), 8)
                a, i, v, p, q = [cur[t, s, plane, :] for s in range(SPECIES)]
                half = 0.5 * (a + p + q)
                electrons = half + jnp.sqrt(half * half + 1.0)
                ai = rates[0] * a * i - rates[1] * p
                av = rates[2] * a * v - rates[3] * q
                re = rates[4] * (i * v - 1.0)
                sources = (a - ai - av, i - ai - re, v - av - re, p + ai, q + av)
                for s in range(SPECIES):
                    gain = fermi_gain[s]
                    spread = mobility[s] * (1.0 + gain * electrons) / (1.0 + gain)
                    inverse = 1.0 / (1.0 + 6.0 * spread)
                    low = pltpu.roll(ghost[t, 4, s], (128 - x) % 128, 1)
                    high = pltpu.roll(ghost[t, 5, s], (31 - x + 128) % 128, 1)
                    extra = jnp.where(z == 0, low, 0.0) + jnp.where(z == 31, high, 0.0)
                    low = jnp.broadcast_to(ghost[t, 2, s, xi:xi + 1, :], (8, 128))
                    low = pltpu.roll(low, (128 - 32 * xo) % 128, 1)
                    high = jnp.broadcast_to(ghost[t, 3, s, xi:xi + 1, :], (8, 128))
                    high = pltpu.roll(high, (96 - 32 * xo) % 128, 1)
                    extra = extra + jnp.where(first_y, low, 0.0) + jnp.where(last_y, high, 0.0)
                    extra = extra + jnp.where(x == 0, ghost[t, 0, s], 0.0) + jnp.where(x == 31, ghost[t, 1, s], 0.0)
                    coef[s, plane, :] = spread * inverse
                    base[s, plane, :] = (sources[s] + spread * extra) * inverse
            return carry

        lax.fori_loop(0, 4, prepare, 0)

        def species(s, carry):
            def sweep(get, put):
                before = None
                here = get(0)
                for x in range(B):
                    after = get(x + 1) if x + 1 < B else None
                    total = jnp.where(z == 0, 0.0, pltpu.roll(here, 1, 1)) + jnp.where(z == 31, 0.0, pltpu.roll(here, 127, 1))
                    down = pltpu.roll(here, 32, 1)
                    down = jnp.where(lane >= 32, down, pltpu.roll(down, 1, 0))
                    up = pltpu.roll(here, 96, 1)
                    up = jnp.where(lane < 96, up, pltpu.roll(up, 7, 0))
                    total = total + jnp.where(first_y, 0.0, down) + jnp.where(last_y, 0.0, up)
                    if before is not None:
                        total = total + before
                    if after is not None:
                        total = total + after
                    put(x, base[s, 8 * x:8 * x + 8, :] + coef[s, 8 * x:8 * x + 8, :] * total)
                    before, here = here, after

            def put_ping(x, value):
                ping[8 * x:8 * x + 8, :] = value

            def put_last(x, value):
                pong[t, s, 8 * x:8 * x + 8, :] = value

            def put_pong(x, value):
                pong[t, s, 8 * x:8 * x + 8, :] = value

            sweep(lambda x: cur[t, s, 8 * x:8 * x + 8, :], put_pong)
            sweep(lambda x: pong[t, s, 8 * x:8 * x + 8, :], put_ping)
            sweep(lambda x: ping[8 * x:8 * x + 8, :], put_last)
            pltpu.make_async_copy(
                pong.at[t, pl.ds(s, 1)].reshape(1, 1, B**3), out.at[pl.ds(s, 1), pl.ds(t, 1), :], out_sem.at[t, s]
            ).start()
            return carry

        lax.fori_loop(0, SPECIES, species, 0)

    def put_out(t, s):
        return pltpu.make_async_copy(
            pong.at[t, pl.ds(s, 1)].reshape(1, 1, B**3), out.at[pl.ds(s, 1), pl.ds(t, 1), :], out_sem.at[t, s])

    for t in range(KEEP):
        @pl.when(src_s[0, t] >= 0)
        def _():
            patch(t)

        @pl.when(src_s[0, t] < 0)
        def _():
            pong[t] = jnp.zeros((SPECIES, ROWS, 128), jnp.float32)
            for s in range(SPECIES):
                put_out(t, s).start()
    for copy in zeros:
        copy.wait()
    for t in range(KEEP):
        for s in range(SPECIES):
            put_out(t, s).wait()


def in_vmem():
    return pl.BlockSpec(memory_space=pltpu.VMEM)


def in_smem():
    return pl.BlockSpec(memory_space=pltpu.SMEM)


def anywhere():
    return pl.BlockSpec(memory_space=pl.ANY)


def exchange(nx, ny, conc, neighbours, source):
    f32, i32 = jnp.float32, jnp.int32
    dma = pltpu.SemaphoreType.DMA
    n_flags = 3 + nx - 1 + 6
    return pl.pallas_call(
        functools.partial(exchange_kernel, nx, ny),
        out_shape=(
            jax.ShapeDtypeStruct((4, SPECIES, ROWS, 128), f32),
            jax.ShapeDtypeStruct((4, 6, SPECIES, 8, 128), f32),
            jax.ShapeDtypeStruct((KEEP, 6, SPECIES, 8, 128), f32),
            jax.ShapeDtypeStruct((8, 128), i32),
        ),
        in_specs=[anywhere(), in_smem(), in_smem(), in_vmem(), in_vmem()],
        out_specs=(anywhere(), anywhere(), in_vmem(), in_vmem()),
        scratch_shapes=[
            pltpu.VMEM((SPECIES, CAP, B**3), f32),
            pltpu.VMEM((CAP, SPECIES, ROWS, 128), f32),
            pltpu.VMEM((CAP * 6, SPECIES, 8, 128), f32),
            pltpu.VMEM((13, 8, 128), i32),
            pltpu.VMEM((5, 8, 128), i32),
            pltpu.SMEM((5, 8, 128), i32),
            pltpu.VMEM((4, SPECIES, ROWS, 128), f32),
            pltpu.VMEM((4, ROOM, SPECIES, 8, 128), f32),
            pltpu.VMEM((4, ROOM, SPECIES, 8, 128), f32),
            pltpu.VMEM((4, 6, SPECIES, 8, 128), f32),
            pltpu.VMEM((n_flags, 8, 128), i32),
            dma,
            dma((12,)), dma((12,)),
            dma,
            dma((4, SPECIES)), dma((4, SPECIES)), dma((4,)), dma((4,)), dma((4,)), dma((4,)),
            dma((n_flags,)), dma((n_flags,)),
        ],
        compiler_params=pltpu.CompilerParams(collective_id=0, has_side_effects=True, vmem_limit_bytes=40 * 2**20),
    )(conc, neighbours, source, neighbours, source)


def smooth(nx, ny, conc, landp, landg, ghost_own, source, mobility, fermi_gain, rates):
    f32 = jnp.float32
    dma = pltpu.SemaphoreType.DMA
    return pl.pallas_call(
        functools.partial(smooth_kernel, nx, ny),
        out_shape=jax.ShapeDtypeStruct((SPECIES, CAP, B**3), f32),
        in_specs=[in_smem()] * 4 + [anywhere()] * 4,
        out_specs=anywhere(),
        scratch_shapes=[
            pltpu.VMEM((KEEP, SPECIES, ROWS, 128), f32),
            pltpu.VMEM((KEEP, 6, SPECIES, 8, 128), f32),
            pltpu.VMEM((SPECIES, ROWS, 128), f32),
            pltpu.VMEM((SPECIES, ROWS, 128), f32),
            pltpu.VMEM((ROWS, 128), f32),
            pltpu.VMEM((KEEP, SPECIES, ROWS, 128), f32),
            pltpu.VMEM((1, CAP - KEEP, B**3), f32),
            dma((KEEP,)),
            dma((KEEP,)),
            dma((KEEP, SPECIES)),
            dma((SPECIES,)),
        ],
        compiler_params=pltpu.CompilerParams(vmem_limit_bytes=60 * 2**20),
    )(source, mobility, fermi_gain, rates, conc, landp, landg, ghost_own)


OPPOSITE = (1, 0, 3, 2, 5, 4)


def passed_along(x, axis, by):
    devices = lax.axis_size(axis)
    pairs = [(i, i + by) for i in range(devices) if 0 <= i + by < devices]
    return lax.ppermute(x, axis, pairs)


def with_halo(x, sides, width):
    edges = {}
    for axis, dim in sides:
        devices, length = (lax.axis_size(axis), x.shape[dim])
        up = [(i, (i + 1) % devices) for i in range(devices - 1)]
        last = lax.slice_in_dim(x, length - width, length, axis=dim)
        leading = lax.slice_in_dim(x, 0, width, axis=dim)
        edges[dim] = (
            lax.ppermute(last, axis, up),
            lax.ppermute(leading, axis, [(b, a) for a, b in up]),
        )
    done = []
    for _, dim in sides:
        low, high = edges[dim]
        around = [(width, width) if d in done else (0, 0) for d in range(x.ndim)]
        x = jnp.concatenate([jnp.pad(low, around), x, jnp.pad(high, around)], axis=dim)
        done.append(dim)
    return x


def faces_of(blocks):
    last = blocks.shape[-1] - 1
    return jnp.stack(
        [
            blocks[..., 0, :, :],
            blocks[..., last, :, :],
            blocks[..., :, 0, :],
            blocks[..., :, last, :],
            blocks[..., :, :, 0],
            blocks[..., :, :, last],
        ],
        axis=-4,
    )


def neighbour_sum(iterate, ghosts):
    lower_x = jnp.concatenate([ghosts[0][:, None], iterate[:, :-1]], axis=1)
    upper_x = jnp.concatenate([iterate[:, 1:], ghosts[1][:, None]], axis=1)
    lower_y = jnp.concatenate([ghosts[2][:, :, None], iterate[:, :, :-1]], axis=2)
    upper_y = jnp.concatenate([iterate[:, :, 1:], ghosts[3][:, :, None]], axis=2)
    lower_z = jnp.concatenate([ghosts[4][..., None], iterate[..., :-1]], axis=3)
    upper_z = jnp.concatenate([iterate[..., 1:], ghosts[5][..., None]], axis=3)
    return lower_x + upper_x + lower_y + upper_y + lower_z + upper_z


def smooth_plain(current, ghosts, mobility, fermi_gain, rates):
    dopant_sum = current[0] + current[3] + current[4]
    half_total = 0.5 * dopant_sum
    electrons = half_total + jnp.sqrt(half_total * half_total + 1.0)
    gain_column = fermi_gain[:, None, None, None]
    spread = (
        mobility[:, None, None, None] * (1.0 + gain_column * electrons[None]) / (1.0 + gain_column)
    )
    dopant, interstitial, vacancy, pair_inter, pair_vacancy = (
        current[0],
        current[1],
        current[2],
        current[3],
        current[4],
    )
    forming_ai = rates[0] * dopant * interstitial - rates[1] * pair_inter
    forming_av = rates[2] * dopant * vacancy - rates[3] * pair_vacancy
    recombine = rates[4] * (interstitial * vacancy - 1.0)
    source = jnp.stack(
        [
            dopant - forming_ai - forming_av,
            interstitial - forming_ai - recombine,
            vacancy - forming_av - recombine,
            pair_inter + forming_ai,
            pair_vacancy + forming_av,
        ],
        axis=0,
    )
    diagonal = 1.0 + 6.0 * spread
    iterate = current
    for repeat in range(SWEEPS):
        iterate = (source + spread * neighbour_sum(iterate, ghosts)) / diagonal
    return iterate


def smooth_all(current, ghosts, mobility, fermi_gain, rates):

    def per_patch(paired):
        return smooth_plain(paired[0], paired[1], mobility, fermi_gain, rates)

    return lax.map(per_patch, (current, ghosts))


def gather_ghosts(face_table, neighbours, column_index, row_index, rows_count, capacity):
    face_rows = face_table.reshape(9 * capacity * 6, SPECIES, B, B)
    safe_slot = jnp.maximum(neighbours, 0)
    source_device = safe_slot // capacity
    step_x = source_device // rows_count - column_index + 1
    step_y = source_device % rows_count - row_index + 1
    opposite = jnp.array(OPPOSITE, jnp.int32)
    face_ids = jnp.arange(6, dtype=jnp.int32)
    remote = ((step_x * 3 + step_y) * capacity + safe_slot % capacity) * 6 + opposite[None, :]
    local = (4 * capacity + jnp.arange(capacity, dtype=jnp.int32)[:, None]) * 6 + face_ids[None, :]
    picked = jnp.clip(jnp.where(neighbours >= 0, remote, local), 0, 9 * capacity * 6 - 1)
    one = functools.partial(lax.dynamic_index_in_dim, face_rows, axis=0, keepdims=False)
    ghosts = lax.map(one, picked.reshape(-1))
    return ghosts.reshape(picked.shape + face_rows.shape[1:])


def counted(hits):
    places = jnp.arange(hits.shape[0])
    before = places[None, :] <= places[:, None]
    return jnp.sum(jnp.where(before & hits[None, :], 1, 0), axis=1) - 1


def pick_rows(pulls, this_device, capacity, payload):
    wanted = (pulls >= 0) & (pulls // capacity == this_device)
    position = counted(wanted)
    chosen = wanted[None, :] & (position[None, :] == jnp.arange(MOVE, dtype=jnp.int32)[:, None])
    slot_list = jnp.sum(jnp.where(chosen, pulls % capacity, 0), axis=1)
    return payload[slot_list]


def place_rows(index, source_device, sender, start):
    from_sender = (source_device == sender) & (source_device >= 0)
    position = counted(from_sender)
    return jnp.where(from_sender, start + position, index)


def relocate(payload, source_slot, requests, this_device, rows_count, capacity):
    source_device = jnp.where(source_slot >= 0, source_slot // capacity, -1)
    index = jnp.where(
        (source_slot >= 0) & (source_device == this_device), source_slot % capacity, -1
    )
    pieces = [payload]
    start = capacity
    for offset in (1, -1):
        outgoing = pick_rows(requests[1 + offset, 1], this_device, capacity, payload)
        arrived = passed_along(outgoing, "gx", offset)
        index = place_rows(index, source_device, this_device - offset * rows_count, start)
        pieces.append(arrived)
        start = start + MOVE
    for offset in (1, -1):
        outgoing = pick_rows(requests[1, 1 + offset], this_device, capacity, payload)
        arrived = passed_along(outgoing, "gy", offset)
        index = place_rows(index, source_device, this_device - offset, start)
        pieces.append(arrived)
        start = start + MOVE
    candidates = jnp.concatenate(pieces, axis=0)
    gathered = candidates[jnp.maximum(index, 0)]
    return jnp.where((index >= 0)[:, None], gathered, jnp.zeros_like(gathered))


def general(concentration, neighbours, source_slot, mobility, fermi_gain, rates):
    capacity = concentration.shape[0]
    cells = concentration.shape[2]
    column_index = lax.axis_index("gx")
    row_index = lax.axis_index("gy")
    rows_count = lax.axis_size("gy")
    this_device = column_index * rows_count + row_index
    blocks = concentration.reshape(capacity, SPECIES, B, B, B)
    own_faces = faces_of(blocks).reshape(1, 1, capacity, 6, SPECIES, B * B)
    face_table = with_halo(own_faces, (("gx", 0), ("gy", 1)), 1)
    requests = with_halo(source_slot.reshape(1, 1, capacity), (("gx", 0), ("gy", 1)), 1)
    ghosts = gather_ghosts(face_table, neighbours, column_index, row_index, rows_count, capacity)
    working = KEEP - 1 + MOVE
    payload = jnp.concatenate(
        [
            concentration.reshape(capacity, SPECIES * cells),
            ghosts.reshape(capacity, 6 * SPECIES * B * B),
        ],
        axis=1,
    )
    arrived = relocate(payload, source_slot, requests, this_device, rows_count, capacity)[:working]
    current = arrived[:, : SPECIES * cells].reshape(working, SPECIES, B, B, B)
    layers = arrived[:, SPECIES * cells :].reshape(working, 6, SPECIES, B, B)
    swept = smooth_all(current, layers, mobility, fermi_gain, rates).reshape(
        working, SPECIES, cells
    )
    live_rows = (source_slot[:working] >= 0)[:, None, None]
    swept = jnp.where(live_rows, swept, jnp.zeros_like(swept))
    return jnp.concatenate(
        [swept, jnp.zeros((capacity - working, SPECIES, cells), jnp.float32)], axis=0
    )


def body(nx, ny, concentration, neighbours, source_slot, mobility, fermi_gain, rates):
    source = source_slot.reshape(1, CAP)
    conc = concentration.transpose(1, 0, 2)
    landp, landg, ghost, flag = exchange(nx, ny, conc, neighbours, source)

    def common():
        return smooth(nx, ny, conc, landp, landg, ghost, source, mobility, fermi_gain, rates).transpose(1, 0, 2)

    def crowded():
        return general(concentration, neighbours, source_slot, mobility, fermi_gain, rates)

    return lax.cond(flag[0, 0] == 0, common, crowded)


def solution(mesh):
    placed = (P(("gx", "gy"), None, None), P(("gx", "gy"), None), P(("gx", "gy")), P(), P(), P())
    return jax.shard_map(
        functools.partial(body, mesh.shape["gx"], mesh.shape["gy"]),
        mesh=mesh, in_specs=placed, out_specs=P(("gx", "gy"), None, None), check_vma=False,
    )
```

```python
import functools

import jax
import jax.numpy as jnp
from jax import lax
from jax.experimental import pallas as pl
from jax.experimental.pallas import tpu as pltpu
from jax.sharding import PartitionSpec as P

B = 32
SPECIES = 5
SWEEPS = 3
KEEP = 2
MOVE = 1
CAP = 6
ROWS = 256
EARLY = 12
ROOM = 6
MESH = pl.DeviceIdType.MESH

NEAR = ((-1, 0), (1, 0), (0, -1), (0, 1))
FAR = ((-2, 0), (2, 0), (0, -2), (0, 2), (-1, -1), (-1, 1), (1, -1), (1, 1))
AROUND = NEAR + FAR
ORDER = (2, 3, 0, 1)
PLACE = {(0, 0): 0, **{step: i + 1 for i, step in enumerate(AROUND)}}


def iota(shape, dim):
    return lax.broadcasted_iota(jnp.int32, shape, dim)


def step_patch(mobility, fermi_gain, rates, cell, layer, coef, base, ping, result, finish):
    lane = iota((8, 128), 1)
    sub = iota((8, 128), 0)
    z = lane % 32
    first_y = (sub == 0) & (lane < 32)
    last_y = (sub == 7) & (lane >= 96)
    whole = pl.ds(0, 8)
    scale = [mobility[s] / jnp.full((8, 128), 1.0 + fermi_gain[s]) for s in range(SPECIES)]

    def prepare(xo, carry):
        for xi in range(8):
            x = xo * 8 + xi
            plane = pl.ds(pl.multiple_of(x * 8, 8), 8)
            a, i, v, p, q = [cell(s, plane) for s in range(SPECIES)]
            half = 0.5 * (a + p + q)
            electrons = half + jnp.sqrt(half * half + 1.0)
            ai = rates[0] * a * i - rates[1] * p
            av = rates[2] * a * v - rates[3] * q
            re = rates[4] * (i * v - 1.0)
            sources = (a - ai - av, i - ai - re, v - av - re, p + ai, q + av)
            for s in range(SPECIES):
                spread = scale[s] * (1.0 + fermi_gain[s] * electrons)
                inverse = 1.0 / (1.0 + 6.0 * spread)
                low = pltpu.roll(layer(4, s, whole), (128 - x) % 128, 1)
                high = pltpu.roll(layer(5, s, whole), (31 - x + 128) % 128, 1)
                extra = jnp.where(z == 0, low, jnp.where(z == 31, high, 0.0))
                low = jnp.broadcast_to(layer(2, s, pl.ds(xi, 1)), (8, 128))
                high = jnp.broadcast_to(layer(3, s, pl.ds(xi, 1)), (8, 128))
                low = pltpu.roll(low, (128 - 32 * xo) % 128, 1)
                high = pltpu.roll(high, (96 - 32 * xo) % 128, 1)
                extra = extra + jnp.where(first_y, low, jnp.where(last_y, high, 0.0))
                if xi == 0:
                    extra = extra + jnp.where(x == 0, layer(0, s, whole), 0.0)
                if xi == 7:
                    extra = extra + jnp.where(x == B - 1, layer(1, s, whole), 0.0)
                weight = spread * inverse
                coef[s, plane, :] = weight
                base[s, plane, :] = sources[s] * inverse + weight * extra
        return carry

    lax.fori_loop(0, 4, prepare, 0)

    def species(s, carry):
        def sweep(get, put):
            before = None
            here = get(0)
            for x in range(B):
                after = get(x + 1) if x + 1 < B else None
                total = jnp.where(z == 0, 0.0, pltpu.roll(here, 1, 1)) + jnp.where(z == 31, 0.0, pltpu.roll(here, 127, 1))
                down = pltpu.roll(here, 32, 1)
                down = jnp.where(lane >= 32, down, pltpu.roll(down, 1, 0))
                up = pltpu.roll(here, 96, 1)
                up = jnp.where(lane < 96, up, pltpu.roll(up, 7, 0))
                total = total + jnp.where(first_y, 0.0, down) + jnp.where(last_y, 0.0, up)
                if before is not None:
                    total = total + before
                if after is not None:
                    total = total + after
                put(x, base[s, 8 * x:8 * x + 8, :] + coef[s, 8 * x:8 * x + 8, :] * total)
                before, here = here, after

        def put_ping(x, value):
            ping[8 * x:8 * x + 8, :] = value

        def put_result(x, value):
            result[s, 8 * x:8 * x + 8, :] = value

        sweep(lambda x: cell(s, pl.ds(8 * x, 8)), put_result)
        sweep(lambda x: result[s, 8 * x:8 * x + 8, :], put_ping)
        sweep(lambda x: ping[8 * x:8 * x + 8, :], put_result)
        finish(s)
        return carry

    lax.fori_loop(0, SPECIES, species, 0)


def exchange_kernel(
    nx, ny,
    conc, nbr_s, src_s, mobility, fermi_gain, rates, nbr_v, src_v,
    landp, landg, swept, flag_out,
    raw, dense, own_faces, meta, table, table_s, sendp, sendf, landf, sendg, flags, ghost, coef, base, ping, result,
    in_sem, meta_ss, meta_rs, tab_sem, p_ss, p_rs, f_ss, f_rs, g_ss, g_rs, fl_ss, fl_rs, out_sem,
):
    gx, gy = lax.axis_index("gx"), lax.axis_index("gy")
    me = gx * ny + gy

    def inside(step):
        x, y = gx + step[0], gy + step[1]
        return (x >= 0) & (x < nx) & (y >= 0) & (y < ny)

    def at(step):
        return (gx + step[0], gy + step[1])

    load = pltpu.make_async_copy(conc, raw, in_sem)
    load.start()

    row, col = gy // 4, gy % 4
    ring = (
        [(gx, row * 4 + (col + k) % 4) for k in range(1, 4)],
        [((gx + k) % nx, gy) for k in range(1, nx)],
        [(gx, ((row + k) % 4) * 4 + col) for k in range(1, 4)],
    )

    meta[...] = jnp.full(meta.shape, -1, jnp.int32)
    meta[0, 0:CAP, 0:6] = nbr_v[...]
    meta[0, CAP:CAP + 1, 0:CAP] = src_v[...]

    barrier = pltpu.get_barrier_semaphore()
    expected = nx - 1 + 6
    for step in AROUND:
        there = inside(step)
        expected = expected + there.astype(jnp.int32)

        @pl.when(there)
        def _():
            pl.semaphore_signal(barrier, inc=1, device_id=at(step), device_id_type=MESH)
    for group in ring:
        for target in group:
            pl.semaphore_signal(barrier, inc=1, device_id=target, device_id_type=MESH)
    load.wait()

    def spread_out(k, carry):
        s, x = k // B, k % B
        planes = raw[s, :, pl.ds(pl.multiple_of(x * 1024, 1024), 1024)].reshape(CAP, 8, 128)
        for q in range(CAP):
            dense[q, s, pl.ds(pl.multiple_of(x * 8, 8), 8), :] = planes[q]
        return carry

    lax.fori_loop(0, SPECIES * B, spread_out, 0)

    lane8 = iota((8, 128), 1)

    def faces(k, carry):
        q, s = k // SPECIES, k % SPECIES
        own_faces[q * 6 + 0, s] = dense[q, s, 0:8, :]
        own_faces[q * 6 + 1, s] = dense[q, s, ROWS - 8:ROWS, :]
        low = jnp.zeros((8, 128), jnp.float32)
        high = jnp.zeros((8, 128), jnp.float32)
        for b in range(4):
            first = dense[q, s, pl.ds(64 * b, 8, stride=8), :]
            final = dense[q, s, pl.ds(64 * b + 7, 8, stride=8), :]
            here = lane8 // 32 == b
            low = jnp.where(here, pltpu.roll(first, 32 * b, 1) if b else first, low)
            high = jnp.where(here, pltpu.roll(final, 32 * (b + 1), 1) if b < 3 else final, high)
        own_faces[q * 6 + 2, s] = low
        own_faces[q * 6 + 3, s] = high
        low = jnp.zeros((8, 128), jnp.float32)
        high = jnp.zeros((8, 128), jnp.float32)
        for x in range(B):
            turned = pltpu.roll(dense[q, s, 8 * x:8 * x + 8, :], x + 1, 1)
            high = jnp.where(lane8 % 32 == x, turned, high)
            low = jnp.where(lane8 % 32 == (x + 1) % 32, turned, low)
        own_faces[q * 6 + 4, s] = pltpu.roll(low, 127, 1)
        own_faces[q * 6 + 5, s] = pltpu.roll(high, 96, 1)
        return carry

    lax.fori_loop(0, EARLY, faces, 0)
    pl.semaphore_wait(barrier, expected)

    def opposite(i):
        return AROUND.index((-AROUND[i][0], -AROUND[i][1]))

    def meta_send(i):
        return pltpu.make_async_remote_copy(
            src_ref=meta.at[0], dst_ref=meta.at[1 + opposite(i)],
            send_sem=meta_ss.at[i], recv_sem=meta_rs.at[opposite(i)], device_id=at(AROUND[i]), device_id_type=MESH)

    for i, step in enumerate(AROUND):
        @pl.when(inside(step))
        def _():
            meta_send(i).start()

    lax.fori_loop(EARLY, CAP * SPECIES, faces, 0)

    for i, step in enumerate(AROUND):
        @pl.when(inside(step))
        def _():
            meta_send(i).wait_send()
            pltpu.make_async_remote_copy(
                src_ref=meta.at[0], dst_ref=meta.at[1 + i], send_sem=meta_ss.at[i], recv_sem=meta_rs.at[i],
                device_id=at(step), device_id_type=MESH).wait_recv()

    def device(step):
        return me + step[0] * ny + step[1]

    def sources(step):
        return meta[PLACE[step], CAP:CAP + 1, :]

    taken = []
    for d, step in enumerate(NEAR):
        rel = sources(step) - me * CAP
        slot = jnp.max(jnp.where((rel >= 0) & (rel < CAP), rel, -1))
        taken.append(slot)
    safe = [jnp.maximum(slot, 0) for slot in taken]

    def patch_send(d, s):
        return pltpu.make_async_remote_copy(
            src_ref=sendp.at[d, s], dst_ref=landp.at[d ^ 1, s], send_sem=p_ss.at[d, s], recv_sem=p_rs.at[d ^ 1, s],
            device_id=at(NEAR[d]), device_id_type=MESH)

    def patch_wait(d, s):
        return pltpu.make_async_remote_copy(
            src_ref=sendp.at[d, s], dst_ref=landp.at[d, s], send_sem=p_ss.at[d, s], recv_sem=p_rs.at[d, s],
            device_id=at(NEAR[d]), device_id_type=MESH)

    def patches(some):
        for d in ORDER:
            @pl.when(inside(NEAR[d]))
            def _():
                for s in some:
                    def stage(r, carry):
                        part = pl.ds(pl.multiple_of(r * 64, 64), 64)
                        sendp[d, s, part, :] = dense[safe[d], s, part, :]
                        return carry
                    lax.fori_loop(0, 4, stage, 0)
                    patch_send(d, s).start()

    patches((0,))

    def face_send(d):
        return pltpu.make_async_remote_copy(
            src_ref=sendf.at[d], dst_ref=landf.at[d ^ 1], send_sem=f_ss.at[d], recv_sem=f_rs.at[d ^ 1],
            device_id=at(NEAR[d]), device_id_type=MESH)

    def face_wait(d):
        return pltpu.make_async_remote_copy(
            src_ref=sendf.at[d], dst_ref=landf.at[d], send_sem=f_ss.at[d], recv_sem=f_rs.at[d],
            device_id=at(NEAR[d]), device_id_type=MESH)

    def ghost_send(d):
        return pltpu.make_async_remote_copy(
            src_ref=sendg.at[d], dst_ref=landg.at[d ^ 1], send_sem=g_ss.at[d], recv_sem=g_rs.at[d ^ 1],
            device_id=at(NEAR[d]), device_id_type=MESH)

    def ghost_wait(d):
        return pltpu.make_async_remote_copy(
            src_ref=sendg.at[d], dst_ref=landg.at[d], send_sem=g_ss.at[d], recv_sem=g_rs.at[d],
            device_id=at(NEAR[d]), device_id_type=MESH)

    side = iota((8, 128), 1)
    far_side = side + 1 - 2 * (side % 2)
    slot_row = iota((8, 128), 0)
    lane1 = iota((1, 128), 1)

    def named(step):
        owner = device(step)
        hit = jnp.zeros((8, 128), jnp.bool_)
        for extra in ((0, 0),) + NEAR:
            hit = hit | (sources((step[0] + extra[0], step[1] + extra[1])) == owner * CAP + slot_row)
        return jnp.max(hit.astype(jnp.int32), axis=1, keepdims=True) > 0

    def wanted(step, of, names):
        rel = meta[PLACE[step]] - device(of) * CAP
        good = names & (rel >= 0) & (rel < CAP) & (slot_row < CAP) & (side < 6)
        code = jnp.where(good, rel * 6 + far_side, 127)
        hit = jnp.zeros((8, 128), jnp.bool_)
        for f in range(6):
            hit = hit | (code[:, f:f + 1] == side)
        mask = jnp.max(hit.astype(jnp.int32), axis=0, keepdims=True)
        mask = jnp.where(lane1 < 36, mask, 0)
        total = mask
        for k in (1, 2, 4, 8, 16, 32):
            total = total + jnp.where(lane1 >= k, pltpu.roll(total, k, 1), 0)
        return mask, total - mask

    mine = named((0, 0))
    over = jnp.zeros((8, 128), jnp.int32)
    for d, step in enumerate(NEAR):
        mask, rank = wanted(step, (0, 0), named(step))
        over = jnp.maximum(over, jnp.where((mask > 0) & (rank >= ROOM), 1, 0))
        chosen = jnp.where((mask > 0) & (rank == slot_row), side, 0)
        table[d] = jnp.broadcast_to(jnp.max(chosen, axis=1, keepdims=True), (8, 128))
        _, rank = wanted((0, 0), step, mine)
        table[4, d:d + 1, :] = rank
    over = jnp.broadcast_to(jnp.max(jnp.max(over, axis=1, keepdims=True), axis=0, keepdims=True), (8, 128))
    flags[0] = over
    to_scalars = pltpu.make_async_copy(table, table_s, tab_sem)
    to_scalars.start()

    def flag_copy(base, k, target, held):
        return pltpu.make_async_remote_copy(
            src_ref=flags.at[held], dst_ref=flags.at[base + k], send_sem=fl_ss.at[base + k],
            recv_sem=fl_rs.at[base + k], device_id=target, device_id_type=MESH)

    bases = (3, 6, 6 + nx - 1)

    for k, target in enumerate(ring[0]):
        flag_copy(bases[0], k, target, 0).start()

    to_scalars.wait()
    for d in ORDER:
        @pl.when(inside(NEAR[d]))
        def _():
            def stage(p, carry):
                sendf[d, p] = own_faces[table_s[d, p, 0]]
                return carry
            lax.fori_loop(0, ROOM, stage, 0)
            face_send(d).start()

    patches((1, 2, 3, 4))

    def flag_round(n, held, following):
        for k, target in enumerate(ring[n]):
            copy = flag_copy(bases[n], k, target, held)
            copy.wait()
        total = flags[held]
        for k in range(len(ring[n])):
            total = jnp.maximum(total, flags[bases[n] + k])
        if following is None:
            flag_out[...] = total
        else:
            flags[following] = total
            for k, target in enumerate(ring[n + 1]):
                flag_copy(bases[n + 1], k, target, following).start()

    flag_round(0, 0, 1)

    for d, step in enumerate(NEAR):
        @pl.when(inside(step))
        def _():
            face_wait(d).wait_recv()

    def ghost_place(slot, f):
        nb = nbr_s[slot, f]
        rel = nb - me * CAP
        here = (rel >= 0) & (rel < CAP)
        opposite_f = f + 1 - 2 * (f % 2)
        own = jnp.where(here, rel * 6 + opposite_f, slot * 6 + f)
        own = jnp.where((nb < 0) | here, own, 0)
        away = jnp.int32(-1)
        for d, step in enumerate(NEAR):
            rel = nb - device(step) * CAP
            there = (nb >= 0) & (rel >= 0) & (rel < CAP)
            code = jnp.where(there, rel * 6 + opposite_f, 0)
            away = jnp.where(there, d * ROOM + jnp.minimum(table_s[4, d, code], ROOM - 1), away)
        return own, away

    def ghost_value(slot, f):
        own, away = ghost_place(slot, f)
        other = jnp.maximum(away, 0)
        return jnp.where(away >= 0, landf[other // ROOM, other % ROOM], own_faces[own])

    for d, step in enumerate(NEAR):
        @pl.when(inside(step))
        def _():
            def stage(f, carry):
                sendg[d, f] = ghost_value(safe[d], f)
                return carry
            lax.fori_loop(0, 6, stage, 0)
            ghost_send(d).start()

    flag_round(1, 1, 2)

    def stay(t, carry):
        rel = src_s[0, t] - me * CAP
        slot = jnp.where((rel >= 0) & (rel < CAP), rel, 0)

        def layer(f, carry):
            ghost[f] = ghost_value(slot, f)
            return carry
        lax.fori_loop(0, 6, layer, 0)
        step_patch(
            mobility, fermi_gain, rates,
            lambda s, rows: dense[slot, s, rows, :], lambda f, s, rows: ghost[f, s, rows, :],
            coef, base, ping, result.at[t], lambda s: None)
        pltpu.make_async_copy(result.at[t], swept.at[t], out_sem.at[t]).start()
        return carry

    lax.fori_loop(0, KEEP, stay, 0)

    flag_round(2, 2, None)

    for d, step in enumerate(NEAR):
        @pl.when(inside(step))
        def _():
            face_send(d).wait_send()
            ghost_send(d).wait_send()
            for s in range(SPECIES):
                patch_send(d, s).wait_send()
                patch_wait(d, s).wait_recv()
            ghost_wait(d).wait_recv()
    for t in range(KEEP):
        pltpu.make_async_copy(result.at[t], swept.at[t], out_sem.at[t]).wait()


def smooth_kernel(
    nx, ny,
    src_s, mobility, fermi_gain, rates, landp, landg, swept,
    out,
    cur, ghost, coef, base, ping, pong, blank, cur_sem, ghost_sem, out_sem, zero_sem,
):
    gx, gy = lax.axis_index("gx"), lax.axis_index("gy")
    me = gx * ny + gy
    whence = []
    for t in range(KEEP):
        source = src_s[0, t]
        rel = source - me * CAP
        own = (rel >= 0) & (rel < CAP)
        came = jnp.int32(0)
        for d, step in enumerate(NEAR):
            away = source - (me + step[0] * ny + step[1]) * CAP
            came = jnp.where((away >= 0) & (away < CAP), d, came)
        whence.append((source, own, jnp.where(own, rel, 0), came))

    def fetch_own(t):
        return (pltpu.make_async_copy(swept.at[t], pong.at[t], cur_sem.at[t]),)

    def fetch_moved(t):
        return (
            pltpu.make_async_copy(landp.at[whence[t][3]], cur.at[t], cur_sem.at[t]),
            pltpu.make_async_copy(landg.at[whence[t][3]], ghost.at[t], ghost_sem.at[t]),
        )

    for t in range(KEEP):
        source, own, slot, came = whence[t]

        @pl.when((source >= 0) & own)
        def _():
            for copy in fetch_own(t):
                copy.start()

        @pl.when((source >= 0) & jnp.logical_not(own))
        def _():
            for copy in fetch_moved(t):
                copy.start()

    blank[...] = jnp.zeros(blank.shape, jnp.float32)
    zeros = [
        pltpu.make_async_copy(blank, out.at[pl.ds(s, 1), pl.ds(KEEP, CAP - KEEP), :], zero_sem.at[s])
        for s in range(SPECIES)
    ]
    for copy in zeros:
        copy.start()
    def put_out(t, s):
        return pltpu.make_async_copy(
            pong.at[t, pl.ds(s, 1)].reshape(1, 1, B**3), out.at[pl.ds(s, 1), pl.ds(t, 1), :], out_sem.at[t, s])

    for t in range(KEEP):
        source, own, slot, came = whence[t]

        @pl.when(source < 0)
        def _():
            pong[t] = jnp.zeros((SPECIES, ROWS, 128), jnp.float32)
            for s in range(SPECIES):
                put_out(t, s).start()

        @pl.when((source >= 0) & own)
        def _():
            for copy in fetch_own(t):
                copy.wait()
            for s in range(SPECIES):
                put_out(t, s).start()

    for t in range(KEEP):
        source, own, slot, came = whence[t]

        @pl.when((source >= 0) & jnp.logical_not(own))
        def _():
            for copy in fetch_moved(t):
                copy.wait()
            step_patch(
                mobility, fermi_gain, rates,
                lambda s, rows: cur[t, s, rows, :], lambda f, s, rows: ghost[t, f, s, rows, :],
                coef, base, ping, pong.at[t], lambda s: put_out(t, s).start())

    for copy in zeros:
        copy.wait()
    for t in range(KEEP):
        for s in range(SPECIES):
            put_out(t, s).wait()


def in_vmem():
    return pl.BlockSpec(memory_space=pltpu.VMEM)


def in_smem():
    return pl.BlockSpec(memory_space=pltpu.SMEM)


def anywhere():
    return pl.BlockSpec(memory_space=pl.ANY)


def exchange(nx, ny, conc, neighbours, source, mobility, fermi_gain, rates):
    f32, i32 = jnp.float32, jnp.int32
    dma = pltpu.SemaphoreType.DMA
    n_flags = 3 + nx - 1 + 6
    return pl.pallas_call(
        functools.partial(exchange_kernel, nx, ny),
        out_shape=(
            jax.ShapeDtypeStruct((4, SPECIES, ROWS, 128), f32),
            jax.ShapeDtypeStruct((4, 6, SPECIES, 8, 128), f32),
            jax.ShapeDtypeStruct((KEEP, SPECIES, ROWS, 128), f32),
            jax.ShapeDtypeStruct((8, 128), i32),
        ),
        in_specs=[anywhere()] + [in_smem()] * 5 + [in_vmem()] * 2,
        out_specs=(anywhere(), anywhere(), anywhere(), in_vmem()),
        scratch_shapes=[
            pltpu.VMEM((SPECIES, CAP, B**3), f32),
            pltpu.VMEM((CAP, SPECIES, ROWS, 128), f32),
            pltpu.VMEM((CAP * 6, SPECIES, 8, 128), f32),
            pltpu.VMEM((13, 8, 128), i32),
            pltpu.VMEM((5, 8, 128), i32),
            pltpu.SMEM((5, 8, 128), i32),
            pltpu.VMEM((4, SPECIES, ROWS, 128), f32),
            pltpu.VMEM((4, ROOM, SPECIES, 8, 128), f32),
            pltpu.VMEM((4, ROOM, SPECIES, 8, 128), f32),
            pltpu.VMEM((4, 6, SPECIES, 8, 128), f32),
            pltpu.VMEM((n_flags, 8, 128), i32),
            pltpu.VMEM((6, SPECIES, 8, 128), f32),
            pltpu.VMEM((SPECIES, ROWS, 128), f32),
            pltpu.VMEM((SPECIES, ROWS, 128), f32),
            pltpu.VMEM((ROWS, 128), f32),
            pltpu.VMEM((KEEP, SPECIES, ROWS, 128), f32),
            dma,
            dma((12,)), dma((12,)),
            dma,
            dma((4, SPECIES)), dma((4, SPECIES)), dma((4,)), dma((4,)), dma((4,)), dma((4,)),
            dma((n_flags,)), dma((n_flags,)),
            dma((KEEP,)),
        ],
        compiler_params=pltpu.CompilerParams(collective_id=0, has_side_effects=True, vmem_limit_bytes=40 * 2**20),
    )(conc, neighbours, source, mobility, fermi_gain, rates, neighbours, source)


def smooth(nx, ny, landp, landg, swept, source, mobility, fermi_gain, rates):
    f32 = jnp.float32
    dma = pltpu.SemaphoreType.DMA
    return pl.pallas_call(
        functools.partial(smooth_kernel, nx, ny),
        out_shape=jax.ShapeDtypeStruct((SPECIES, CAP, B**3), f32),
        in_specs=[in_smem()] * 4 + [anywhere()] * 3,
        out_specs=anywhere(),
        scratch_shapes=[
            pltpu.VMEM((KEEP, SPECIES, ROWS, 128), f32),
            pltpu.VMEM((KEEP, 6, SPECIES, 8, 128), f32),
            pltpu.VMEM((SPECIES, ROWS, 128), f32),
            pltpu.VMEM((SPECIES, ROWS, 128), f32),
            pltpu.VMEM((ROWS, 128), f32),
            pltpu.VMEM((KEEP, SPECIES, ROWS, 128), f32),
            pltpu.VMEM((1, CAP - KEEP, B**3), f32),
            dma((KEEP,)),
            dma((KEEP,)),
            dma((KEEP, SPECIES)),
            dma((SPECIES,)),
        ],
        compiler_params=pltpu.CompilerParams(vmem_limit_bytes=60 * 2**20),
    )(source, mobility, fermi_gain, rates, landp, landg, swept)


OPPOSITE = (1, 0, 3, 2, 5, 4)


def passed_along(x, axis, by):
    devices = lax.axis_size(axis)
    pairs = [(i, i + by) for i in range(devices) if 0 <= i + by < devices]
    return lax.ppermute(x, axis, pairs)


def with_halo(x, sides, width):
    edges = {}
    for axis, dim in sides:
        devices, length = (lax.axis_size(axis), x.shape[dim])
        up = [(i, (i + 1) % devices) for i in range(devices - 1)]
        last = lax.slice_in_dim(x, length - width, length, axis=dim)
        leading = lax.slice_in_dim(x, 0, width, axis=dim)
        edges[dim] = (
            lax.ppermute(last, axis, up),
            lax.ppermute(leading, axis, [(b, a) for a, b in up]),
        )
    done = []
    for _, dim in sides:
        low, high = edges[dim]
        around = [(width, width) if d in done else (0, 0) for d in range(x.ndim)]
        x = jnp.concatenate([jnp.pad(low, around), x, jnp.pad(high, around)], axis=dim)
        done.append(dim)
    return x


def faces_of(blocks):
    last = blocks.shape[-1] - 1
    return jnp.stack(
        [
            blocks[..., 0, :, :],
            blocks[..., last, :, :],
            blocks[..., :, 0, :],
            blocks[..., :, last, :],
            blocks[..., :, :, 0],
            blocks[..., :, :, last],
        ],
        axis=-4,
    )


def neighbour_sum(iterate, ghosts):
    lower_x = jnp.concatenate([ghosts[0][:, None], iterate[:, :-1]], axis=1)
    upper_x = jnp.concatenate([iterate[:, 1:], ghosts[1][:, None]], axis=1)
    lower_y = jnp.concatenate([ghosts[2][:, :, None], iterate[:, :, :-1]], axis=2)
    upper_y = jnp.concatenate([iterate[:, :, 1:], ghosts[3][:, :, None]], axis=2)
    lower_z = jnp.concatenate([ghosts[4][..., None], iterate[..., :-1]], axis=3)
    upper_z = jnp.concatenate([iterate[..., 1:], ghosts[5][..., None]], axis=3)
    return lower_x + upper_x + lower_y + upper_y + lower_z + upper_z


def smooth_plain(current, ghosts, mobility, fermi_gain, rates):
    dopant_sum = current[0] + current[3] + current[4]
    half_total = 0.5 * dopant_sum
    electrons = half_total + jnp.sqrt(half_total * half_total + 1.0)
    gain_column = fermi_gain[:, None, None, None]
    spread = (
        mobility[:, None, None, None] * (1.0 + gain_column * electrons[None]) / (1.0 + gain_column)
    )
    dopant, interstitial, vacancy, pair_inter, pair_vacancy = (
        current[0],
        current[1],
        current[2],
        current[3],
        current[4],
    )
    forming_ai = rates[0] * dopant * interstitial - rates[1] * pair_inter
    forming_av = rates[2] * dopant * vacancy - rates[3] * pair_vacancy
    recombine = rates[4] * (interstitial * vacancy - 1.0)
    source = jnp.stack(
        [
            dopant - forming_ai - forming_av,
            interstitial - forming_ai - recombine,
            vacancy - forming_av - recombine,
            pair_inter + forming_ai,
            pair_vacancy + forming_av,
        ],
        axis=0,
    )
    diagonal = 1.0 + 6.0 * spread
    iterate = current
    for repeat in range(SWEEPS):
        iterate = (source + spread * neighbour_sum(iterate, ghosts)) / diagonal
    return iterate


def smooth_all(current, ghosts, mobility, fermi_gain, rates):

    def per_patch(paired):
        return smooth_plain(paired[0], paired[1], mobility, fermi_gain, rates)

    return lax.map(per_patch, (current, ghosts))


def gather_ghosts(face_table, neighbours, column_index, row_index, rows_count, capacity):
    face_rows = face_table.reshape(9 * capacity * 6, SPECIES, B, B)
    safe_slot = jnp.maximum(neighbours, 0)
    source_device = safe_slot // capacity
    step_x = source_device // rows_count - column_index + 1
    step_y = source_device % rows_count - row_index + 1
    opposite = jnp.array(OPPOSITE, jnp.int32)
    face_ids = jnp.arange(6, dtype=jnp.int32)
    remote = ((step_x * 3 + step_y) * capacity + safe_slot % capacity) * 6 + opposite[None, :]
    local = (4 * capacity + jnp.arange(capacity, dtype=jnp.int32)[:, None]) * 6 + face_ids[None, :]
    picked = jnp.clip(jnp.where(neighbours >= 0, remote, local), 0, 9 * capacity * 6 - 1)
    one = functools.partial(lax.dynamic_index_in_dim, face_rows, axis=0, keepdims=False)
    ghosts = lax.map(one, picked.reshape(-1))
    return ghosts.reshape(picked.shape + face_rows.shape[1:])


def counted(hits):
    places = jnp.arange(hits.shape[0])
    before = places[None, :] <= places[:, None]
    return jnp.sum(jnp.where(before & hits[None, :], 1, 0), axis=1) - 1


def pick_rows(pulls, this_device, capacity, payload):
    wanted = (pulls >= 0) & (pulls // capacity == this_device)
    position = counted(wanted)
    chosen = wanted[None, :] & (position[None, :] == jnp.arange(MOVE, dtype=jnp.int32)[:, None])
    slot_list = jnp.sum(jnp.where(chosen, pulls % capacity, 0), axis=1)
    return payload[slot_list]


def place_rows(index, source_device, sender, start):
    from_sender = (source_device == sender) & (source_device >= 0)
    position = counted(from_sender)
    return jnp.where(from_sender, start + position, index)


def relocate(payload, source_slot, requests, this_device, rows_count, capacity):
    source_device = jnp.where(source_slot >= 0, source_slot // capacity, -1)
    index = jnp.where(
        (source_slot >= 0) & (source_device == this_device), source_slot % capacity, -1
    )
    pieces = [payload]
    start = capacity
    for offset in (1, -1):
        outgoing = pick_rows(requests[1 + offset, 1], this_device, capacity, payload)
        arrived = passed_along(outgoing, "gx", offset)
        index = place_rows(index, source_device, this_device - offset * rows_count, start)
        pieces.append(arrived)
        start = start + MOVE
    for offset in (1, -1):
        outgoing = pick_rows(requests[1, 1 + offset], this_device, capacity, payload)
        arrived = passed_along(outgoing, "gy", offset)
        index = place_rows(index, source_device, this_device - offset, start)
        pieces.append(arrived)
        start = start + MOVE
    candidates = jnp.concatenate(pieces, axis=0)
    gathered = candidates[jnp.maximum(index, 0)]
    return jnp.where((index >= 0)[:, None], gathered, jnp.zeros_like(gathered))


def general(concentration, neighbours, source_slot, mobility, fermi_gain, rates):
    capacity = concentration.shape[0]
    cells = concentration.shape[2]
    column_index = lax.axis_index("gx")
    row_index = lax.axis_index("gy")
    rows_count = lax.axis_size("gy")
    this_device = column_index * rows_count + row_index
    blocks = concentration.reshape(capacity, SPECIES, B, B, B)
    own_faces = faces_of(blocks).reshape(1, 1, capacity, 6, SPECIES, B * B)
    face_table = with_halo(own_faces, (("gx", 0), ("gy", 1)), 1)
    requests = with_halo(source_slot.reshape(1, 1, capacity), (("gx", 0), ("gy", 1)), 1)
    ghosts = gather_ghosts(face_table, neighbours, column_index, row_index, rows_count, capacity)
    working = KEEP - 1 + MOVE
    payload = jnp.concatenate(
        [
            concentration.reshape(capacity, SPECIES * cells),
            ghosts.reshape(capacity, 6 * SPECIES * B * B),
        ],
        axis=1,
    )
    arrived = relocate(payload, source_slot, requests, this_device, rows_count, capacity)[:working]
    current = arrived[:, : SPECIES * cells].reshape(working, SPECIES, B, B, B)
    layers = arrived[:, SPECIES * cells :].reshape(working, 6, SPECIES, B, B)
    swept = smooth_all(current, layers, mobility, fermi_gain, rates).reshape(
        working, SPECIES, cells
    )
    live_rows = (source_slot[:working] >= 0)[:, None, None]
    swept = jnp.where(live_rows, swept, jnp.zeros_like(swept))
    return jnp.concatenate(
        [swept, jnp.zeros((capacity - working, SPECIES, cells), jnp.float32)], axis=0
    )


def body(nx, ny, concentration, neighbours, source_slot, mobility, fermi_gain, rates):
    source = source_slot.reshape(1, CAP)
    conc = concentration.transpose(1, 0, 2)
    landp, landg, swept, flag = exchange(nx, ny, conc, neighbours, source, mobility, fermi_gain, rates)

    def common():
        return smooth(nx, ny, landp, landg, swept, source, mobility, fermi_gain, rates).transpose(1, 0, 2)

    def crowded():
        return general(concentration, neighbours, source_slot, mobility, fermi_gain, rates)

    return lax.cond(flag[0, 0] == 0, common, crowded)


def solution(mesh):
    placed = (P(("gx", "gy"), None, None), P(("gx", "gy"), None), P(("gx", "gy")), P(), P(), P())
    return jax.shard_map(
        functools.partial(body, mesh.shape["gx"], mesh.shape["gy"]),
        mesh=mesh, in_specs=placed, out_specs=P(("gx", "gy"), None, None), check_vma=False,
    )
```

```python
import functools

import jax
import jax.numpy as jnp
from jax import lax
from jax.experimental import pallas as pl
from jax.experimental.pallas import tpu as pltpu
from jax.sharding import PartitionSpec as P

B = 32
SPECIES = 5
SWEEPS = 3
KEEP = 2
MOVE = 1
CAP = 6
ROWS = 256
EARLY = 12
ROOM = 6
MESH = pl.DeviceIdType.MESH

NEAR = ((-1, 0), (1, 0), (0, -1), (0, 1))
FAR = ((-2, 0), (2, 0), (0, -2), (0, 2), (-1, -1), (-1, 1), (1, -1), (1, 1))
AROUND = NEAR + FAR
ORDER = (2, 3, 0, 1)
HALF = ROWS // 2
PLACE = {(0, 0): 0, **{step: i + 1 for i, step in enumerate(AROUND)}}


def iota(shape, dim):
    return lax.broadcasted_iota(jnp.int32, shape, dim)


def step_patch(mobility, fermi_gain, rates, cell, layer, coef, base, ping, result, finish):
    lane = iota((8, 128), 1)
    sub = iota((8, 128), 0)
    z = lane % 32
    first_y = (sub == 0) & (lane < 32)
    last_y = (sub == 7) & (lane >= 96)
    whole = pl.ds(0, 8)
    scale = [mobility[s] / jnp.full((8, 128), 1.0 + fermi_gain[s]) for s in range(SPECIES)]

    def prepare(xo, carry):
        for xi in range(8):
            x = xo * 8 + xi
            plane = pl.ds(pl.multiple_of(x * 8, 8), 8)
            a, i, v, p, q = [cell(s, plane) for s in range(SPECIES)]
            half = 0.5 * (a + p + q)
            electrons = half + jnp.sqrt(half * half + 1.0)
            ai = rates[0] * a * i - rates[1] * p
            av = rates[2] * a * v - rates[3] * q
            re = rates[4] * (i * v - 1.0)
            sources = (a - ai - av, i - ai - re, v - av - re, p + ai, q + av)
            for s in range(SPECIES):
                spread = scale[s] * (1.0 + fermi_gain[s] * electrons)
                inverse = 1.0 / (1.0 + 6.0 * spread)
                low = pltpu.roll(layer(4, s, whole), (128 - x) % 128, 1)
                high = pltpu.roll(layer(5, s, whole), (31 - x + 128) % 128, 1)
                extra = jnp.where(z == 0, low, jnp.where(z == 31, high, 0.0))
                low = jnp.broadcast_to(layer(2, s, pl.ds(xi, 1)), (8, 128))
                high = jnp.broadcast_to(layer(3, s, pl.ds(xi, 1)), (8, 128))
                low = pltpu.roll(low, (128 - 32 * xo) % 128, 1)
                high = pltpu.roll(high, (96 - 32 * xo) % 128, 1)
                extra = extra + jnp.where(first_y, low, jnp.where(last_y, high, 0.0))
                if xi == 0:
                    extra = extra + jnp.where(x == 0, layer(0, s, whole), 0.0)
                if xi == 7:
                    extra = extra + jnp.where(x == B - 1, layer(1, s, whole), 0.0)
                weight = spread * inverse
                coef[s, plane, :] = weight
                base[s, plane, :] = sources[s] * inverse + weight * extra
        return carry

    lax.fori_loop(0, 4, prepare, 0)

    def species(s, carry):
        def sweep(get, put):
            before = None
            here = get(0)
            for x in range(B):
                after = get(x + 1) if x + 1 < B else None
                total = jnp.where(z == 0, 0.0, pltpu.roll(here, 1, 1)) + jnp.where(z == 31, 0.0, pltpu.roll(here, 127, 1))
                down = pltpu.roll(here, 32, 1)
                down = jnp.where(lane >= 32, down, pltpu.roll(down, 1, 0))
                up = pltpu.roll(here, 96, 1)
                up = jnp.where(lane < 96, up, pltpu.roll(up, 7, 0))
                total = total + jnp.where(first_y, 0.0, down) + jnp.where(last_y, 0.0, up)
                if before is not None:
                    total = total + before
                if after is not None:
                    total = total + after
                put(x, base[s, 8 * x:8 * x + 8, :] + coef[s, 8 * x:8 * x + 8, :] * total)
                before, here = here, after

        def put_ping(x, value):
            ping[8 * x:8 * x + 8, :] = value

        def put_result(x, value):
            result[s, 8 * x:8 * x + 8, :] = value

        sweep(lambda x: cell(s, pl.ds(8 * x, 8)), put_result)
        sweep(lambda x: result[s, 8 * x:8 * x + 8, :], put_ping)
        sweep(lambda x: ping[8 * x:8 * x + 8, :], put_result)
        finish(s)
        return carry

    lax.fori_loop(0, SPECIES, species, 0)


def exchange_kernel(
    nx, ny,
    conc, nbr_s, src_s, mobility, fermi_gain, rates, nbr_v, src_v,
    landp, landz, landq, landg, swept, flag_out,
    raw, dense, own_faces, meta, table, table_s, sendp, sendq, heldq, sendz, sendf, landf, sendg, flags, ghost, coef, base, ping, result,
    in_sem, meta_ss, meta_rs, tab_sem, p_ss, p_rs, q_ss, q_rs, z_ss, z_rs, h_ss, h_rs, f_ss, f_rs, g_ss, g_rs, fl_ss, fl_rs, out_sem,
):
    gx, gy = lax.axis_index("gx"), lax.axis_index("gy")
    me = gx * ny + gy

    def inside(step):
        x, y = gx + step[0], gy + step[1]
        return (x >= 0) & (x < nx) & (y >= 0) & (y < ny)

    def at(step):
        return (gx + step[0], gy + step[1])

    load = pltpu.make_async_copy(conc, raw, in_sem)
    load.start()

    row, col = gy // 4, gy % 4
    ring = (
        [(gx, row * 4 + (col + k) % 4) for k in range(1, 4)],
        [((gx + k) % nx, gy) for k in range(1, nx)],
        [(gx, ((row + k) % 4) * 4 + col) for k in range(1, 4)],
    )

    meta[...] = jnp.full(meta.shape, -1, jnp.int32)
    meta[0, 0:CAP, 0:6] = nbr_v[...]
    meta[0, CAP:CAP + 1, 0:CAP] = src_v[...]

    barrier = pltpu.get_barrier_semaphore()
    expected = nx - 1 + 6
    for step in AROUND:
        there = inside(step)
        expected = expected + there.astype(jnp.int32)

        @pl.when(there)
        def _():
            pl.semaphore_signal(barrier, inc=1, device_id=at(step), device_id_type=MESH)
    for group in ring:
        for target in group:
            pl.semaphore_signal(barrier, inc=1, device_id=target, device_id_type=MESH)
    load.wait()

    def spread_out(k, carry):
        s, x = k // B, k % B
        planes = raw[s, :, pl.ds(pl.multiple_of(x * 1024, 1024), 1024)].reshape(CAP, 8, 128)
        for q in range(CAP):
            dense[q, s, pl.ds(pl.multiple_of(x * 8, 8), 8), :] = planes[q]
        return carry

    lax.fori_loop(0, SPECIES * B, spread_out, 0)

    lane8 = iota((8, 128), 1)

    def faces(k, carry):
        q, s = k // SPECIES, k % SPECIES
        own_faces[q * 6 + 0, s] = dense[q, s, 0:8, :]
        own_faces[q * 6 + 1, s] = dense[q, s, ROWS - 8:ROWS, :]
        low = jnp.zeros((8, 128), jnp.float32)
        high = jnp.zeros((8, 128), jnp.float32)
        for b in range(4):
            first = dense[q, s, pl.ds(64 * b, 8, stride=8), :]
            final = dense[q, s, pl.ds(64 * b + 7, 8, stride=8), :]
            here = lane8 // 32 == b
            low = jnp.where(here, pltpu.roll(first, 32 * b, 1) if b else first, low)
            high = jnp.where(here, pltpu.roll(final, 32 * (b + 1), 1) if b < 3 else final, high)
        own_faces[q * 6 + 2, s] = low
        own_faces[q * 6 + 3, s] = high
        low = jnp.zeros((8, 128), jnp.float32)
        high = jnp.zeros((8, 128), jnp.float32)
        for x in range(B):
            turned = pltpu.roll(dense[q, s, 8 * x:8 * x + 8, :], x + 1, 1)
            high = jnp.where(lane8 % 32 == x, turned, high)
            low = jnp.where(lane8 % 32 == (x + 1) % 32, turned, low)
        own_faces[q * 6 + 4, s] = pltpu.roll(low, 127, 1)
        own_faces[q * 6 + 5, s] = pltpu.roll(high, 96, 1)
        return carry

    lax.fori_loop(0, EARLY, faces, 0)
    pl.semaphore_wait(barrier, expected)

    def opposite(i):
        return AROUND.index((-AROUND[i][0], -AROUND[i][1]))

    def meta_send(i):
        return pltpu.make_async_remote_copy(
            src_ref=meta.at[0], dst_ref=meta.at[1 + opposite(i)],
            send_sem=meta_ss.at[i], recv_sem=meta_rs.at[opposite(i)], device_id=at(AROUND[i]), device_id_type=MESH)

    for i, step in enumerate(AROUND):
        @pl.when(inside(step))
        def _():
            meta_send(i).start()

    lax.fori_loop(EARLY, CAP * SPECIES, faces, 0)

    for i, step in enumerate(AROUND):
        @pl.when(inside(step))
        def _():
            meta_send(i).wait_send()
            pltpu.make_async_remote_copy(
                src_ref=meta.at[0], dst_ref=meta.at[1 + i], send_sem=meta_ss.at[i], recv_sem=meta_rs.at[i],
                device_id=at(step), device_id_type=MESH).wait_recv()

    def device(step):
        return me + step[0] * ny + step[1]

    def sources(step):
        return meta[PLACE[step], CAP:CAP + 1, :]

    taken = []
    for d, step in enumerate(NEAR):
        rel = sources(step) - me * CAP
        slot = jnp.max(jnp.where((rel >= 0) & (rel < CAP), rel, -1))
        taken.append(slot)
    safe = [jnp.maximum(slot, 0) for slot in taken]
    asked = [slot >= 0 for slot in taken]

    def patch_send(d, s):
        return pltpu.make_async_remote_copy(
            src_ref=sendp.at[d, s], dst_ref=landp.at[d ^ 1, s], send_sem=p_ss.at[d, s], recv_sem=p_rs.at[d ^ 1, s],
            device_id=at(NEAR[d]), device_id_type=MESH)

    def patch_wait(d, s):
        return pltpu.make_async_remote_copy(
            src_ref=sendp.at[d, s], dst_ref=landp.at[d, s], send_sem=p_ss.at[d, s], recv_sem=p_rs.at[d, s],
            device_id=at(NEAR[d]), device_id_type=MESH)

    def stage(to, slot, s, first, rows):
        def part(r, carry):
            to[pl.ds(pl.multiple_of(r * 64, 64), 64), :] = dense[slot, s, pl.ds(pl.multiple_of(first + r * 64, 64), 64), :]
            return carry
        lax.fori_loop(0, rows // 64, part, 0)

    core = gx % 2
    twin = (gx + 1 - 2 * core, gy)
    mine_first, twin_first = core * HALF, (1 - core) * HALF

    def copy_along(src, dst, ss, rs, target):
        return pltpu.make_async_remote_copy(
            src_ref=src, dst_ref=dst, send_sem=ss, recv_sem=rs, device_id=target, device_id_type=MESH)

    def give(e, s):
        return copy_along(sendq.at[e, s], heldq.at[e, s], q_ss.at[e, s], q_rs.at[e, s], twin)

    def carry_send(e, s):
        return copy_along(sendz.at[e, s], landz.at[1 - e, s], z_ss.at[e, s], z_rs.at[1 - e, s], at(NEAR[2 + e]))

    def carry_wait(e, s):
        return copy_along(sendz.at[e, s], landz.at[e, s], z_ss.at[e, s], z_rs.at[e, s], at(NEAR[2 + e]))

    def hand(e, s):
        return copy_along(landz.at[e, s], landq.at[e, s], h_ss.at[e, s], h_rs.at[e, s], twin)

    for s in range(SPECIES):
        for e in range(2):
            @pl.when(inside(NEAR[2 + e]))
            def _():
                stage(sendq.at[e, s], safe[2 + e], s, twin_first, HALF)
                give(e, s).start()

    def straight():
        for d in range(2):
            @pl.when(inside(NEAR[d]))
            def _():
                for s in range(SPECIES):
                    stage(sendp.at[d, s], safe[d], s, 0, ROWS)
                    patch_send(d, s).start()


    def face_send(d):
        return pltpu.make_async_remote_copy(
            src_ref=sendf.at[d], dst_ref=landf.at[d ^ 1], send_sem=f_ss.at[d], recv_sem=f_rs.at[d ^ 1],
            device_id=at(NEAR[d]), device_id_type=MESH)

    def face_wait(d):
        return pltpu.make_async_remote_copy(
            src_ref=sendf.at[d], dst_ref=landf.at[d], send_sem=f_ss.at[d], recv_sem=f_rs.at[d],
            device_id=at(NEAR[d]), device_id_type=MESH)

    def ghost_send(d):
        return pltpu.make_async_remote_copy(
            src_ref=sendg.at[d], dst_ref=landg.at[d ^ 1], send_sem=g_ss.at[d], recv_sem=g_rs.at[d ^ 1],
            device_id=at(NEAR[d]), device_id_type=MESH)

    def ghost_wait(d):
        return pltpu.make_async_remote_copy(
            src_ref=sendg.at[d], dst_ref=landg.at[d], send_sem=g_ss.at[d], recv_sem=g_rs.at[d],
            device_id=at(NEAR[d]), device_id_type=MESH)

    side = iota((8, 128), 1)
    far_side = side + 1 - 2 * (side % 2)
    slot_row = iota((8, 128), 0)
    lane1 = iota((1, 128), 1)

    def named(step):
        owner = device(step)
        hit = jnp.zeros((8, 128), jnp.bool_)
        for extra in ((0, 0),) + NEAR:
            hit = hit | (sources((step[0] + extra[0], step[1] + extra[1])) == owner * CAP + slot_row)
        return jnp.max(hit.astype(jnp.int32), axis=1, keepdims=True) > 0

    def wanted(step, of, names):
        rel = meta[PLACE[step]] - device(of) * CAP
        good = names & (rel >= 0) & (rel < CAP) & (slot_row < CAP) & (side < 6)
        code = jnp.where(good, rel * 6 + far_side, 127)
        hit = jnp.zeros((8, 128), jnp.bool_)
        for f in range(6):
            hit = hit | (code[:, f:f + 1] == side)
        mask = jnp.max(hit.astype(jnp.int32), axis=0, keepdims=True)
        mask = jnp.where(lane1 < 36, mask, 0)
        total = mask
        for k in (1, 2, 4, 8, 16, 32):
            total = total + jnp.where(lane1 >= k, pltpu.roll(total, k, 1), 0)
        return mask, total - mask

    mine = named((0, 0))
    over = jnp.zeros((8, 128), jnp.int32)
    for d, step in enumerate(NEAR):
        mask, rank = wanted(step, (0, 0), named(step))
        over = jnp.maximum(over, jnp.where((mask > 0) & (rank >= ROOM), 1, 0))
        chosen = jnp.where((mask > 0) & (rank == slot_row), side, 0)
        table[d] = jnp.broadcast_to(jnp.max(chosen, axis=1, keepdims=True), (8, 128))
        _, rank = wanted((0, 0), step, mine)
        table[4, d:d + 1, :] = rank
    over = jnp.broadcast_to(jnp.max(jnp.max(over, axis=1, keepdims=True), axis=0, keepdims=True), (8, 128))
    twin_base = (me + (1 - 2 * core) * ny) * CAP
    for e, dy in enumerate((-1, 1)):
        rel = sources((0, dy)) - me * CAP
        other = jnp.where(core == 0, sources((1, dy)), sources((-1, dy))) - twin_base
        both = jnp.where((rel >= 0) & (rel < CAP), 1, 0) * jnp.max(
            jnp.where((other >= 0) & (other < CAP), 1, 0), axis=1, keepdims=True)
        over = jnp.maximum(over, jnp.max(both, axis=1, keepdims=True))
    flags[0] = over
    to_scalars = pltpu.make_async_copy(table, table_s, tab_sem)
    to_scalars.start()

    def flag_copy(base, k, target, held):
        return pltpu.make_async_remote_copy(
            src_ref=flags.at[held], dst_ref=flags.at[base + k], send_sem=fl_ss.at[base + k],
            recv_sem=fl_rs.at[base + k], device_id=target, device_id_type=MESH)

    bases = (3, 6, 6 + nx - 1)

    for k, target in enumerate(ring[0]):
        flag_copy(bases[0], k, target, 0).start()

    to_scalars.wait()
    for d in ORDER:
        @pl.when(inside(NEAR[d]))
        def _():
            def stage(p, carry):
                sendf[d, p] = own_faces[table_s[d, p, 0]]
                return carry
            lax.fori_loop(0, ROOM, stage, 0)
            face_send(d).start()

    straight()
    for s in range(SPECIES):
        for e in range(2):
            @pl.when(inside(NEAR[2 + e]))
            def _():
                give(e, s).wait_recv()
                for r in range(HALF // 64):
                    there = pl.ds(pl.multiple_of(mine_first + r * 64, 64), 64)
                    sendz[e, s, r * 64:r * 64 + 64, :] = jnp.where(
                        asked[2 + e], dense[safe[2 + e], s, there, :], heldq[e, s, r * 64:r * 64 + 64, :])
                carry_send(e, s).start()

    def flag_round(n, held, following):
        for k, target in enumerate(ring[n]):
            copy = flag_copy(bases[n], k, target, held)
            copy.wait()
        total = flags[held]
        for k in range(len(ring[n])):
            total = jnp.maximum(total, flags[bases[n] + k])
        if following is None:
            flag_out[...] = total
        else:
            flags[following] = total
            for k, target in enumerate(ring[n + 1]):
                flag_copy(bases[n + 1], k, target, following).start()

    flag_round(0, 0, 1)

    for d, step in enumerate(NEAR):
        @pl.when(inside(step))
        def _():
            face_wait(d).wait_recv()

    def ghost_place(slot, f):
        nb = nbr_s[slot, f]
        rel = nb - me * CAP
        here = (rel >= 0) & (rel < CAP)
        opposite_f = f + 1 - 2 * (f % 2)
        own = jnp.where(here, rel * 6 + opposite_f, slot * 6 + f)
        own = jnp.where((nb < 0) | here, own, 0)
        away = jnp.int32(-1)
        for d, step in enumerate(NEAR):
            rel = nb - device(step) * CAP
            there = (nb >= 0) & (rel >= 0) & (rel < CAP)
            code = jnp.where(there, rel * 6 + opposite_f, 0)
            away = jnp.where(there, d * ROOM + jnp.minimum(table_s[4, d, code], ROOM - 1), away)
        return own, away

    def ghost_value(slot, f):
        own, away = ghost_place(slot, f)
        other = jnp.maximum(away, 0)
        return jnp.where(away >= 0, landf[other // ROOM, other % ROOM], own_faces[own])

    for d, step in enumerate(NEAR):
        @pl.when(inside(step))
        def _():
            def stage(f, carry):
                sendg[d, f] = ghost_value(safe[d], f)
                return carry
            lax.fori_loop(0, 6, stage, 0)
            ghost_send(d).start()

    flag_round(1, 1, 2)

    def stay(t, carry):
        rel = src_s[0, t] - me * CAP
        slot = jnp.where((rel >= 0) & (rel < CAP), rel, 0)

        def layer(f, carry):
            ghost[f] = ghost_value(slot, f)
            return carry
        lax.fori_loop(0, 6, layer, 0)
        step_patch(
            mobility, fermi_gain, rates,
            lambda s, rows: dense[slot, s, rows, :], lambda f, s, rows: ghost[f, s, rows, :],
            coef, base, ping, result.at[t], lambda s: None)
        pltpu.make_async_copy(result.at[t], swept.at[t], out_sem.at[t]).start()
        return carry

    stay(0, 0)
    for s in range(SPECIES):
        for e in range(2):
            @pl.when(inside(NEAR[2 + e]))
            def _():
                carry_wait(e, s).wait_recv()
                hand(e, s).start()
    stay(1, 0)

    flag_round(2, 2, None)

    for d, step in enumerate(NEAR):
        @pl.when(inside(step))
        def _():
            face_send(d).wait_send()
            ghost_send(d).wait_send()
            for s in range(SPECIES):
                if d < 2:
                    patch_send(d, s).wait_send()
                    patch_wait(d, s).wait_recv()
                else:
                    give(d - 2, s).wait_send()
                    carry_send(d - 2, s).wait_send()
                    hand(d - 2, s).wait()
            ghost_wait(d).wait_recv()
    for t in range(KEEP):
        pltpu.make_async_copy(result.at[t], swept.at[t], out_sem.at[t]).wait()


def smooth_kernel(
    nx, ny,
    src_s, mobility, fermi_gain, rates, landp, landz, landq, landg, swept,
    out,
    cur, ghost, coef, base, ping, pong, blank, cur_sem, half_sem, ghost_sem, out_sem, zero_sem,
):
    gx, gy = lax.axis_index("gx"), lax.axis_index("gy")
    me = gx * ny + gy
    whence = []
    for t in range(KEEP):
        source = src_s[0, t]
        rel = source - me * CAP
        own = (rel >= 0) & (rel < CAP)
        came = jnp.int32(0)
        for d, step in enumerate(NEAR):
            away = source - (me + step[0] * ny + step[1]) * CAP
            came = jnp.where((away >= 0) & (away < CAP), d, came)
        whence.append((source, own, jnp.where(own, rel, 0), came))

    def fetch_own(t):
        return (pltpu.make_async_copy(swept.at[t], pong.at[t], cur_sem.at[t]),)

    core = gx % 2

    def fetch_moved(t):
        came = whence[t][3]
        e = jnp.maximum(came - 2, 0)
        straight = (
            pltpu.make_async_copy(landp.at[jnp.minimum(came, 1)], cur.at[t], cur_sem.at[t]),
        )
        halves = (
            pltpu.make_async_copy(landz.at[e], cur.at[t, :, pl.ds(pl.multiple_of(core * HALF, HALF), HALF), :], cur_sem.at[t]),
            pltpu.make_async_copy(landq.at[e], cur.at[t, :, pl.ds(pl.multiple_of((1 - core) * HALF, HALF), HALF), :], half_sem.at[t]),
        )
        layers = pltpu.make_async_copy(landg.at[came], ghost.at[t], ghost_sem.at[t])
        return straight, halves, layers

    def start_moved(t):
        straight, halves, layers = fetch_moved(t)
        layers.start()

        @pl.when(whence[t][3] < 2)
        def _():
            straight[0].start()

        @pl.when(whence[t][3] >= 2)
        def _():
            halves[0].start()
            halves[1].start()

    def wait_moved(t):
        straight, halves, layers = fetch_moved(t)
        layers.wait()

        @pl.when(whence[t][3] < 2)
        def _():
            straight[0].wait()

        @pl.when(whence[t][3] >= 2)
        def _():
            halves[0].wait()
            halves[1].wait()

    for t in range(KEEP):
        source, own, slot, came = whence[t]

        @pl.when((source >= 0) & own)
        def _():
            for copy in fetch_own(t):
                copy.start()

        @pl.when((source >= 0) & jnp.logical_not(own))
        def _():
            start_moved(t)

    blank[...] = jnp.zeros(blank.shape, jnp.float32)
    zeros = [
        pltpu.make_async_copy(blank, out.at[pl.ds(s, 1), pl.ds(KEEP, CAP - KEEP), :], zero_sem.at[s])
        for s in range(SPECIES)
    ]
    for copy in zeros:
        copy.start()
    def put_out(t, s):
        return pltpu.make_async_copy(
            pong.at[t, pl.ds(s, 1)].reshape(1, 1, B**3), out.at[pl.ds(s, 1), pl.ds(t, 1), :], out_sem.at[t, s])

    for t in range(KEEP):
        source, own, slot, came = whence[t]

        @pl.when(source < 0)
        def _():
            pong[t] = jnp.zeros((SPECIES, ROWS, 128), jnp.float32)
            for s in range(SPECIES):
                put_out(t, s).start()

        @pl.when((source >= 0) & own)
        def _():
            for copy in fetch_own(t):
                copy.wait()
            for s in range(SPECIES):
                put_out(t, s).start()

    for t in range(KEEP):
        source, own, slot, came = whence[t]

        @pl.when((source >= 0) & jnp.logical_not(own))
        def _():
            wait_moved(t)
            step_patch(
                mobility, fermi_gain, rates,
                lambda s, rows: cur[t, s, rows, :], lambda f, s, rows: ghost[t, f, s, rows, :],
                coef, base, ping, pong.at[t], lambda s: put_out(t, s).start())

    for copy in zeros:
        copy.wait()
    for t in range(KEEP):
        for s in range(SPECIES):
            put_out(t, s).wait()


def in_vmem():
    return pl.BlockSpec(memory_space=pltpu.VMEM)


def in_smem():
    return pl.BlockSpec(memory_space=pltpu.SMEM)


def anywhere():
    return pl.BlockSpec(memory_space=pl.ANY)


def exchange(nx, ny, conc, neighbours, source, mobility, fermi_gain, rates):
    f32, i32 = jnp.float32, jnp.int32
    dma = pltpu.SemaphoreType.DMA
    n_flags = 3 + nx - 1 + 6
    return pl.pallas_call(
        functools.partial(exchange_kernel, nx, ny),
        out_shape=(
            jax.ShapeDtypeStruct((2, SPECIES, ROWS, 128), f32),
            jax.ShapeDtypeStruct((2, SPECIES, HALF, 128), f32),
            jax.ShapeDtypeStruct((2, SPECIES, HALF, 128), f32),
            jax.ShapeDtypeStruct((4, 6, SPECIES, 8, 128), f32),
            jax.ShapeDtypeStruct((KEEP, SPECIES, ROWS, 128), f32),
            jax.ShapeDtypeStruct((8, 128), i32),
        ),
        in_specs=[anywhere()] + [in_smem()] * 5 + [in_vmem()] * 2,
        out_specs=(anywhere(),) * 5 + (in_vmem(),),
        scratch_shapes=[
            pltpu.VMEM((SPECIES, CAP, B**3), f32),
            pltpu.VMEM((CAP, SPECIES, ROWS, 128), f32),
            pltpu.VMEM((CAP * 6, SPECIES, 8, 128), f32),
            pltpu.VMEM((13, 8, 128), i32),
            pltpu.VMEM((5, 8, 128), i32),
            pltpu.SMEM((5, 8, 128), i32),
            pltpu.VMEM((2, SPECIES, ROWS, 128), f32),
            pltpu.VMEM((2, SPECIES, HALF, 128), f32),
            pltpu.VMEM((2, SPECIES, HALF, 128), f32),
            pltpu.VMEM((2, SPECIES, HALF, 128), f32),
            pltpu.VMEM((4, ROOM, SPECIES, 8, 128), f32),
            pltpu.VMEM((4, ROOM, SPECIES, 8, 128), f32),
            pltpu.VMEM((4, 6, SPECIES, 8, 128), f32),
            pltpu.VMEM((n_flags, 8, 128), i32),
            pltpu.VMEM((6, SPECIES, 8, 128), f32),
            pltpu.VMEM((SPECIES, ROWS, 128), f32),
            pltpu.VMEM((SPECIES, ROWS, 128), f32),
            pltpu.VMEM((ROWS, 128), f32),
            pltpu.VMEM((KEEP, SPECIES, ROWS, 128), f32),
            dma,
            dma((12,)), dma((12,)),
            dma,
            dma((2, SPECIES)), dma((2, SPECIES)), dma((2, SPECIES)), dma((2, SPECIES)),
            dma((2, SPECIES)), dma((2, SPECIES)), dma((2, SPECIES)), dma((2, SPECIES)), dma((4,)), dma((4,)), dma((4,)), dma((4,)),
            dma((n_flags,)), dma((n_flags,)),
            dma((KEEP,)),
        ],
        compiler_params=pltpu.CompilerParams(collective_id=0, has_side_effects=True, vmem_limit_bytes=40 * 2**20),
    )(conc, neighbours, source, mobility, fermi_gain, rates, neighbours, source)


def smooth(nx, ny, landp, landz, landq, landg, swept, source, mobility, fermi_gain, rates):
    f32 = jnp.float32
    dma = pltpu.SemaphoreType.DMA
    return pl.pallas_call(
        functools.partial(smooth_kernel, nx, ny),
        out_shape=jax.ShapeDtypeStruct((SPECIES, CAP, B**3), f32),
        in_specs=[in_smem()] * 4 + [anywhere()] * 5,
        out_specs=anywhere(),
        scratch_shapes=[
            pltpu.VMEM((KEEP, SPECIES, ROWS, 128), f32),
            pltpu.VMEM((KEEP, 6, SPECIES, 8, 128), f32),
            pltpu.VMEM((SPECIES, ROWS, 128), f32),
            pltpu.VMEM((SPECIES, ROWS, 128), f32),
            pltpu.VMEM((ROWS, 128), f32),
            pltpu.VMEM((KEEP, SPECIES, ROWS, 128), f32),
            pltpu.VMEM((1, CAP - KEEP, B**3), f32),
            dma((KEEP,)),
            dma((KEEP,)),
            dma((KEEP,)),
            dma((KEEP, SPECIES)),
            dma((SPECIES,)),
        ],
        compiler_params=pltpu.CompilerParams(vmem_limit_bytes=60 * 2**20),
    )(source, mobility, fermi_gain, rates, landp, landz, landq, landg, swept)


OPPOSITE = (1, 0, 3, 2, 5, 4)


def passed_along(x, axis, by):
    devices = lax.axis_size(axis)
    pairs = [(i, i + by) for i in range(devices) if 0 <= i + by < devices]
    return lax.ppermute(x, axis, pairs)


def with_halo(x, sides, width):
    edges = {}
    for axis, dim in sides:
        devices, length = (lax.axis_size(axis), x.shape[dim])
        up = [(i, (i + 1) % devices) for i in range(devices - 1)]
        last = lax.slice_in_dim(x, length - width, length, axis=dim)
        leading = lax.slice_in_dim(x, 0, width, axis=dim)
        edges[dim] = (
            lax.ppermute(last, axis, up),
            lax.ppermute(leading, axis, [(b, a) for a, b in up]),
        )
    done = []
    for _, dim in sides:
        low, high = edges[dim]
        around = [(width, width) if d in done else (0, 0) for d in range(x.ndim)]
        x = jnp.concatenate([jnp.pad(low, around), x, jnp.pad(high, around)], axis=dim)
        done.append(dim)
    return x


def faces_of(blocks):
    last = blocks.shape[-1] - 1
    return jnp.stack(
        [
            blocks[..., 0, :, :],
            blocks[..., last, :, :],
            blocks[..., :, 0, :],
            blocks[..., :, last, :],
            blocks[..., :, :, 0],
            blocks[..., :, :, last],
        ],
        axis=-4,
    )


def neighbour_sum(iterate, ghosts):
    lower_x = jnp.concatenate([ghosts[0][:, None], iterate[:, :-1]], axis=1)
    upper_x = jnp.concatenate([iterate[:, 1:], ghosts[1][:, None]], axis=1)
    lower_y = jnp.concatenate([ghosts[2][:, :, None], iterate[:, :, :-1]], axis=2)
    upper_y = jnp.concatenate([iterate[:, :, 1:], ghosts[3][:, :, None]], axis=2)
    lower_z = jnp.concatenate([ghosts[4][..., None], iterate[..., :-1]], axis=3)
    upper_z = jnp.concatenate([iterate[..., 1:], ghosts[5][..., None]], axis=3)
    return lower_x + upper_x + lower_y + upper_y + lower_z + upper_z


def smooth_plain(current, ghosts, mobility, fermi_gain, rates):
    dopant_sum = current[0] + current[3] + current[4]
    half_total = 0.5 * dopant_sum
    electrons = half_total + jnp.sqrt(half_total * half_total + 1.0)
    gain_column = fermi_gain[:, None, None, None]
    spread = (
        mobility[:, None, None, None] * (1.0 + gain_column * electrons[None]) / (1.0 + gain_column)
    )
    dopant, interstitial, vacancy, pair_inter, pair_vacancy = (
        current[0],
        current[1],
        current[2],
        current[3],
        current[4],
    )
    forming_ai = rates[0] * dopant * interstitial - rates[1] * pair_inter
    forming_av = rates[2] * dopant * vacancy - rates[3] * pair_vacancy
    recombine = rates[4] * (interstitial * vacancy - 1.0)
    source = jnp.stack(
        [
            dopant - forming_ai - forming_av,
            interstitial - forming_ai - recombine,
            vacancy - forming_av - recombine,
            pair_inter + forming_ai,
            pair_vacancy + forming_av,
        ],
        axis=0,
    )
    diagonal = 1.0 + 6.0 * spread
    iterate = current
    for repeat in range(SWEEPS):
        iterate = (source + spread * neighbour_sum(iterate, ghosts)) / diagonal
    return iterate


def smooth_all(current, ghosts, mobility, fermi_gain, rates):

    def per_patch(paired):
        return smooth_plain(paired[0], paired[1], mobility, fermi_gain, rates)

    return lax.map(per_patch, (current, ghosts))


def gather_ghosts(face_table, neighbours, column_index, row_index, rows_count, capacity):
    face_rows = face_table.reshape(9 * capacity * 6, SPECIES, B, B)
    safe_slot = jnp.maximum(neighbours, 0)
    source_device = safe_slot // capacity
    step_x = source_device // rows_count - column_index + 1
    step_y = source_device % rows_count - row_index + 1
    opposite = jnp.array(OPPOSITE, jnp.int32)
    face_ids = jnp.arange(6, dtype=jnp.int32)
    remote = ((step_x * 3 + step_y) * capacity + safe_slot % capacity) * 6 + opposite[None, :]
    local = (4 * capacity + jnp.arange(capacity, dtype=jnp.int32)[:, None]) * 6 + face_ids[None, :]
    picked = jnp.clip(jnp.where(neighbours >= 0, remote, local), 0, 9 * capacity * 6 - 1)
    one = functools.partial(lax.dynamic_index_in_dim, face_rows, axis=0, keepdims=False)
    ghosts = lax.map(one, picked.reshape(-1))
    return ghosts.reshape(picked.shape + face_rows.shape[1:])


def counted(hits):
    places = jnp.arange(hits.shape[0])
    before = places[None, :] <= places[:, None]
    return jnp.sum(jnp.where(before & hits[None, :], 1, 0), axis=1) - 1


def pick_rows(pulls, this_device, capacity, payload):
    wanted = (pulls >= 0) & (pulls // capacity == this_device)
    position = counted(wanted)
    chosen = wanted[None, :] & (position[None, :] == jnp.arange(MOVE, dtype=jnp.int32)[:, None])
    slot_list = jnp.sum(jnp.where(chosen, pulls % capacity, 0), axis=1)
    return payload[slot_list]


def place_rows(index, source_device, sender, start):
    from_sender = (source_device == sender) & (source_device >= 0)
    position = counted(from_sender)
    return jnp.where(from_sender, start + position, index)


def relocate(payload, source_slot, requests, this_device, rows_count, capacity):
    source_device = jnp.where(source_slot >= 0, source_slot // capacity, -1)
    index = jnp.where(
        (source_slot >= 0) & (source_device == this_device), source_slot % capacity, -1
    )
    pieces = [payload]
    start = capacity
    for offset in (1, -1):
        outgoing = pick_rows(requests[1 + offset, 1], this_device, capacity, payload)
        arrived = passed_along(outgoing, "gx", offset)
        index = place_rows(index, source_device, this_device - offset * rows_count, start)
        pieces.append(arrived)
        start = start + MOVE
    for offset in (1, -1):
        outgoing = pick_rows(requests[1, 1 + offset], this_device, capacity, payload)
        arrived = passed_along(outgoing, "gy", offset)
        index = place_rows(index, source_device, this_device - offset, start)
        pieces.append(arrived)
        start = start + MOVE
    candidates = jnp.concatenate(pieces, axis=0)
    gathered = candidates[jnp.maximum(index, 0)]
    return jnp.where((index >= 0)[:, None], gathered, jnp.zeros_like(gathered))


def general(concentration, neighbours, source_slot, mobility, fermi_gain, rates):
    capacity = concentration.shape[0]
    cells = concentration.shape[2]
    column_index = lax.axis_index("gx")
    row_index = lax.axis_index("gy")
    rows_count = lax.axis_size("gy")
    this_device = column_index * rows_count + row_index
    blocks = concentration.reshape(capacity, SPECIES, B, B, B)
    own_faces = faces_of(blocks).reshape(1, 1, capacity, 6, SPECIES, B * B)
    face_table = with_halo(own_faces, (("gx", 0), ("gy", 1)), 1)
    requests = with_halo(source_slot.reshape(1, 1, capacity), (("gx", 0), ("gy", 1)), 1)
    ghosts = gather_ghosts(face_table, neighbours, column_index, row_index, rows_count, capacity)
    working = KEEP - 1 + MOVE
    payload = jnp.concatenate(
        [
            concentration.reshape(capacity, SPECIES * cells),
            ghosts.reshape(capacity, 6 * SPECIES * B * B),
        ],
        axis=1,
    )
    arrived = relocate(payload, source_slot, requests, this_device, rows_count, capacity)[:working]
    current = arrived[:, : SPECIES * cells].reshape(working, SPECIES, B, B, B)
    layers = arrived[:, SPECIES * cells :].reshape(working, 6, SPECIES, B, B)
    swept = smooth_all(current, layers, mobility, fermi_gain, rates).reshape(
        working, SPECIES, cells
    )
    live_rows = (source_slot[:working] >= 0)[:, None, None]
    swept = jnp.where(live_rows, swept, jnp.zeros_like(swept))
    return jnp.concatenate(
        [swept, jnp.zeros((capacity - working, SPECIES, cells), jnp.float32)], axis=0
    )


def body(nx, ny, concentration, neighbours, source_slot, mobility, fermi_gain, rates):
    source = source_slot.reshape(1, CAP)
    conc = concentration.transpose(1, 0, 2)
    landp, landz, landq, landg, swept, flag = exchange(nx, ny, conc, neighbours, source, mobility, fermi_gain, rates)

    def common():
        return smooth(nx, ny, landp, landz, landq, landg, swept, source, mobility, fermi_gain, rates).transpose(1, 0, 2)

    def crowded():
        return general(concentration, neighbours, source_slot, mobility, fermi_gain, rates)

    return lax.cond(flag[0, 0] == 0, common, crowded)


def solution(mesh):
    placed = (P(("gx", "gy"), None, None), P(("gx", "gy"), None), P(("gx", "gy")), P(), P(), P())
    return jax.shard_map(
        functools.partial(body, mesh.shape["gx"], mesh.shape["gy"]),
        mesh=mesh, in_specs=placed, out_specs=P(("gx", "gy"), None, None), check_vma=False,
    )
```

```python
import functools

import jax
import jax.numpy as jnp
from jax import lax
from jax.experimental import pallas as pl
from jax.experimental.pallas import tpu as pltpu
from jax.sharding import PartitionSpec as P

B = 32
SPECIES = 5
SWEEPS = 3
KEEP = 2
MOVE = 1
CAP = 6
ROWS = 256
EARLY = 12
ROOM = 6
MESH = pl.DeviceIdType.MESH

NEAR = ((-1, 0), (1, 0), (0, -1), (0, 1))
FAR = ((-2, 0), (2, 0), (0, -2), (0, 2), (-1, -1), (-1, 1), (1, -1), (1, 1))
AROUND = NEAR + FAR
ORDER = (2, 3, 0, 1)
HALF = ROWS // 2
PLACE = {(0, 0): 0, **{step: i + 1 for i, step in enumerate(AROUND)}}


def iota(shape, dim):
    return lax.broadcasted_iota(jnp.int32, shape, dim)


def prepare_patch(mobility, fermi_gain, rates, cell, coef, base):
    scale = [mobility[s] / jnp.full((8, 128), 1.0 + fermi_gain[s]) for s in range(SPECIES)]

    def planes(xo, carry):
        for xi in range(8):
            plane = pl.ds(pl.multiple_of(xo * 64 + xi * 8, 8), 8)
            a, i, v, p, q = [cell(s, plane) for s in range(SPECIES)]
            half = 0.5 * (a + p + q)
            electrons = half + jnp.sqrt(half * half + 1.0)
            ai = rates[0] * a * i - rates[1] * p
            av = rates[2] * a * v - rates[3] * q
            re = rates[4] * (i * v - 1.0)
            sources = (a - ai - av, i - ai - re, v - av - re, p + ai, q + av)
            for s in range(SPECIES):
                spread = scale[s] * (1.0 + fermi_gain[s] * electrons)
                inverse = 1.0 / (1.0 + 6.0 * spread)
                coef[s, plane, :] = spread * inverse
                base[s, plane, :] = sources[s] * inverse
        return carry

    lax.fori_loop(0, 4, planes, 0)


def sweep_patch(cell, layer, coef, base, ping, result, finish):
    lane = iota((8, 128), 1)
    sub = iota((8, 128), 0)
    z = lane % 32
    first_y = (sub == 0) & (lane < 32)
    last_y = (sub == 7) & (lane >= 96)
    whole = pl.ds(0, 8)

    def ghosts(s):
        for x in range(B):
            plane = pl.ds(8 * x, 8)
            low = pltpu.roll(layer(4, s, whole), (128 - x) % 128, 1) if x else layer(4, s, whole)
            high = pltpu.roll(layer(5, s, whole), 31 - x, 1) if x < 31 else layer(5, s, whole)
            extra = jnp.where(z == 0, low, jnp.where(z == 31, high, 0.0))
            low = jnp.broadcast_to(layer(2, s, pl.ds(x % 8, 1)), (8, 128))
            high = jnp.broadcast_to(layer(3, s, pl.ds(x % 8, 1)), (8, 128))
            xo = x // 8
            low = pltpu.roll(low, 128 - 32 * xo, 1) if xo else low
            high = pltpu.roll(high, 96 - 32 * xo, 1) if xo < 3 else high
            extra = extra + jnp.where(first_y, low, jnp.where(last_y, high, 0.0))
            if x == 0:
                extra = extra + layer(0, s, whole)
            if x == B - 1:
                extra = extra + layer(1, s, whole)
            base[s, plane, :] = base[s, plane, :] + coef[s, plane, :] * extra

    def species(s, carry):
        def sweep(get, put):
            before = None
            here = get(0)
            for x in range(B):
                after = get(x + 1) if x + 1 < B else None
                total = jnp.where(z == 0, 0.0, pltpu.roll(here, 1, 1)) + jnp.where(z == 31, 0.0, pltpu.roll(here, 127, 1))
                down = pltpu.roll(here, 32, 1)
                down = jnp.where(lane >= 32, down, pltpu.roll(down, 1, 0))
                up = pltpu.roll(here, 96, 1)
                up = jnp.where(lane < 96, up, pltpu.roll(up, 7, 0))
                total = total + jnp.where(first_y, 0.0, down) + jnp.where(last_y, 0.0, up)
                if before is not None:
                    total = total + before
                if after is not None:
                    total = total + after
                put(x, base[s, 8 * x:8 * x + 8, :] + coef[s, 8 * x:8 * x + 8, :] * total)
                before, here = here, after

        def put_ping(x, value):
            ping[8 * x:8 * x + 8, :] = value

        def put_result(x, value):
            result[s, 8 * x:8 * x + 8, :] = value

        ghosts(s)
        sweep(lambda x: cell(s, pl.ds(8 * x, 8)), put_result)
        sweep(lambda x: result[s, 8 * x:8 * x + 8, :], put_ping)
        sweep(lambda x: ping[8 * x:8 * x + 8, :], put_result)
        finish(s)
        return carry

    lax.fori_loop(0, SPECIES, species, 0)


def exchange_kernel(
    nx, ny,
    conc, nbr_s, src_s, mobility, fermi_gain, rates, nbr_v, src_v,
    landp, landz, landq, landg, swept, flag_out,
    raw, dense, own_faces, meta, table, table_s, sendp, sendq, heldq, sendz, sendf, landf, sendg, flags, ghost, coef, base, ping, result,
    in_sem, meta_ss, meta_rs, tab_sem, p_ss, p_rs, q_ss, q_rs, z_ss, z_rs, h_ss, h_rs, f_ss, f_rs, g_ss, g_rs, fl_ss, fl_rs, out_sem,
):
    gx, gy = lax.axis_index("gx"), lax.axis_index("gy")
    me = gx * ny + gy

    def inside(step):
        x, y = gx + step[0], gy + step[1]
        return (x >= 0) & (x < nx) & (y >= 0) & (y < ny)

    def at(step):
        return (gx + step[0], gy + step[1])

    load = pltpu.make_async_copy(conc, raw, in_sem)
    load.start()

    row, col = gy // 4, gy % 4
    ring = (
        [(gx, row * 4 + (col + k) % 4) for k in range(1, 4)],
        [((gx + k) % nx, gy) for k in range(1, nx)],
        [(gx, ((row + k) % 4) * 4 + col) for k in range(1, 4)],
    )

    meta[...] = jnp.full(meta.shape, -1, jnp.int32)
    meta[0, 0:CAP, 0:6] = nbr_v[...]
    meta[0, CAP:CAP + 1, 0:CAP] = src_v[...]

    barrier = pltpu.get_barrier_semaphore()
    expected = nx - 1 + 6
    for step in AROUND:
        there = inside(step)
        expected = expected + there.astype(jnp.int32)

        @pl.when(there)
        def _():
            pl.semaphore_signal(barrier, inc=1, device_id=at(step), device_id_type=MESH)
    for group in ring:
        for target in group:
            pl.semaphore_signal(barrier, inc=1, device_id=target, device_id_type=MESH)
    load.wait()

    def spread_out(k, carry):
        s, x = k // B, k % B
        planes = raw[s, :, pl.ds(pl.multiple_of(x * 1024, 1024), 1024)].reshape(CAP, 8, 128)
        for q in range(CAP):
            dense[q, s, pl.ds(pl.multiple_of(x * 8, 8), 8), :] = planes[q]
        return carry

    lax.fori_loop(0, SPECIES * B, spread_out, 0)

    lane8 = iota((8, 128), 1)

    def faces(k, carry):
        q, s = k // SPECIES, k % SPECIES
        own_faces[q * 6 + 0, s] = dense[q, s, 0:8, :]
        own_faces[q * 6 + 1, s] = dense[q, s, ROWS - 8:ROWS, :]
        low = jnp.zeros((8, 128), jnp.float32)
        high = jnp.zeros((8, 128), jnp.float32)
        for b in range(4):
            first = dense[q, s, pl.ds(64 * b, 8, stride=8), :]
            final = dense[q, s, pl.ds(64 * b + 7, 8, stride=8), :]
            here = lane8 // 32 == b
            low = jnp.where(here, pltpu.roll(first, 32 * b, 1) if b else first, low)
            high = jnp.where(here, pltpu.roll(final, 32 * (b + 1), 1) if b < 3 else final, high)
        own_faces[q * 6 + 2, s] = low
        own_faces[q * 6 + 3, s] = high
        low = jnp.zeros((8, 128), jnp.float32)
        high = jnp.zeros((8, 128), jnp.float32)
        for x in range(B):
            turned = pltpu.roll(dense[q, s, 8 * x:8 * x + 8, :], x + 1, 1)
            high = jnp.where(lane8 % 32 == x, turned, high)
            low = jnp.where(lane8 % 32 == (x + 1) % 32, turned, low)
        own_faces[q * 6 + 4, s] = pltpu.roll(low, 127, 1)
        own_faces[q * 6 + 5, s] = pltpu.roll(high, 96, 1)
        return carry

    lax.fori_loop(0, EARLY, faces, 0)
    pl.semaphore_wait(barrier, expected)

    def opposite(i):
        return AROUND.index((-AROUND[i][0], -AROUND[i][1]))

    def meta_send(i):
        return pltpu.make_async_remote_copy(
            src_ref=meta.at[0], dst_ref=meta.at[1 + opposite(i)],
            send_sem=meta_ss.at[i], recv_sem=meta_rs.at[opposite(i)], device_id=at(AROUND[i]), device_id_type=MESH)

    for i, step in enumerate(AROUND):
        @pl.when(inside(step))
        def _():
            meta_send(i).start()

    lax.fori_loop(EARLY, CAP * SPECIES, faces, 0)

    for i, step in enumerate(AROUND):
        @pl.when(inside(step))
        def _():
            meta_send(i).wait_send()
            pltpu.make_async_remote_copy(
                src_ref=meta.at[0], dst_ref=meta.at[1 + i], send_sem=meta_ss.at[i], recv_sem=meta_rs.at[i],
                device_id=at(step), device_id_type=MESH).wait_recv()

    def device(step):
        return me + step[0] * ny + step[1]

    def sources(step):
        return meta[PLACE[step], CAP:CAP + 1, :]

    taken = []
    for d, step in enumerate(NEAR):
        rel = sources(step) - me * CAP
        slot = jnp.max(jnp.where((rel >= 0) & (rel < CAP), rel, -1))
        taken.append(slot)
    safe = [jnp.maximum(slot, 0) for slot in taken]
    asked = [slot >= 0 for slot in taken]

    def patch_send(d, s):
        return pltpu.make_async_remote_copy(
            src_ref=sendp.at[d, s], dst_ref=landp.at[d ^ 1, s], send_sem=p_ss.at[d, s], recv_sem=p_rs.at[d ^ 1, s],
            device_id=at(NEAR[d]), device_id_type=MESH)

    def patch_wait(d, s):
        return pltpu.make_async_remote_copy(
            src_ref=sendp.at[d, s], dst_ref=landp.at[d, s], send_sem=p_ss.at[d, s], recv_sem=p_rs.at[d, s],
            device_id=at(NEAR[d]), device_id_type=MESH)

    core = gx % 2
    twin = (gx + 1 - 2 * core, gy)
    mine_first, twin_first = core * HALF, (1 - core) * HALF

    def copy_along(src, dst, ss, rs, target):
        return pltpu.make_async_remote_copy(
            src_ref=src, dst_ref=dst, send_sem=ss, recv_sem=rs, device_id=target, device_id_type=MESH)

    def give(e, s):
        return copy_along(sendq.at[e, s], heldq.at[e, s], q_ss.at[e, s], q_rs.at[e, s], twin)

    def carry_send(e, s):
        return copy_along(sendz.at[e, s], landz.at[1 - e, s], z_ss.at[e, s], z_rs.at[1 - e, s], at(NEAR[2 + e]))

    def carry_wait(e, s):
        return copy_along(sendz.at[e, s], landz.at[e, s], z_ss.at[e, s], z_rs.at[e, s], at(NEAR[2 + e]))

    def hand(e, s):
        return copy_along(landz.at[e, s], landq.at[e, s], h_ss.at[e, s], h_rs.at[e, s], twin)

    for s in range(SPECIES):
        for e in range(2):
            @pl.when(inside(NEAR[2 + e]))
            def _():
                sendq[e, s] = dense[safe[2 + e], s, pl.ds(pl.multiple_of(twin_first, HALF), HALF), :]
                give(e, s).start()

    def straight():
        for d in range(2):
            @pl.when(inside(NEAR[d]))
            def _():
                for s in range(SPECIES):
                    sendp[d, s] = dense[safe[d], s]
                    patch_send(d, s).start()


    def face_send(d):
        return pltpu.make_async_remote_copy(
            src_ref=sendf.at[d], dst_ref=landf.at[d ^ 1], send_sem=f_ss.at[d], recv_sem=f_rs.at[d ^ 1],
            device_id=at(NEAR[d]), device_id_type=MESH)

    def face_wait(d):
        return pltpu.make_async_remote_copy(
            src_ref=sendf.at[d], dst_ref=landf.at[d], send_sem=f_ss.at[d], recv_sem=f_rs.at[d],
            device_id=at(NEAR[d]), device_id_type=MESH)

    def ghost_send(d):
        return pltpu.make_async_remote_copy(
            src_ref=sendg.at[d], dst_ref=landg.at[d ^ 1], send_sem=g_ss.at[d], recv_sem=g_rs.at[d ^ 1],
            device_id=at(NEAR[d]), device_id_type=MESH)

    def ghost_wait(d):
        return pltpu.make_async_remote_copy(
            src_ref=sendg.at[d], dst_ref=landg.at[d], send_sem=g_ss.at[d], recv_sem=g_rs.at[d],
            device_id=at(NEAR[d]), device_id_type=MESH)

    side = iota((8, 128), 1)
    far_side = side + 1 - 2 * (side % 2)
    slot_row = iota((8, 128), 0)
    lane1 = iota((1, 128), 1)

    def named(step):
        owner = device(step)
        hit = jnp.zeros((8, 128), jnp.bool_)
        for extra in ((0, 0),) + NEAR:
            hit = hit | (sources((step[0] + extra[0], step[1] + extra[1])) == owner * CAP + slot_row)
        return jnp.max(hit.astype(jnp.int32), axis=1, keepdims=True) > 0

    def wanted(step, of, names):
        rel = meta[PLACE[step]] - device(of) * CAP
        good = names & (rel >= 0) & (rel < CAP) & (slot_row < CAP) & (side < 6)
        code = jnp.where(good, rel * 6 + far_side, 127)
        hit = jnp.zeros((8, 128), jnp.bool_)
        for f in range(6):
            hit = hit | (code[:, f:f + 1] == side)
        mask = jnp.max(hit.astype(jnp.int32), axis=0, keepdims=True)
        mask = jnp.where(lane1 < 36, mask, 0)
        total = mask
        for k in (1, 2, 4, 8, 16, 32):
            total = total + jnp.where(lane1 >= k, pltpu.roll(total, k, 1), 0)
        return mask, total - mask

    mine = named((0, 0))
    over = jnp.zeros((8, 128), jnp.int32)
    for d, step in enumerate(NEAR):
        mask, rank = wanted(step, (0, 0), named(step))
        over = jnp.maximum(over, jnp.where((mask > 0) & (rank >= ROOM), 1, 0))
        chosen = jnp.where((mask > 0) & (rank == slot_row), side, 0)
        table[d] = jnp.broadcast_to(jnp.max(chosen, axis=1, keepdims=True), (8, 128))
        _, rank = wanted((0, 0), step, mine)
        table[4, d:d + 1, :] = rank
    over = jnp.broadcast_to(jnp.max(jnp.max(over, axis=1, keepdims=True), axis=0, keepdims=True), (8, 128))
    twin_base = (me + (1 - 2 * core) * ny) * CAP
    for e, dy in enumerate((-1, 1)):
        rel = sources((0, dy)) - me * CAP
        other = jnp.where(core == 0, sources((1, dy)), sources((-1, dy))) - twin_base
        both = jnp.where((rel >= 0) & (rel < CAP), 1, 0) * jnp.max(
            jnp.where((other >= 0) & (other < CAP), 1, 0), axis=1, keepdims=True)
        over = jnp.maximum(over, jnp.max(both, axis=1, keepdims=True))
    flags[0] = over
    to_scalars = pltpu.make_async_copy(table, table_s, tab_sem)
    to_scalars.start()

    def flag_copy(base, k, target, held):
        return pltpu.make_async_remote_copy(
            src_ref=flags.at[held], dst_ref=flags.at[base + k], send_sem=fl_ss.at[base + k],
            recv_sem=fl_rs.at[base + k], device_id=target, device_id_type=MESH)

    bases = (3, 6, 6 + nx - 1)

    for k, target in enumerate(ring[0]):
        flag_copy(bases[0], k, target, 0).start()

    to_scalars.wait()
    for d in ORDER:
        @pl.when(inside(NEAR[d]))
        def _():
            def stage(p, carry):
                sendf[d, p] = own_faces[table_s[d, p, 0]]
                return carry
            lax.fori_loop(0, ROOM, stage, 0)
            face_send(d).start()

    straight()
    for s in range(SPECIES):
        for e in range(2):
            @pl.when(inside(NEAR[2 + e]))
            def _():
                give(e, s).wait_recv()
                own = dense[safe[2 + e], s, pl.ds(pl.multiple_of(mine_first, HALF), HALF), :]
                sendz[e, s] = jnp.where(asked[2 + e], own, heldq[e, s])
                carry_send(e, s).start()

    def flag_round(n, held, following):
        for k, target in enumerate(ring[n]):
            copy = flag_copy(bases[n], k, target, held)
            copy.wait()
        total = flags[held]
        for k in range(len(ring[n])):
            total = jnp.maximum(total, flags[bases[n] + k])
        if following is None:
            flag_out[...] = total
        else:
            flags[following] = total
            for k, target in enumerate(ring[n + 1]):
                flag_copy(bases[n + 1], k, target, following).start()

    kept = []
    for t in range(KEEP):
        rel = src_s[0, t] - me * CAP
        kept.append(jnp.where((rel >= 0) & (rel < CAP), rel, 0))

    def ready(t, carry):
        slot = jnp.where(t == 0, kept[0], kept[1])
        prepare_patch(
            mobility, fermi_gain, rates, lambda s, rows: dense[slot, s, rows, :], coef.at[t], base.at[t])
        return carry
    lax.fori_loop(0, KEEP, ready, 0)

    for d, step in enumerate(NEAR):
        @pl.when(inside(step))
        def _():
            face_wait(d).wait_recv()

    def ghost_place(slot, f):
        nb = nbr_s[slot, f]
        rel = nb - me * CAP
        here = (rel >= 0) & (rel < CAP)
        opposite_f = f + 1 - 2 * (f % 2)
        own = jnp.where(here, rel * 6 + opposite_f, slot * 6 + f)
        own = jnp.where((nb < 0) | here, own, 0)
        away = jnp.int32(-1)
        for d, step in enumerate(NEAR):
            rel = nb - device(step) * CAP
            there = (nb >= 0) & (rel >= 0) & (rel < CAP)
            code = jnp.where(there, rel * 6 + opposite_f, 0)
            away = jnp.where(there, d * ROOM + jnp.minimum(table_s[4, d, code], ROOM - 1), away)
        return own, away

    def ghost_value(slot, f):
        own, away = ghost_place(slot, f)
        other = jnp.maximum(away, 0)
        return jnp.where(away >= 0, landf[other // ROOM, other % ROOM], own_faces[own])

    for d, step in enumerate(NEAR):
        @pl.when(inside(step))
        def _():
            def stage(f, carry):
                sendg[d, f] = ghost_value(safe[d], f)
                return carry
            lax.fori_loop(0, 6, stage, 0)
            ghost_send(d).start()

    flag_round(0, 0, 1)

    def stay(t):
        slot = kept[t]

        def layer(f, carry):
            ghost[f] = ghost_value(slot, f)
            return carry
        lax.fori_loop(0, 6, layer, 0)
        sweep_patch(
            lambda s, rows: dense[slot, s, rows, :], lambda f, s, rows: ghost[f, s, rows, :],
            coef.at[t], base.at[t], ping, result.at[t], lambda s: None)
        pltpu.make_async_copy(result.at[t], swept.at[t], out_sem.at[t]).start()

    stay(0)
    flag_round(1, 1, 2)
    for s in range(SPECIES):
        for e in range(2):
            @pl.when(inside(NEAR[2 + e]))
            def _():
                carry_wait(e, s).wait_recv()
                hand(e, s).start()
    stay(1)

    flag_round(2, 2, None)

    for d, step in enumerate(NEAR):
        @pl.when(inside(step))
        def _():
            face_send(d).wait_send()
            ghost_send(d).wait_send()
            for s in range(SPECIES):
                if d < 2:
                    patch_send(d, s).wait_send()
                    patch_wait(d, s).wait_recv()
                else:
                    give(d - 2, s).wait_send()
                    carry_send(d - 2, s).wait_send()
                    hand(d - 2, s).wait()
            ghost_wait(d).wait_recv()
    for t in range(KEEP):
        pltpu.make_async_copy(result.at[t], swept.at[t], out_sem.at[t]).wait()


def smooth_kernel(
    nx, ny,
    src_s, mobility, fermi_gain, rates, landp, landz, landq, landg, swept,
    out,
    cur, ghost, coef, base, ping, pong, blank, cur_sem, half_sem, ghost_sem, out_sem, zero_sem,
):
    gx, gy = lax.axis_index("gx"), lax.axis_index("gy")
    me = gx * ny + gy
    whence = []
    for t in range(KEEP):
        source = src_s[0, t]
        rel = source - me * CAP
        own = (rel >= 0) & (rel < CAP)
        came = jnp.int32(0)
        for d, step in enumerate(NEAR):
            away = source - (me + step[0] * ny + step[1]) * CAP
            came = jnp.where((away >= 0) & (away < CAP), d, came)
        whence.append((source, own, jnp.where(own, rel, 0), came))

    def fetch_own(t):
        return (pltpu.make_async_copy(swept.at[t], pong.at[t], cur_sem.at[t]),)

    core = gx % 2

    def fetch_moved(t):
        came = whence[t][3]
        e = jnp.maximum(came - 2, 0)
        straight = (
            pltpu.make_async_copy(landp.at[jnp.minimum(came, 1)], cur.at[t], cur_sem.at[t]),
        )
        halves = (
            pltpu.make_async_copy(landz.at[e], cur.at[t, :, pl.ds(pl.multiple_of(core * HALF, HALF), HALF), :], cur_sem.at[t]),
            pltpu.make_async_copy(landq.at[e], cur.at[t, :, pl.ds(pl.multiple_of((1 - core) * HALF, HALF), HALF), :], half_sem.at[t]),
        )
        layers = pltpu.make_async_copy(landg.at[came], ghost.at[t], ghost_sem.at[t])
        return straight, halves, layers

    def start_moved(t):
        straight, halves, layers = fetch_moved(t)
        layers.start()

        @pl.when(whence[t][3] < 2)
        def _():
            straight[0].start()

        @pl.when(whence[t][3] >= 2)
        def _():
            halves[0].start()
            halves[1].start()

    def wait_moved(t):
        straight, halves, layers = fetch_moved(t)
        layers.wait()

        @pl.when(whence[t][3] < 2)
        def _():
            straight[0].wait()

        @pl.when(whence[t][3] >= 2)
        def _():
            halves[0].wait()
            halves[1].wait()

    for t in range(KEEP):
        source, own, slot, came = whence[t]

        @pl.when((source >= 0) & own)
        def _():
            for copy in fetch_own(t):
                copy.start()

        @pl.when((source >= 0) & jnp.logical_not(own))
        def _():
            start_moved(t)

    blank[...] = jnp.zeros(blank.shape, jnp.float32)
    zeros = [
        pltpu.make_async_copy(blank, out.at[pl.ds(s, 1), pl.ds(KEEP, CAP - KEEP), :], zero_sem.at[s])
        for s in range(SPECIES)
    ]
    for copy in zeros:
        copy.start()
    def put_out(t, s):
        return pltpu.make_async_copy(
            pong.at[t, pl.ds(s, 1)].reshape(1, 1, B**3), out.at[pl.ds(s, 1), pl.ds(t, 1), :], out_sem.at[t, s])

    for t in range(KEEP):
        source, own, slot, came = whence[t]

        @pl.when(source < 0)
        def _():
            pong[t] = jnp.zeros((SPECIES, ROWS, 128), jnp.float32)
            for s in range(SPECIES):
                put_out(t, s).start()

        @pl.when((source >= 0) & own)
        def _():
            for copy in fetch_own(t):
                copy.wait()
            for s in range(SPECIES):
                put_out(t, s).start()

    for t in range(KEEP):
        source, own, slot, came = whence[t]

        @pl.when((source >= 0) & jnp.logical_not(own))
        def _():
            wait_moved(t)
            prepare_patch(mobility, fermi_gain, rates, lambda s, rows: cur[t, s, rows, :], coef, base)
            sweep_patch(
                lambda s, rows: cur[t, s, rows, :], lambda f, s, rows: ghost[t, f, s, rows, :], coef, base, ping, pong.at[t],
                lambda s: put_out(t, s).start())

    for copy in zeros:
        copy.wait()
    for t in range(KEEP):
        for s in range(SPECIES):
            put_out(t, s).wait()


def in_vmem():
    return pl.BlockSpec(memory_space=pltpu.VMEM)


def in_smem():
    return pl.BlockSpec(memory_space=pltpu.SMEM)


def anywhere():
    return pl.BlockSpec(memory_space=pl.ANY)


def exchange(nx, ny, conc, neighbours, source, mobility, fermi_gain, rates):
    f32, i32 = jnp.float32, jnp.int32
    dma = pltpu.SemaphoreType.DMA
    n_flags = 3 + nx - 1 + 6
    return pl.pallas_call(
        functools.partial(exchange_kernel, nx, ny),
        out_shape=(
            jax.ShapeDtypeStruct((2, SPECIES, ROWS, 128), f32),
            jax.ShapeDtypeStruct((2, SPECIES, HALF, 128), f32),
            jax.ShapeDtypeStruct((2, SPECIES, HALF, 128), f32),
            jax.ShapeDtypeStruct((4, 6, SPECIES, 8, 128), f32),
            jax.ShapeDtypeStruct((KEEP, SPECIES, ROWS, 128), f32),
            jax.ShapeDtypeStruct((8, 128), i32),
        ),
        in_specs=[anywhere()] + [in_smem()] * 5 + [in_vmem()] * 2,
        out_specs=(anywhere(),) * 5 + (in_vmem(),),
        scratch_shapes=[
            pltpu.VMEM((SPECIES, CAP, B**3), f32),
            pltpu.VMEM((CAP, SPECIES, ROWS, 128), f32),
            pltpu.VMEM((CAP * 6, SPECIES, 8, 128), f32),
            pltpu.VMEM((13, 8, 128), i32),
            pltpu.VMEM((5, 8, 128), i32),
            pltpu.SMEM((5, 8, 128), i32),
            pltpu.VMEM((2, SPECIES, ROWS, 128), f32),
            pltpu.VMEM((2, SPECIES, HALF, 128), f32),
            pltpu.VMEM((2, SPECIES, HALF, 128), f32),
            pltpu.VMEM((2, SPECIES, HALF, 128), f32),
            pltpu.VMEM((4, ROOM, SPECIES, 8, 128), f32),
            pltpu.VMEM((4, ROOM, SPECIES, 8, 128), f32),
            pltpu.VMEM((4, 6, SPECIES, 8, 128), f32),
            pltpu.VMEM((n_flags, 8, 128), i32),
            pltpu.VMEM((6, SPECIES, 8, 128), f32),
            pltpu.VMEM((KEEP, SPECIES, ROWS, 128), f32),
            pltpu.VMEM((KEEP, SPECIES, ROWS, 128), f32),
            pltpu.VMEM((ROWS, 128), f32),
            pltpu.VMEM((KEEP, SPECIES, ROWS, 128), f32),
            dma,
            dma((12,)), dma((12,)),
            dma,
            dma((2, SPECIES)), dma((2, SPECIES)), dma((2, SPECIES)), dma((2, SPECIES)),
            dma((2, SPECIES)), dma((2, SPECIES)), dma((2, SPECIES)), dma((2, SPECIES)), dma((4,)), dma((4,)), dma((4,)), dma((4,)),
            dma((n_flags,)), dma((n_flags,)),
            dma((KEEP,)),
        ],
        compiler_params=pltpu.CompilerParams(collective_id=0, has_side_effects=True, vmem_limit_bytes=40 * 2**20),
    )(conc, neighbours, source, mobility, fermi_gain, rates, neighbours, source)


def smooth(nx, ny, landp, landz, landq, landg, swept, source, mobility, fermi_gain, rates):
    f32 = jnp.float32
    dma = pltpu.SemaphoreType.DMA
    return pl.pallas_call(
        functools.partial(smooth_kernel, nx, ny),
        out_shape=jax.ShapeDtypeStruct((SPECIES, CAP, B**3), f32),
        in_specs=[in_smem()] * 4 + [anywhere()] * 5,
        out_specs=anywhere(),
        scratch_shapes=[
            pltpu.VMEM((KEEP, SPECIES, ROWS, 128), f32),
            pltpu.VMEM((KEEP, 6, SPECIES, 8, 128), f32),
            pltpu.VMEM((SPECIES, ROWS, 128), f32),
            pltpu.VMEM((SPECIES, ROWS, 128), f32),
            pltpu.VMEM((ROWS, 128), f32),
            pltpu.VMEM((KEEP, SPECIES, ROWS, 128), f32),
            pltpu.VMEM((1, CAP - KEEP, B**3), f32),
            dma((KEEP,)),
            dma((KEEP,)),
            dma((KEEP,)),
            dma((KEEP, SPECIES)),
            dma((SPECIES,)),
        ],
        compiler_params=pltpu.CompilerParams(vmem_limit_bytes=60 * 2**20),
    )(source, mobility, fermi_gain, rates, landp, landz, landq, landg, swept)


OPPOSITE = (1, 0, 3, 2, 5, 4)


def passed_along(x, axis, by):
    devices = lax.axis_size(axis)
    pairs = [(i, i + by) for i in range(devices) if 0 <= i + by < devices]
    return lax.ppermute(x, axis, pairs)


def with_halo(x, sides, width):
    edges = {}
    for axis, dim in sides:
        devices, length = (lax.axis_size(axis), x.shape[dim])
        up = [(i, (i + 1) % devices) for i in range(devices - 1)]
        last = lax.slice_in_dim(x, length - width, length, axis=dim)
        leading = lax.slice_in_dim(x, 0, width, axis=dim)
        edges[dim] = (
            lax.ppermute(last, axis, up),
            lax.ppermute(leading, axis, [(b, a) for a, b in up]),
        )
    done = []
    for _, dim in sides:
        low, high = edges[dim]
        around = [(width, width) if d in done else (0, 0) for d in range(x.ndim)]
        x = jnp.concatenate([jnp.pad(low, around), x, jnp.pad(high, around)], axis=dim)
        done.append(dim)
    return x


def faces_of(blocks):
    last = blocks.shape[-1] - 1
    return jnp.stack(
        [
            blocks[..., 0, :, :],
            blocks[..., last, :, :],
            blocks[..., :, 0, :],
            blocks[..., :, last, :],
            blocks[..., :, :, 0],
            blocks[..., :, :, last],
        ],
        axis=-4,
    )


def neighbour_sum(iterate, ghosts):
    lower_x = jnp.concatenate([ghosts[0][:, None], iterate[:, :-1]], axis=1)
    upper_x = jnp.concatenate([iterate[:, 1:], ghosts[1][:, None]], axis=1)
    lower_y = jnp.concatenate([ghosts[2][:, :, None], iterate[:, :, :-1]], axis=2)
    upper_y = jnp.concatenate([iterate[:, :, 1:], ghosts[3][:, :, None]], axis=2)
    lower_z = jnp.concatenate([ghosts[4][..., None], iterate[..., :-1]], axis=3)
    upper_z = jnp.concatenate([iterate[..., 1:], ghosts[5][..., None]], axis=3)
    return lower_x + upper_x + lower_y + upper_y + lower_z + upper_z


def smooth_plain(current, ghosts, mobility, fermi_gain, rates):
    dopant_sum = current[0] + current[3] + current[4]
    half_total = 0.5 * dopant_sum
    electrons = half_total + jnp.sqrt(half_total * half_total + 1.0)
    gain_column = fermi_gain[:, None, None, None]
    spread = (
        mobility[:, None, None, None] * (1.0 + gain_column * electrons[None]) / (1.0 + gain_column)
    )
    dopant, interstitial, vacancy, pair_inter, pair_vacancy = (
        current[0],
        current[1],
        current[2],
        current[3],
        current[4],
    )
    forming_ai = rates[0] * dopant * interstitial - rates[1] * pair_inter
    forming_av = rates[2] * dopant * vacancy - rates[3] * pair_vacancy
    recombine = rates[4] * (interstitial * vacancy - 1.0)
    source = jnp.stack(
        [
            dopant - forming_ai - forming_av,
            interstitial - forming_ai - recombine,
            vacancy - forming_av - recombine,
            pair_inter + forming_ai,
            pair_vacancy + forming_av,
        ],
        axis=0,
    )
    diagonal = 1.0 + 6.0 * spread
    iterate = current
    for repeat in range(SWEEPS):
        iterate = (source + spread * neighbour_sum(iterate, ghosts)) / diagonal
    return iterate


def smooth_all(current, ghosts, mobility, fermi_gain, rates):

    def per_patch(paired):
        return smooth_plain(paired[0], paired[1], mobility, fermi_gain, rates)

    return lax.map(per_patch, (current, ghosts))


def gather_ghosts(face_table, neighbours, column_index, row_index, rows_count, capacity):
    face_rows = face_table.reshape(9 * capacity * 6, SPECIES, B, B)
    safe_slot = jnp.maximum(neighbours, 0)
    source_device = safe_slot // capacity
    step_x = source_device // rows_count - column_index + 1
    step_y = source_device % rows_count - row_index + 1
    opposite = jnp.array(OPPOSITE, jnp.int32)
    face_ids = jnp.arange(6, dtype=jnp.int32)
    remote = ((step_x * 3 + step_y) * capacity + safe_slot % capacity) * 6 + opposite[None, :]
    local = (4 * capacity + jnp.arange(capacity, dtype=jnp.int32)[:, None]) * 6 + face_ids[None, :]
    picked = jnp.clip(jnp.where(neighbours >= 0, remote, local), 0, 9 * capacity * 6 - 1)
    one = functools.partial(lax.dynamic_index_in_dim, face_rows, axis=0, keepdims=False)
    ghosts = lax.map(one, picked.reshape(-1))
    return ghosts.reshape(picked.shape + face_rows.shape[1:])


def counted(hits):
    places = jnp.arange(hits.shape[0])
    before = places[None, :] <= places[:, None]
    return jnp.sum(jnp.where(before & hits[None, :], 1, 0), axis=1) - 1


def pick_rows(pulls, this_device, capacity, payload):
    wanted = (pulls >= 0) & (pulls // capacity == this_device)
    position = counted(wanted)
    chosen = wanted[None, :] & (position[None, :] == jnp.arange(MOVE, dtype=jnp.int32)[:, None])
    slot_list = jnp.sum(jnp.where(chosen, pulls % capacity, 0), axis=1)
    return payload[slot_list]


def place_rows(index, source_device, sender, start):
    from_sender = (source_device == sender) & (source_device >= 0)
    position = counted(from_sender)
    return jnp.where(from_sender, start + position, index)


def relocate(payload, source_slot, requests, this_device, rows_count, capacity):
    source_device = jnp.where(source_slot >= 0, source_slot // capacity, -1)
    index = jnp.where(
        (source_slot >= 0) & (source_device == this_device), source_slot % capacity, -1
    )
    pieces = [payload]
    start = capacity
    for offset in (1, -1):
        outgoing = pick_rows(requests[1 + offset, 1], this_device, capacity, payload)
        arrived = passed_along(outgoing, "gx", offset)
        index = place_rows(index, source_device, this_device - offset * rows_count, start)
        pieces.append(arrived)
        start = start + MOVE
    for offset in (1, -1):
        outgoing = pick_rows(requests[1, 1 + offset], this_device, capacity, payload)
        arrived = passed_along(outgoing, "gy", offset)
        index = place_rows(index, source_device, this_device - offset, start)
        pieces.append(arrived)
        start = start + MOVE
    candidates = jnp.concatenate(pieces, axis=0)
    gathered = candidates[jnp.maximum(index, 0)]
    return jnp.where((index >= 0)[:, None], gathered, jnp.zeros_like(gathered))


def general(concentration, neighbours, source_slot, mobility, fermi_gain, rates):
    capacity = concentration.shape[0]
    cells = concentration.shape[2]
    column_index = lax.axis_index("gx")
    row_index = lax.axis_index("gy")
    rows_count = lax.axis_size("gy")
    this_device = column_index * rows_count + row_index
    blocks = concentration.reshape(capacity, SPECIES, B, B, B)
    own_faces = faces_of(blocks).reshape(1, 1, capacity, 6, SPECIES, B * B)
    face_table = with_halo(own_faces, (("gx", 0), ("gy", 1)), 1)
    requests = with_halo(source_slot.reshape(1, 1, capacity), (("gx", 0), ("gy", 1)), 1)
    ghosts = gather_ghosts(face_table, neighbours, column_index, row_index, rows_count, capacity)
    working = KEEP - 1 + MOVE
    payload = jnp.concatenate(
        [
            concentration.reshape(capacity, SPECIES * cells),
            ghosts.reshape(capacity, 6 * SPECIES * B * B),
        ],
        axis=1,
    )
    arrived = relocate(payload, source_slot, requests, this_device, rows_count, capacity)[:working]
    current = arrived[:, : SPECIES * cells].reshape(working, SPECIES, B, B, B)
    layers = arrived[:, SPECIES * cells :].reshape(working, 6, SPECIES, B, B)
    swept = smooth_all(current, layers, mobility, fermi_gain, rates).reshape(
        working, SPECIES, cells
    )
    live_rows = (source_slot[:working] >= 0)[:, None, None]
    swept = jnp.where(live_rows, swept, jnp.zeros_like(swept))
    return jnp.concatenate(
        [swept, jnp.zeros((capacity - working, SPECIES, cells), jnp.float32)], axis=0
    )


def body(nx, ny, concentration, neighbours, source_slot, mobility, fermi_gain, rates):
    source = source_slot.reshape(1, CAP)
    conc = concentration.transpose(1, 0, 2)
    landp, landz, landq, landg, swept, flag = exchange(nx, ny, conc, neighbours, source, mobility, fermi_gain, rates)

    def common():
        return smooth(nx, ny, landp, landz, landq, landg, swept, source, mobility, fermi_gain, rates).transpose(1, 0, 2)

    def crowded():
        return general(concentration, neighbours, source_slot, mobility, fermi_gain, rates)

    return lax.cond(flag[0, 0] == 0, common, crowded)


def solution(mesh):
    placed = (P(("gx", "gy"), None, None), P(("gx", "gy"), None), P(("gx", "gy")), P(), P(), P())
    return jax.shard_map(
        functools.partial(body, mesh.shape["gx"], mesh.shape["gy"]),
        mesh=mesh, in_specs=placed, out_specs=P(("gx", "gy"), None, None), check_vma=False,
    )
```

```python
import functools

import jax
import jax.numpy as jnp
from jax import lax
from jax.experimental import pallas as pl
from jax.experimental.pallas import tpu as pltpu
from jax.sharding import PartitionSpec as P

B = 32
SPECIES = 5
SWEEPS = 3
KEEP = 2
MOVE = 1
CAP = 6
ROWS = 256
EARLY = 12
ROOM = 6
MESH = pl.DeviceIdType.MESH

NEAR = ((-1, 0), (1, 0), (0, -1), (0, 1))
FAR = ((-2, 0), (2, 0), (0, -2), (0, 2), (-1, -1), (-1, 1), (1, -1), (1, 1))
AROUND = NEAR + FAR
ORDER = (2, 3, 0, 1)
HALF = ROWS // 2
PLACE = {(0, 0): 0, **{step: i + 1 for i, step in enumerate(AROUND)}}


def iota(shape, dim):
    return lax.broadcasted_iota(jnp.int32, shape, dim)


def prepare_patch(mobility, fermi_gain, rates, cell, coef, base):
    scale = [mobility[s] / jnp.full((8, 128), 1.0 + fermi_gain[s]) for s in range(SPECIES)]

    def planes(xo, carry):
        for xi in range(8):
            plane = pl.ds(pl.multiple_of(xo * 64 + xi * 8, 8), 8)
            a, i, v, p, q = [cell(s, plane) for s in range(SPECIES)]
            half = 0.5 * (a + p + q)
            square = half * half + 1.0
            electrons = half + square * lax.rsqrt(square)
            ai = rates[0] * a * i - rates[1] * p
            av = rates[2] * a * v - rates[3] * q
            re = rates[4] * (i * v - 1.0)
            sources = (a - ai - av, i - ai - re, v - av - re, p + ai, q + av)
            for s in range(SPECIES):
                spread = scale[s] * (1.0 + fermi_gain[s] * electrons)
                diagonal = 1.0 + 6.0 * spread
                inverse = pl.reciprocal(diagonal, approx=True)
                inverse = inverse * (2.0 - diagonal * inverse)
                coef[s, plane, :] = spread * inverse
                base[s, plane, :] = sources[s] * inverse
        return carry

    lax.fori_loop(0, 4, planes, 0)


def sweep_patch(cell, layer, coef, base, ping, result, finish):
    lane = iota((8, 128), 1)
    sub = iota((8, 128), 0)
    z = lane % 32
    first_y = (sub == 0) & (lane < 32)
    last_y = (sub == 7) & (lane >= 96)
    whole = pl.ds(0, 8)

    def ghosts(s):
        for x in range(B):
            plane = pl.ds(8 * x, 8)
            low = pltpu.roll(layer(4, s, whole), (128 - x) % 128, 1) if x else layer(4, s, whole)
            high = pltpu.roll(layer(5, s, whole), 31 - x, 1) if x < 31 else layer(5, s, whole)
            extra = jnp.where(z == 0, low, jnp.where(z == 31, high, 0.0))
            low = jnp.broadcast_to(layer(2, s, pl.ds(x % 8, 1)), (8, 128))
            high = jnp.broadcast_to(layer(3, s, pl.ds(x % 8, 1)), (8, 128))
            xo = x // 8
            low = pltpu.roll(low, 128 - 32 * xo, 1) if xo else low
            high = pltpu.roll(high, 96 - 32 * xo, 1) if xo < 3 else high
            extra = extra + jnp.where(first_y, low, jnp.where(last_y, high, 0.0))
            if x == 0:
                extra = extra + layer(0, s, whole)
            if x == B - 1:
                extra = extra + layer(1, s, whole)
            base[s, plane, :] = base[s, plane, :] + coef[s, plane, :] * extra

    def species(s, carry):
        def sweep(get, put):
            before = None
            here = get(0)
            for x in range(B):
                after = get(x + 1) if x + 1 < B else None
                total = jnp.where(z == 0, 0.0, pltpu.roll(here, 1, 1)) + jnp.where(z == 31, 0.0, pltpu.roll(here, 127, 1))
                down = pltpu.roll(here, 32, 1)
                down = jnp.where(lane >= 32, down, pltpu.roll(down, 1, 0))
                up = pltpu.roll(here, 96, 1)
                up = jnp.where(lane < 96, up, pltpu.roll(up, 7, 0))
                total = total + jnp.where(first_y, 0.0, down) + jnp.where(last_y, 0.0, up)
                if before is not None:
                    total = total + before
                if after is not None:
                    total = total + after
                put(x, base[s, 8 * x:8 * x + 8, :] + coef[s, 8 * x:8 * x + 8, :] * total)
                before, here = here, after

        def put_ping(x, value):
            ping[8 * x:8 * x + 8, :] = value

        def put_result(x, value):
            result[s, 8 * x:8 * x + 8, :] = value

        ghosts(s)
        sweep(lambda x: cell(s, pl.ds(8 * x, 8)), put_result)
        sweep(lambda x: result[s, 8 * x:8 * x + 8, :], put_ping)
        sweep(lambda x: ping[8 * x:8 * x + 8, :], put_result)
        finish(s)
        return carry

    lax.fori_loop(0, SPECIES, species, 0)


def exchange_kernel(
    nx, ny,
    conc, nbr_s, src_s, mobility, fermi_gain, rates, nbr_v, src_v,
    landp, landz, landq, landg, swept, flag_out,
    raw, dense, own_faces, meta, table, table_s, sendp, sendq, heldq, sendz, sendf, landf, sendg, flags, ghost, coef, base, ping, result,
    in_sem, meta_ss, meta_rs, tab_sem, p_ss, p_rs, q_ss, q_rs, z_ss, z_rs, h_ss, h_rs, f_ss, f_rs, g_ss, g_rs, fl_ss, fl_rs, out_sem,
):
    gx, gy = lax.axis_index("gx"), lax.axis_index("gy")
    me = gx * ny + gy

    def inside(step):
        x, y = gx + step[0], gy + step[1]
        return (x >= 0) & (x < nx) & (y >= 0) & (y < ny)

    def at(step):
        return (gx + step[0], gy + step[1])

    load = pltpu.make_async_copy(conc, raw, in_sem)
    load.start()

    row, col = gy // 4, gy % 4
    ring = (
        [(gx, row * 4 + (col + k) % 4) for k in range(1, 4)],
        [((gx + k) % nx, gy) for k in range(1, nx)],
        [(gx, ((row + k) % 4) * 4 + col) for k in range(1, 4)],
    )

    meta[...] = jnp.full(meta.shape, -1, jnp.int32)
    meta[0, 0:CAP, 0:6] = nbr_v[...]
    meta[0, CAP:CAP + 1, 0:CAP] = src_v[...]

    barrier = pltpu.get_barrier_semaphore()
    expected = nx - 1 + 6
    for step in AROUND:
        there = inside(step)
        expected = expected + there.astype(jnp.int32)

        @pl.when(there)
        def _():
            pl.semaphore_signal(barrier, inc=1, device_id=at(step), device_id_type=MESH)
    for group in ring:
        for target in group:
            pl.semaphore_signal(barrier, inc=1, device_id=target, device_id_type=MESH)
    load.wait()

    def spread_out(k, carry):
        s, x = k // B, k % B
        planes = raw[s, :, pl.ds(pl.multiple_of(x * 1024, 1024), 1024)].reshape(CAP, 8, 128)
        for q in range(CAP):
            dense[q, s, pl.ds(pl.multiple_of(x * 8, 8), 8), :] = planes[q]
        return carry

    lax.fori_loop(0, SPECIES * B, spread_out, 0)

    lane8 = iota((8, 128), 1)

    def faces(k, carry):
        q, s = k // SPECIES, k % SPECIES
        own_faces[q * 6 + 0, s] = dense[q, s, 0:8, :]
        own_faces[q * 6 + 1, s] = dense[q, s, ROWS - 8:ROWS, :]
        low = jnp.zeros((8, 128), jnp.float32)
        high = jnp.zeros((8, 128), jnp.float32)
        for b in range(4):
            first = dense[q, s, pl.ds(64 * b, 8, stride=8), :]
            final = dense[q, s, pl.ds(64 * b + 7, 8, stride=8), :]
            here = lane8 // 32 == b
            low = jnp.where(here, pltpu.roll(first, 32 * b, 1) if b else first, low)
            high = jnp.where(here, pltpu.roll(final, 32 * (b + 1), 1) if b < 3 else final, high)
        own_faces[q * 6 + 2, s] = low
        own_faces[q * 6 + 3, s] = high
        low = jnp.zeros((8, 128), jnp.float32)
        high = jnp.zeros((8, 128), jnp.float32)
        for x in range(B):
            turned = pltpu.roll(dense[q, s, 8 * x:8 * x + 8, :], x + 1, 1)
            high = jnp.where(lane8 % 32 == x, turned, high)
            low = jnp.where(lane8 % 32 == (x + 1) % 32, turned, low)
        own_faces[q * 6 + 4, s] = pltpu.roll(low, 127, 1)
        own_faces[q * 6 + 5, s] = pltpu.roll(high, 96, 1)
        return carry

    lax.fori_loop(0, EARLY, faces, 0)
    pl.semaphore_wait(barrier, expected)

    def opposite(i):
        return AROUND.index((-AROUND[i][0], -AROUND[i][1]))

    def meta_send(i):
        return pltpu.make_async_remote_copy(
            src_ref=meta.at[0], dst_ref=meta.at[1 + opposite(i)],
            send_sem=meta_ss.at[i], recv_sem=meta_rs.at[opposite(i)], device_id=at(AROUND[i]), device_id_type=MESH)

    for i, step in enumerate(AROUND):
        @pl.when(inside(step))
        def _():
            meta_send(i).start()

    lax.fori_loop(EARLY, CAP * SPECIES, faces, 0)

    for i, step in enumerate(AROUND):
        @pl.when(inside(step))
        def _():
            meta_send(i).wait_send()
            pltpu.make_async_remote_copy(
                src_ref=meta.at[0], dst_ref=meta.at[1 + i], send_sem=meta_ss.at[i], recv_sem=meta_rs.at[i],
                device_id=at(step), device_id_type=MESH).wait_recv()

    def device(step):
        return me + step[0] * ny + step[1]

    def sources(step):
        return meta[PLACE[step], CAP:CAP + 1, :]

    taken = []
    for d, step in enumerate(NEAR):
        rel = sources(step) - me * CAP
        slot = jnp.max(jnp.where((rel >= 0) & (rel < CAP), rel, -1))
        taken.append(slot)
    safe = [jnp.maximum(slot, 0) for slot in taken]
    asked = [slot >= 0 for slot in taken]

    def patch_send(d, s):
        return pltpu.make_async_remote_copy(
            src_ref=sendp.at[d, s], dst_ref=landp.at[d ^ 1, s], send_sem=p_ss.at[d, s], recv_sem=p_rs.at[d ^ 1, s],
            device_id=at(NEAR[d]), device_id_type=MESH)

    def patch_wait(d, s):
        return pltpu.make_async_remote_copy(
            src_ref=sendp.at[d, s], dst_ref=landp.at[d, s], send_sem=p_ss.at[d, s], recv_sem=p_rs.at[d, s],
            device_id=at(NEAR[d]), device_id_type=MESH)

    core = gx % 2
    twin = (gx + 1 - 2 * core, gy)
    mine_first, twin_first = core * HALF, (1 - core) * HALF

    def copy_along(src, dst, ss, rs, target):
        return pltpu.make_async_remote_copy(
            src_ref=src, dst_ref=dst, send_sem=ss, recv_sem=rs, device_id=target, device_id_type=MESH)

    def give(e, s):
        return copy_along(sendq.at[e, s], heldq.at[e, s], q_ss.at[e, s], q_rs.at[e, s], twin)

    def carry_send(e, s):
        return copy_along(sendz.at[e, s], landz.at[1 - e, s], z_ss.at[e, s], z_rs.at[1 - e, s], at(NEAR[2 + e]))

    def carry_wait(e, s):
        return copy_along(sendz.at[e, s], landz.at[e, s], z_ss.at[e, s], z_rs.at[e, s], at(NEAR[2 + e]))

    def hand(e, s):
        return copy_along(landz.at[e, s], landq.at[e, s], h_ss.at[e, s], h_rs.at[e, s], twin)

    for s in range(SPECIES):
        for e in range(2):
            @pl.when(inside(NEAR[2 + e]))
            def _():
                sendq[e, s] = dense[safe[2 + e], s, pl.ds(pl.multiple_of(twin_first, HALF), HALF), :]
                give(e, s).start()

    def straight():
        for d in range(2):
            @pl.when(inside(NEAR[d]))
            def _():
                for s in range(SPECIES):
                    sendp[d, s] = dense[safe[d], s]
                    patch_send(d, s).start()


    def face_send(d):
        return pltpu.make_async_remote_copy(
            src_ref=sendf.at[d], dst_ref=landf.at[d ^ 1], send_sem=f_ss.at[d], recv_sem=f_rs.at[d ^ 1],
            device_id=at(NEAR[d]), device_id_type=MESH)

    def face_wait(d):
        return pltpu.make_async_remote_copy(
            src_ref=sendf.at[d], dst_ref=landf.at[d], send_sem=f_ss.at[d], recv_sem=f_rs.at[d],
            device_id=at(NEAR[d]), device_id_type=MESH)

    def ghost_send(d):
        return pltpu.make_async_remote_copy(
            src_ref=sendg.at[d], dst_ref=landg.at[d ^ 1], send_sem=g_ss.at[d], recv_sem=g_rs.at[d ^ 1],
            device_id=at(NEAR[d]), device_id_type=MESH)

    def ghost_wait(d):
        return pltpu.make_async_remote_copy(
            src_ref=sendg.at[d], dst_ref=landg.at[d], send_sem=g_ss.at[d], recv_sem=g_rs.at[d],
            device_id=at(NEAR[d]), device_id_type=MESH)

    side = iota((8, 128), 1)
    far_side = side + 1 - 2 * (side % 2)
    slot_row = iota((8, 128), 0)
    lane1 = iota((1, 128), 1)

    def named(step):
        owner = device(step)
        hit = jnp.zeros((8, 128), jnp.bool_)
        for extra in ((0, 0),) + NEAR:
            hit = hit | (sources((step[0] + extra[0], step[1] + extra[1])) == owner * CAP + slot_row)
        return jnp.max(hit.astype(jnp.int32), axis=1, keepdims=True) > 0

    def wanted(step, of, names):
        rel = meta[PLACE[step]] - device(of) * CAP
        good = names & (rel >= 0) & (rel < CAP) & (slot_row < CAP) & (side < 6)
        code = jnp.where(good, rel * 6 + far_side, 127)
        hit = jnp.zeros((8, 128), jnp.bool_)
        for f in range(6):
            hit = hit | (code[:, f:f + 1] == side)
        mask = jnp.max(hit.astype(jnp.int32), axis=0, keepdims=True)
        mask = jnp.where(lane1 < 36, mask, 0)
        total = mask
        for k in (1, 2, 4, 8, 16, 32):
            total = total + jnp.where(lane1 >= k, pltpu.roll(total, k, 1), 0)
        return mask, total - mask

    mine = named((0, 0))
    over = jnp.zeros((8, 128), jnp.int32)
    for d, step in enumerate(NEAR):
        mask, rank = wanted(step, (0, 0), named(step))
        over = jnp.maximum(over, jnp.where((mask > 0) & (rank >= ROOM), 1, 0))
        chosen = jnp.where((mask > 0) & (rank == slot_row), side, 0)
        table[d] = jnp.broadcast_to(jnp.max(chosen, axis=1, keepdims=True), (8, 128))
        _, rank = wanted((0, 0), step, mine)
        table[4, d:d + 1, :] = rank
    over = jnp.broadcast_to(jnp.max(jnp.max(over, axis=1, keepdims=True), axis=0, keepdims=True), (8, 128))
    twin_base = (me + (1 - 2 * core) * ny) * CAP
    for e, dy in enumerate((-1, 1)):
        rel = sources((0, dy)) - me * CAP
        other = jnp.where(core == 0, sources((1, dy)), sources((-1, dy))) - twin_base
        both = jnp.where((rel >= 0) & (rel < CAP), 1, 0) * jnp.max(
            jnp.where((other >= 0) & (other < CAP), 1, 0), axis=1, keepdims=True)
        over = jnp.maximum(over, jnp.max(both, axis=1, keepdims=True))
    flags[0] = over
    to_scalars = pltpu.make_async_copy(table, table_s, tab_sem)
    to_scalars.start()

    def flag_copy(base, k, target, held):
        return pltpu.make_async_remote_copy(
            src_ref=flags.at[held], dst_ref=flags.at[base + k], send_sem=fl_ss.at[base + k],
            recv_sem=fl_rs.at[base + k], device_id=target, device_id_type=MESH)

    bases = (3, 6, 6 + nx - 1)

    for k, target in enumerate(ring[0]):
        flag_copy(bases[0], k, target, 0).start()

    to_scalars.wait()
    for d in ORDER:
        @pl.when(inside(NEAR[d]))
        def _():
            def stage(p, carry):
                sendf[d, p] = own_faces[table_s[d, p, 0]]
                return carry
            lax.fori_loop(0, ROOM, stage, 0)
            face_send(d).start()

    def flag_round(n, held, following):
        for k, target in enumerate(ring[n]):
            copy = flag_copy(bases[n], k, target, held)
            copy.wait()
        total = flags[held]
        for k in range(len(ring[n])):
            total = jnp.maximum(total, flags[bases[n] + k])
        if following is None:
            flag_out[...] = total
        else:
            flags[following] = total
            for k, target in enumerate(ring[n + 1]):
                flag_copy(bases[n + 1], k, target, following).start()

    kept = []
    for t in range(KEEP):
        rel = src_s[0, t] - me * CAP
        kept.append(jnp.where((rel >= 0) & (rel < CAP), rel, 0))

    def ready(t):
        slot = kept[t]
        prepare_patch(
            mobility, fermi_gain, rates, lambda s, rows: dense[slot, s, rows, :], coef.at[t], base.at[t])
    ready(0)
    for s in range(SPECIES):
        for e in range(2):
            @pl.when(inside(NEAR[2 + e]))
            def _():
                give(e, s).wait_recv()
                own = dense[safe[2 + e], s, pl.ds(pl.multiple_of(mine_first, HALF), HALF), :]
                sendz[e, s] = jnp.where(asked[2 + e], own, heldq[e, s])
                carry_send(e, s).start()
    flag_round(0, 0, 1)
    straight()
    ready(1)

    for d, step in enumerate(NEAR):
        @pl.when(inside(step))
        def _():
            face_wait(d).wait_recv()

    def ghost_place(slot, f):
        nb = nbr_s[slot, f]
        rel = nb - me * CAP
        here = (rel >= 0) & (rel < CAP)
        opposite_f = f + 1 - 2 * (f % 2)
        own = jnp.where(here, rel * 6 + opposite_f, slot * 6 + f)
        own = jnp.where((nb < 0) | here, own, 0)
        away = jnp.int32(-1)
        for d, step in enumerate(NEAR):
            rel = nb - device(step) * CAP
            there = (nb >= 0) & (rel >= 0) & (rel < CAP)
            code = jnp.where(there, rel * 6 + opposite_f, 0)
            away = jnp.where(there, d * ROOM + jnp.minimum(table_s[4, d, code], ROOM - 1), away)
        return own, away

    def ghost_value(slot, f):
        own, away = ghost_place(slot, f)
        other = jnp.maximum(away, 0)
        return jnp.where(away >= 0, landf[other // ROOM, other % ROOM], own_faces[own])

    for d, step in enumerate(NEAR):
        @pl.when(inside(step))
        def _():
            def stage(f, carry):
                sendg[d, f] = ghost_value(safe[d], f)
                return carry
            lax.fori_loop(0, 6, stage, 0)
            ghost_send(d).start()

    flag_round(1, 1, 2)

    def stay(t):
        slot = kept[t]

        def layer(f, carry):
            ghost[f] = ghost_value(slot, f)
            return carry
        lax.fori_loop(0, 6, layer, 0)
        sweep_patch(
            lambda s, rows: dense[slot, s, rows, :], lambda f, s, rows: ghost[f, s, rows, :],
            coef.at[t], base.at[t], ping, result.at[t], lambda s: None)
        pltpu.make_async_copy(result.at[t], swept.at[t], out_sem.at[t]).start()

    stay(0)
    flag_round(2, 2, None)
    stay(1)
    for s in range(SPECIES):
        for e in range(2):
            @pl.when(inside(NEAR[2 + e]))
            def _():
                carry_wait(e, s).wait_recv()
                hand(e, s).start()

    for d, step in enumerate(NEAR):
        @pl.when(inside(step))
        def _():
            face_send(d).wait_send()
            ghost_send(d).wait_send()
            for s in range(SPECIES):
                if d < 2:
                    patch_send(d, s).wait_send()
                    patch_wait(d, s).wait_recv()
                else:
                    give(d - 2, s).wait_send()
                    carry_send(d - 2, s).wait_send()
                    hand(d - 2, s).wait()
            ghost_wait(d).wait_recv()
    for t in range(KEEP):
        pltpu.make_async_copy(result.at[t], swept.at[t], out_sem.at[t]).wait()


def smooth_kernel(
    nx, ny,
    src_s, mobility, fermi_gain, rates, landp, landz, landq, landg, swept,
    out,
    cur, ghost, coef, base, ping, pong, blank, cur_sem, half_sem, ghost_sem, out_sem, zero_sem,
):
    gx, gy = lax.axis_index("gx"), lax.axis_index("gy")
    me = gx * ny + gy
    whence = []
    for t in range(KEEP):
        source = src_s[0, t]
        rel = source - me * CAP
        own = (rel >= 0) & (rel < CAP)
        came = jnp.int32(0)
        for d, step in enumerate(NEAR):
            away = source - (me + step[0] * ny + step[1]) * CAP
            came = jnp.where((away >= 0) & (away < CAP), d, came)
        whence.append((source, own, jnp.where(own, rel, 0), came))

    def fetch_own(t):
        return (pltpu.make_async_copy(swept.at[t], pong.at[t], cur_sem.at[t]),)

    core = gx % 2

    def fetch_moved(t):
        came = whence[t][3]
        e = jnp.maximum(came - 2, 0)
        straight = (
            pltpu.make_async_copy(landp.at[jnp.minimum(came, 1)], cur.at[t], cur_sem.at[t]),
        )
        halves = (
            pltpu.make_async_copy(landz.at[e], cur.at[t, :, pl.ds(pl.multiple_of(core * HALF, HALF), HALF), :], cur_sem.at[t]),
            pltpu.make_async_copy(landq.at[e], cur.at[t, :, pl.ds(pl.multiple_of((1 - core) * HALF, HALF), HALF), :], half_sem.at[t]),
        )
        layers = pltpu.make_async_copy(landg.at[came], ghost.at[t], ghost_sem.at[t])
        return straight, halves, layers

    def start_moved(t):
        straight, halves, layers = fetch_moved(t)
        layers.start()

        @pl.when(whence[t][3] < 2)
        def _():
            straight[0].start()

        @pl.when(whence[t][3] >= 2)
        def _():
            halves[0].start()
            halves[1].start()

    def wait_moved(t):
        straight, halves, layers = fetch_moved(t)
        layers.wait()

        @pl.when(whence[t][3] < 2)
        def _():
            straight[0].wait()

        @pl.when(whence[t][3] >= 2)
        def _():
            halves[0].wait()
            halves[1].wait()

    for t in range(KEEP):
        source, own, slot, came = whence[t]

        @pl.when((source >= 0) & own)
        def _():
            for copy in fetch_own(t):
                copy.start()

        @pl.when((source >= 0) & jnp.logical_not(own))
        def _():
            start_moved(t)

    blank[...] = jnp.zeros(blank.shape, jnp.float32)
    zeros = [
        pltpu.make_async_copy(blank, out.at[pl.ds(s, 1), pl.ds(KEEP, CAP - KEEP), :], zero_sem.at[s])
        for s in range(SPECIES)
    ]
    for copy in zeros:
        copy.start()
    def put_out(t, s):
        return pltpu.make_async_copy(
            pong.at[t, pl.ds(s, 1)].reshape(1, 1, B**3), out.at[pl.ds(s, 1), pl.ds(t, 1), :], out_sem.at[t, s])

    for t in range(KEEP):
        source, own, slot, came = whence[t]

        @pl.when(source < 0)
        def _():
            pong[t] = jnp.zeros((SPECIES, ROWS, 128), jnp.float32)
            for s in range(SPECIES):
                put_out(t, s).start()

        @pl.when((source >= 0) & own)
        def _():
            for copy in fetch_own(t):
                copy.wait()
            for s in range(SPECIES):
                put_out(t, s).start()

    for t in range(KEEP):
        source, own, slot, came = whence[t]

        @pl.when((source >= 0) & jnp.logical_not(own))
        def _():
            wait_moved(t)
            prepare_patch(mobility, fermi_gain, rates, lambda s, rows: cur[t, s, rows, :], coef, base)
            sweep_patch(
                lambda s, rows: cur[t, s, rows, :], lambda f, s, rows: ghost[t, f, s, rows, :], coef, base, ping, pong.at[t],
                lambda s: put_out(t, s).start())

    for copy in zeros:
        copy.wait()
    for t in range(KEEP):
        for s in range(SPECIES):
            put_out(t, s).wait()


def in_vmem():
    return pl.BlockSpec(memory_space=pltpu.VMEM)


def in_smem():
    return pl.BlockSpec(memory_space=pltpu.SMEM)


def anywhere():
    return pl.BlockSpec(memory_space=pl.ANY)


def exchange(nx, ny, conc, neighbours, source, mobility, fermi_gain, rates):
    f32, i32 = jnp.float32, jnp.int32
    dma = pltpu.SemaphoreType.DMA
    n_flags = 3 + nx - 1 + 6
    return pl.pallas_call(
        functools.partial(exchange_kernel, nx, ny),
        out_shape=(
            jax.ShapeDtypeStruct((2, SPECIES, ROWS, 128), f32),
            jax.ShapeDtypeStruct((2, SPECIES, HALF, 128), f32),
            jax.ShapeDtypeStruct((2, SPECIES, HALF, 128), f32),
            jax.ShapeDtypeStruct((4, 6, SPECIES, 8, 128), f32),
            jax.ShapeDtypeStruct((KEEP, SPECIES, ROWS, 128), f32),
            jax.ShapeDtypeStruct((8, 128), i32),
        ),
        in_specs=[anywhere()] + [in_smem()] * 5 + [in_vmem()] * 2,
        out_specs=(anywhere(),) * 5 + (in_vmem(),),
        scratch_shapes=[
            pltpu.VMEM((SPECIES, CAP, B**3), f32),
            pltpu.VMEM((CAP, SPECIES, ROWS, 128), f32),
            pltpu.VMEM((CAP * 6, SPECIES, 8, 128), f32),
            pltpu.VMEM((13, 8, 128), i32),
            pltpu.VMEM((5, 8, 128), i32),
            pltpu.SMEM((5, 8, 128), i32),
            pltpu.VMEM((2, SPECIES, ROWS, 128), f32),
            pltpu.VMEM((2, SPECIES, HALF, 128), f32),
            pltpu.VMEM((2, SPECIES, HALF, 128), f32),
            pltpu.VMEM((2, SPECIES, HALF, 128), f32),
            pltpu.VMEM((4, ROOM, SPECIES, 8, 128), f32),
            pltpu.VMEM((4, ROOM, SPECIES, 8, 128), f32),
            pltpu.VMEM((4, 6, SPECIES, 8, 128), f32),
            pltpu.VMEM((n_flags, 8, 128), i32),
            pltpu.VMEM((6, SPECIES, 8, 128), f32),
            pltpu.VMEM((KEEP, SPECIES, ROWS, 128), f32),
            pltpu.VMEM((KEEP, SPECIES, ROWS, 128), f32),
            pltpu.VMEM((ROWS, 128), f32),
            pltpu.VMEM((KEEP, SPECIES, ROWS, 128), f32),
            dma,
            dma((12,)), dma((12,)),
            dma,
            dma((2, SPECIES)), dma((2, SPECIES)), dma((2, SPECIES)), dma((2, SPECIES)),
            dma((2, SPECIES)), dma((2, SPECIES)), dma((2, SPECIES)), dma((2, SPECIES)), dma((4,)), dma((4,)), dma((4,)), dma((4,)),
            dma((n_flags,)), dma((n_flags,)),
            dma((KEEP,)),
        ],
        compiler_params=pltpu.CompilerParams(collective_id=0, has_side_effects=True, vmem_limit_bytes=40 * 2**20),
    )(conc, neighbours, source, mobility, fermi_gain, rates, neighbours, source)


def smooth(nx, ny, landp, landz, landq, landg, swept, source, mobility, fermi_gain, rates):
    f32 = jnp.float32
    dma = pltpu.SemaphoreType.DMA
    return pl.pallas_call(
        functools.partial(smooth_kernel, nx, ny),
        out_shape=jax.ShapeDtypeStruct((SPECIES, CAP, B**3), f32),
        in_specs=[in_smem()] * 4 + [anywhere()] * 5,
        out_specs=anywhere(),
        scratch_shapes=[
            pltpu.VMEM((KEEP, SPECIES, ROWS, 128), f32),
            pltpu.VMEM((KEEP, 6, SPECIES, 8, 128), f32),
            pltpu.VMEM((SPECIES, ROWS, 128), f32),
            pltpu.VMEM((SPECIES, ROWS, 128), f32),
            pltpu.VMEM((ROWS, 128), f32),
            pltpu.VMEM((KEEP, SPECIES, ROWS, 128), f32),
            pltpu.VMEM((1, CAP - KEEP, B**3), f32),
            dma((KEEP,)),
            dma((KEEP,)),
            dma((KEEP,)),
            dma((KEEP, SPECIES)),
            dma((SPECIES,)),
        ],
        compiler_params=pltpu.CompilerParams(vmem_limit_bytes=60 * 2**20),
    )(source, mobility, fermi_gain, rates, landp, landz, landq, landg, swept)


OPPOSITE = (1, 0, 3, 2, 5, 4)


def passed_along(x, axis, by):
    devices = lax.axis_size(axis)
    pairs = [(i, i + by) for i in range(devices) if 0 <= i + by < devices]
    return lax.ppermute(x, axis, pairs)


def with_halo(x, sides, width):
    edges = {}
    for axis, dim in sides:
        devices, length = (lax.axis_size(axis), x.shape[dim])
        up = [(i, (i + 1) % devices) for i in range(devices - 1)]
        last = lax.slice_in_dim(x, length - width, length, axis=dim)
        leading = lax.slice_in_dim(x, 0, width, axis=dim)
        edges[dim] = (
            lax.ppermute(last, axis, up),
            lax.ppermute(leading, axis, [(b, a) for a, b in up]),
        )
    done = []
    for _, dim in sides:
        low, high = edges[dim]
        around = [(width, width) if d in done else (0, 0) for d in range(x.ndim)]
        x = jnp.concatenate([jnp.pad(low, around), x, jnp.pad(high, around)], axis=dim)
        done.append(dim)
    return x


def faces_of(blocks):
    last = blocks.shape[-1] - 1
    return jnp.stack(
        [
            blocks[..., 0, :, :],
            blocks[..., last, :, :],
            blocks[..., :, 0, :],
            blocks[..., :, last, :],
            blocks[..., :, :, 0],
            blocks[..., :, :, last],
        ],
        axis=-4,
    )


def neighbour_sum(iterate, ghosts):
    lower_x = jnp.concatenate([ghosts[0][:, None], iterate[:, :-1]], axis=1)
    upper_x = jnp.concatenate([iterate[:, 1:], ghosts[1][:, None]], axis=1)
    lower_y = jnp.concatenate([ghosts[2][:, :, None], iterate[:, :, :-1]], axis=2)
    upper_y = jnp.concatenate([iterate[:, :, 1:], ghosts[3][:, :, None]], axis=2)
    lower_z = jnp.concatenate([ghosts[4][..., None], iterate[..., :-1]], axis=3)
    upper_z = jnp.concatenate([iterate[..., 1:], ghosts[5][..., None]], axis=3)
    return lower_x + upper_x + lower_y + upper_y + lower_z + upper_z


def smooth_plain(current, ghosts, mobility, fermi_gain, rates):
    dopant_sum = current[0] + current[3] + current[4]
    half_total = 0.5 * dopant_sum
    electrons = half_total + jnp.sqrt(half_total * half_total + 1.0)
    gain_column = fermi_gain[:, None, None, None]
    spread = (
        mobility[:, None, None, None] * (1.0 + gain_column * electrons[None]) / (1.0 + gain_column)
    )
    dopant, interstitial, vacancy, pair_inter, pair_vacancy = (
        current[0],
        current[1],
        current[2],
        current[3],
        current[4],
    )
    forming_ai = rates[0] * dopant * interstitial - rates[1] * pair_inter
    forming_av = rates[2] * dopant * vacancy - rates[3] * pair_vacancy
    recombine = rates[4] * (interstitial * vacancy - 1.0)
    source = jnp.stack(
        [
            dopant - forming_ai - forming_av,
            interstitial - forming_ai - recombine,
            vacancy - forming_av - recombine,
            pair_inter + forming_ai,
            pair_vacancy + forming_av,
        ],
        axis=0,
    )
    diagonal = 1.0 + 6.0 * spread
    iterate = current
    for repeat in range(SWEEPS):
        iterate = (source + spread * neighbour_sum(iterate, ghosts)) / diagonal
    return iterate


def smooth_all(current, ghosts, mobility, fermi_gain, rates):

    def per_patch(paired):
        return smooth_plain(paired[0], paired[1], mobility, fermi_gain, rates)

    return lax.map(per_patch, (current, ghosts))


def gather_ghosts(face_table, neighbours, column_index, row_index, rows_count, capacity):
    face_rows = face_table.reshape(9 * capacity * 6, SPECIES, B, B)
    safe_slot = jnp.maximum(neighbours, 0)
    source_device = safe_slot // capacity
    step_x = source_device // rows_count - column_index + 1
    step_y = source_device % rows_count - row_index + 1
    opposite = jnp.array(OPPOSITE, jnp.int32)
    face_ids = jnp.arange(6, dtype=jnp.int32)
    remote = ((step_x * 3 + step_y) * capacity + safe_slot % capacity) * 6 + opposite[None, :]
    local = (4 * capacity + jnp.arange(capacity, dtype=jnp.int32)[:, None]) * 6 + face_ids[None, :]
    picked = jnp.clip(jnp.where(neighbours >= 0, remote, local), 0, 9 * capacity * 6 - 1)
    one = functools.partial(lax.dynamic_index_in_dim, face_rows, axis=0, keepdims=False)
    ghosts = lax.map(one, picked.reshape(-1))
    return ghosts.reshape(picked.shape + face_rows.shape[1:])


def counted(hits):
    places = jnp.arange(hits.shape[0])
    before = places[None, :] <= places[:, None]
    return jnp.sum(jnp.where(before & hits[None, :], 1, 0), axis=1) - 1


def pick_rows(pulls, this_device, capacity, payload):
    wanted = (pulls >= 0) & (pulls // capacity == this_device)
    position = counted(wanted)
    chosen = wanted[None, :] & (position[None, :] == jnp.arange(MOVE, dtype=jnp.int32)[:, None])
    slot_list = jnp.sum(jnp.where(chosen, pulls % capacity, 0), axis=1)
    return payload[slot_list]


def place_rows(index, source_device, sender, start):
    from_sender = (source_device == sender) & (source_device >= 0)
    position = counted(from_sender)
    return jnp.where(from_sender, start + position, index)


def relocate(payload, source_slot, requests, this_device, rows_count, capacity):
    source_device = jnp.where(source_slot >= 0, source_slot // capacity, -1)
    index = jnp.where(
        (source_slot >= 0) & (source_device == this_device), source_slot % capacity, -1
    )
    pieces = [payload]
    start = capacity
    for offset in (1, -1):
        outgoing = pick_rows(requests[1 + offset, 1], this_device, capacity, payload)
        arrived = passed_along(outgoing, "gx", offset)
        index = place_rows(index, source_device, this_device - offset * rows_count, start)
        pieces.append(arrived)
        start = start + MOVE
    for offset in (1, -1):
        outgoing = pick_rows(requests[1, 1 + offset], this_device, capacity, payload)
        arrived = passed_along(outgoing, "gy", offset)
        index = place_rows(index, source_device, this_device - offset, start)
        pieces.append(arrived)
        start = start + MOVE
    candidates = jnp.concatenate(pieces, axis=0)
    gathered = candidates[jnp.maximum(index, 0)]
    return jnp.where((index >= 0)[:, None], gathered, jnp.zeros_like(gathered))


def general(concentration, neighbours, source_slot, mobility, fermi_gain, rates):
    capacity = concentration.shape[0]
    cells = concentration.shape[2]
    column_index = lax.axis_index("gx")
    row_index = lax.axis_index("gy")
    rows_count = lax.axis_size("gy")
    this_device = column_index * rows_count + row_index
    blocks = concentration.reshape(capacity, SPECIES, B, B, B)
    own_faces = faces_of(blocks).reshape(1, 1, capacity, 6, SPECIES, B * B)
    face_table = with_halo(own_faces, (("gx", 0), ("gy", 1)), 1)
    requests = with_halo(source_slot.reshape(1, 1, capacity), (("gx", 0), ("gy", 1)), 1)
    ghosts = gather_ghosts(face_table, neighbours, column_index, row_index, rows_count, capacity)
    working = KEEP - 1 + MOVE
    payload = jnp.concatenate(
        [
            concentration.reshape(capacity, SPECIES * cells),
            ghosts.reshape(capacity, 6 * SPECIES * B * B),
        ],
        axis=1,
    )
    arrived = relocate(payload, source_slot, requests, this_device, rows_count, capacity)[:working]
    current = arrived[:, : SPECIES * cells].reshape(working, SPECIES, B, B, B)
    layers = arrived[:, SPECIES * cells :].reshape(working, 6, SPECIES, B, B)
    swept = smooth_all(current, layers, mobility, fermi_gain, rates).reshape(
        working, SPECIES, cells
    )
    live_rows = (source_slot[:working] >= 0)[:, None, None]
    swept = jnp.where(live_rows, swept, jnp.zeros_like(swept))
    return jnp.concatenate(
        [swept, jnp.zeros((capacity - working, SPECIES, cells), jnp.float32)], axis=0
    )


def body(nx, ny, concentration, neighbours, source_slot, mobility, fermi_gain, rates):
    source = source_slot.reshape(1, CAP)
    conc = concentration.transpose(1, 0, 2)
    landp, landz, landq, landg, swept, flag = exchange(nx, ny, conc, neighbours, source, mobility, fermi_gain, rates)

    def common():
        return smooth(nx, ny, landp, landz, landq, landg, swept, source, mobility, fermi_gain, rates).transpose(1, 0, 2)

    def crowded():
        return general(concentration, neighbours, source_slot, mobility, fermi_gain, rates)

    return lax.cond(flag[0, 0] == 0, common, crowded)


def solution(mesh):
    placed = (P(("gx", "gy"), None, None), P(("gx", "gy"), None), P(("gx", "gy")), P(), P(), P())
    return jax.shard_map(
        functools.partial(body, mesh.shape["gx"], mesh.shape["gy"]),
        mesh=mesh, in_specs=placed, out_specs=P(("gx", "gy"), None, None), check_vma=False,
    )
```

```python
import functools

import jax
import jax.numpy as jnp
from jax import lax
from jax.experimental import pallas as pl
from jax.experimental.pallas import tpu as pltpu
from jax.sharding import PartitionSpec as P

B = 32
SPECIES = 5
SWEEPS = 3
KEEP = 2
MOVE = 1
CAP = 6
ROWS = 256
EARLY = 12
ROOM = 6
MESH = pl.DeviceIdType.MESH

NEAR = ((-1, 0), (1, 0), (0, -1), (0, 1))
FAR = ((-2, 0), (2, 0), (0, -2), (0, 2), (-1, -1), (-1, 1), (1, -1), (1, 1))
AROUND = NEAR + FAR
ORDER = (2, 3, 0, 1)
HALF = ROWS // 2
PLACE = {(0, 0): 0, **{step: i + 1 for i, step in enumerate(AROUND)}}


def iota(shape, dim):
    return lax.broadcasted_iota(jnp.int32, shape, dim)


def prepare_patch(mobility, fermi_gain, rates, cell, coef, base):
    scale = [mobility[s] / jnp.full((8, 128), 1.0 + fermi_gain[s]) for s in range(SPECIES)]

    def planes(xo, carry):
        for xi in range(8):
            plane = pl.ds(pl.multiple_of(xo * 64 + xi * 8, 8), 8)
            a, i, v, p, q = [cell(s, plane) for s in range(SPECIES)]
            half = 0.5 * (a + p + q)
            square = half * half + 1.0
            electrons = half + square * lax.rsqrt(square)
            ai = rates[0] * a * i - rates[1] * p
            av = rates[2] * a * v - rates[3] * q
            re = rates[4] * (i * v - 1.0)
            sources = (a - ai - av, i - ai - re, v - av - re, p + ai, q + av)
            for s in range(SPECIES):
                spread = scale[s] * (1.0 + fermi_gain[s] * electrons)
                diagonal = 1.0 + 6.0 * spread
                inverse = pl.reciprocal(diagonal, approx=True)
                inverse = inverse * (2.0 - diagonal * inverse)
                coef[s, plane, :] = spread * inverse
                base[s, plane, :] = sources[s] * inverse
        return carry

    lax.fori_loop(0, 4, planes, 0)


def sweep_patch(cell, layer, coef, base, ping, result, finish):
    lane = iota((8, 128), 1)
    sub = iota((8, 128), 0)
    z = lane % 32
    first_y = (sub == 0) & (lane < 32)
    last_y = (sub == 7) & (lane >= 96)
    whole = pl.ds(0, 8)

    def ghosts(s):
        for x in range(B):
            plane = pl.ds(8 * x, 8)
            low = pltpu.roll(layer(4, s, whole), (128 - x) % 128, 1) if x else layer(4, s, whole)
            high = pltpu.roll(layer(5, s, whole), 31 - x, 1) if x < 31 else layer(5, s, whole)
            extra = jnp.where(z == 0, low, jnp.where(z == 31, high, 0.0))
            low = jnp.broadcast_to(layer(2, s, pl.ds(x % 8, 1)), (8, 128))
            high = jnp.broadcast_to(layer(3, s, pl.ds(x % 8, 1)), (8, 128))
            xo = x // 8
            low = pltpu.roll(low, 128 - 32 * xo, 1) if xo else low
            high = pltpu.roll(high, 96 - 32 * xo, 1) if xo < 3 else high
            extra = extra + jnp.where(first_y, low, jnp.where(last_y, high, 0.0))
            if x == 0:
                extra = extra + layer(0, s, whole)
            if x == B - 1:
                extra = extra + layer(1, s, whole)
            base[s, plane, :] = base[s, plane, :] + coef[s, plane, :] * extra

    def species(s, carry):
        def sweep(get, put):
            before = None
            here = get(0)
            for x in range(B):
                after = get(x + 1) if x + 1 < B else None
                total = jnp.where(z == 0, 0.0, pltpu.roll(here, 1, 1)) + jnp.where(z == 31, 0.0, pltpu.roll(here, 127, 1))
                down = pltpu.roll(here, 32, 1)
                down = jnp.where(lane >= 32, down, pltpu.roll(down, 1, 0))
                up = pltpu.roll(here, 96, 1)
                up = jnp.where(lane < 96, up, pltpu.roll(up, 7, 0))
                total = total + jnp.where(first_y, 0.0, down) + jnp.where(last_y, 0.0, up)
                if before is not None:
                    total = total + before
                if after is not None:
                    total = total + after
                put(x, base[s, 8 * x:8 * x + 8, :] + coef[s, 8 * x:8 * x + 8, :] * total)
                before, here = here, after

        def put_ping(x, value):
            ping[8 * x:8 * x + 8, :] = value

        def put_result(x, value):
            result[s, 8 * x:8 * x + 8, :] = value

        ghosts(s)
        sweep(lambda x: cell(s, pl.ds(8 * x, 8)), put_result)
        sweep(lambda x: result[s, 8 * x:8 * x + 8, :], put_ping)
        sweep(lambda x: ping[8 * x:8 * x + 8, :], put_result)
        finish(s)
        return carry

    lax.fori_loop(0, SPECIES, species, 0)


def exchange_kernel(
    nx, ny,
    conc, nbr_s, src_s, mobility, fermi_gain, rates, nbr_v, src_v,
    landp, landz, landq, landg, swept, flag_out,
    raw, dense, own_faces, meta, table, table_s, sendp, sendq, heldq, sendz, sendf, landf, sendg, flags, ghost, coef, base, ping, result,
    in_sem, meta_ss, meta_rs, tab_sem, p_ss, p_rs, q_ss, q_rs, z_ss, z_rs, h_ss, h_rs, f_ss, f_rs, g_ss, g_rs, fl_ss, fl_rs, out_sem,
):
    gx, gy = lax.axis_index("gx"), lax.axis_index("gy")
    me = gx * ny + gy

    def inside(step):
        x, y = gx + step[0], gy + step[1]
        return (x >= 0) & (x < nx) & (y >= 0) & (y < ny)

    def at(step):
        return (gx + step[0], gy + step[1])

    load = pltpu.make_async_copy(conc, raw, in_sem)
    load.start()

    row, col = gy // 4, gy % 4
    ring = (
        [(gx, row * 4 + (col + k) % 4) for k in range(1, 4)],
        [(gx, ((row + k) % 4) * 4 + col) for k in range(1, 4)],
        [((gx + k) % nx, gy) for k in range(1, nx)],
    )

    meta[...] = jnp.full(meta.shape, -1, jnp.int32)
    meta[0, 0:CAP, 0:6] = nbr_v[...]
    meta[0, CAP:CAP + 1, 0:CAP] = src_v[...]

    barrier = pltpu.get_barrier_semaphore()
    expected = nx - 1 + 6
    for step in AROUND:
        there = inside(step)
        expected = expected + there.astype(jnp.int32)

        @pl.when(there)
        def _():
            pl.semaphore_signal(barrier, inc=1, device_id=at(step), device_id_type=MESH)
    for group in ring:
        for target in group:
            pl.semaphore_signal(barrier, inc=1, device_id=target, device_id_type=MESH)
    load.wait()

    def spread_out(k, carry):
        s, x = k // B, k % B
        planes = raw[s, :, pl.ds(pl.multiple_of(x * 1024, 1024), 1024)].reshape(CAP, 8, 128)
        for q in range(CAP):
            dense[q, s, pl.ds(pl.multiple_of(x * 8, 8), 8), :] = planes[q]
        return carry

    lax.fori_loop(0, SPECIES * B, spread_out, 0)

    lane8 = iota((8, 128), 1)

    def faces(k, carry):
        q, s = k // SPECIES, k % SPECIES
        own_faces[q * 6 + 0, s] = dense[q, s, 0:8, :]
        own_faces[q * 6 + 1, s] = dense[q, s, ROWS - 8:ROWS, :]
        low = jnp.zeros((8, 128), jnp.float32)
        high = jnp.zeros((8, 128), jnp.float32)
        for b in range(4):
            first = dense[q, s, pl.ds(64 * b, 8, stride=8), :]
            final = dense[q, s, pl.ds(64 * b + 7, 8, stride=8), :]
            here = lane8 // 32 == b
            low = jnp.where(here, pltpu.roll(first, 32 * b, 1) if b else first, low)
            high = jnp.where(here, pltpu.roll(final, 32 * (b + 1), 1) if b < 3 else final, high)
        own_faces[q * 6 + 2, s] = low
        own_faces[q * 6 + 3, s] = high
        low = jnp.zeros((8, 128), jnp.float32)
        high = jnp.zeros((8, 128), jnp.float32)
        for x in range(B):
            turned = pltpu.roll(dense[q, s, 8 * x:8 * x + 8, :], x + 1, 1)
            high = jnp.where(lane8 % 32 == x, turned, high)
            low = jnp.where(lane8 % 32 == (x + 1) % 32, turned, low)
        own_faces[q * 6 + 4, s] = pltpu.roll(low, 127, 1)
        own_faces[q * 6 + 5, s] = pltpu.roll(high, 96, 1)
        return carry

    lax.fori_loop(0, EARLY, faces, 0)
    pl.semaphore_wait(barrier, expected)

    def opposite(i):
        return AROUND.index((-AROUND[i][0], -AROUND[i][1]))

    def meta_send(i):
        return pltpu.make_async_remote_copy(
            src_ref=meta.at[0], dst_ref=meta.at[1 + opposite(i)],
            send_sem=meta_ss.at[i], recv_sem=meta_rs.at[opposite(i)], device_id=at(AROUND[i]), device_id_type=MESH)

    for i, step in enumerate(AROUND):
        @pl.when(inside(step))
        def _():
            meta_send(i).start()

    lax.fori_loop(EARLY, CAP * SPECIES, faces, 0)

    for i, step in enumerate(AROUND):
        @pl.when(inside(step))
        def _():
            meta_send(i).wait_send()
            pltpu.make_async_remote_copy(
                src_ref=meta.at[0], dst_ref=meta.at[1 + i], send_sem=meta_ss.at[i], recv_sem=meta_rs.at[i],
                device_id=at(step), device_id_type=MESH).wait_recv()

    def device(step):
        return me + step[0] * ny + step[1]

    def sources(step):
        return meta[PLACE[step], CAP:CAP + 1, :]

    taken = []
    for d, step in enumerate(NEAR):
        rel = sources(step) - me * CAP
        slot = jnp.max(jnp.where((rel >= 0) & (rel < CAP), rel, -1))
        taken.append(slot)
    safe = [jnp.maximum(slot, 0) for slot in taken]
    asked = [slot >= 0 for slot in taken]

    def patch_send(d, s):
        return pltpu.make_async_remote_copy(
            src_ref=sendp.at[d, s], dst_ref=landp.at[d ^ 1, s], send_sem=p_ss.at[d, s], recv_sem=p_rs.at[d ^ 1, s],
            device_id=at(NEAR[d]), device_id_type=MESH)

    def patch_wait(d, s):
        return pltpu.make_async_remote_copy(
            src_ref=sendp.at[d, s], dst_ref=landp.at[d, s], send_sem=p_ss.at[d, s], recv_sem=p_rs.at[d, s],
            device_id=at(NEAR[d]), device_id_type=MESH)

    core = gx % 2
    twin = (gx + 1 - 2 * core, gy)
    mine_first, twin_first = core * HALF, (1 - core) * HALF

    def copy_along(src, dst, ss, rs, target):
        return pltpu.make_async_remote_copy(
            src_ref=src, dst_ref=dst, send_sem=ss, recv_sem=rs, device_id=target, device_id_type=MESH)

    def give(e, s):
        return copy_along(sendq.at[e, s], heldq.at[e, s], q_ss.at[e, s], q_rs.at[e, s], twin)

    def carry_send(e, s):
        return copy_along(sendz.at[e, s], landz.at[1 - e, s], z_ss.at[e, s], z_rs.at[1 - e, s], at(NEAR[2 + e]))

    def carry_wait(e, s):
        return copy_along(sendz.at[e, s], landz.at[e, s], z_ss.at[e, s], z_rs.at[e, s], at(NEAR[2 + e]))

    def hand(e, s):
        return copy_along(landz.at[e, s], landq.at[e, s], h_ss.at[e, s], h_rs.at[e, s], twin)

    for s in range(SPECIES):
        for e in range(2):
            @pl.when(inside(NEAR[2 + e]))
            def _():
                sendq[e, s] = dense[safe[2 + e], s, pl.ds(pl.multiple_of(twin_first, HALF), HALF), :]
                give(e, s).start()

    def straight():
        for d in range(2):
            @pl.when(inside(NEAR[d]))
            def _():
                for s in range(SPECIES):
                    sendp[d, s] = dense[safe[d], s]
                    patch_send(d, s).start()


    def face_send(d):
        return pltpu.make_async_remote_copy(
            src_ref=sendf.at[d], dst_ref=landf.at[d ^ 1], send_sem=f_ss.at[d], recv_sem=f_rs.at[d ^ 1],
            device_id=at(NEAR[d]), device_id_type=MESH)

    def face_wait(d):
        return pltpu.make_async_remote_copy(
            src_ref=sendf.at[d], dst_ref=landf.at[d], send_sem=f_ss.at[d], recv_sem=f_rs.at[d],
            device_id=at(NEAR[d]), device_id_type=MESH)

    def ghost_send(d):
        return pltpu.make_async_remote_copy(
            src_ref=sendg.at[d], dst_ref=landg.at[d ^ 1], send_sem=g_ss.at[d], recv_sem=g_rs.at[d ^ 1],
            device_id=at(NEAR[d]), device_id_type=MESH)

    def ghost_wait(d):
        return pltpu.make_async_remote_copy(
            src_ref=sendg.at[d], dst_ref=landg.at[d], send_sem=g_ss.at[d], recv_sem=g_rs.at[d],
            device_id=at(NEAR[d]), device_id_type=MESH)

    side = iota((8, 128), 1)
    far_side = side + 1 - 2 * (side % 2)
    slot_row = iota((8, 128), 0)
    lane1 = iota((1, 128), 1)

    def named(step):
        owner = device(step)
        hit = jnp.zeros((8, 128), jnp.bool_)
        for extra in ((0, 0),) + NEAR:
            hit = hit | (sources((step[0] + extra[0], step[1] + extra[1])) == owner * CAP + slot_row)
        return jnp.max(hit.astype(jnp.int32), axis=1, keepdims=True) > 0

    def wanted(step, of, names):
        rel = meta[PLACE[step]] - device(of) * CAP
        good = names & (rel >= 0) & (rel < CAP) & (slot_row < CAP) & (side < 6)
        code = jnp.where(good, rel * 6 + far_side, 127)
        hit = jnp.zeros((8, 128), jnp.bool_)
        for f in range(6):
            hit = hit | (code[:, f:f + 1] == side)
        mask = jnp.max(hit.astype(jnp.int32), axis=0, keepdims=True)
        mask = jnp.where(lane1 < 36, mask, 0)
        total = mask
        for k in (1, 2, 4, 8, 16, 32):
            total = total + jnp.where(lane1 >= k, pltpu.roll(total, k, 1), 0)
        return mask, total - mask

    mine = named((0, 0))
    over = jnp.zeros((8, 128), jnp.int32)
    for d, step in enumerate(NEAR):
        mask, rank = wanted(step, (0, 0), named(step))
        over = jnp.maximum(over, jnp.where((mask > 0) & (rank >= ROOM), 1, 0))
        chosen = jnp.where((mask > 0) & (rank == slot_row), side, 0)
        table[d] = jnp.broadcast_to(jnp.max(chosen, axis=1, keepdims=True), (8, 128))
        _, rank = wanted((0, 0), step, mine)
        table[4, d:d + 1, :] = rank
    over = jnp.broadcast_to(jnp.max(jnp.max(over, axis=1, keepdims=True), axis=0, keepdims=True), (8, 128))
    twin_base = (me + (1 - 2 * core) * ny) * CAP
    for e, dy in enumerate((-1, 1)):
        rel = sources((0, dy)) - me * CAP
        other = jnp.where(core == 0, sources((1, dy)), sources((-1, dy))) - twin_base
        both = jnp.where((rel >= 0) & (rel < CAP), 1, 0) * jnp.max(
            jnp.where((other >= 0) & (other < CAP), 1, 0), axis=1, keepdims=True)
        over = jnp.maximum(over, jnp.max(both, axis=1, keepdims=True))
    flags[0] = over
    to_scalars = pltpu.make_async_copy(table, table_s, tab_sem)
    to_scalars.start()

    def flag_copy(base, k, target, held):
        return pltpu.make_async_remote_copy(
            src_ref=flags.at[held], dst_ref=flags.at[base + k], send_sem=fl_ss.at[base + k],
            recv_sem=fl_rs.at[base + k], device_id=target, device_id_type=MESH)

    bases = (3, 6, 9)

    for k, target in enumerate(ring[0]):
        flag_copy(bases[0], k, target, 0).start()

    to_scalars.wait()
    for d in ORDER:
        @pl.when(inside(NEAR[d]))
        def _():
            def stage(p, carry):
                sendf[d, p] = own_faces[table_s[d, p, 0]]
                return carry
            lax.fori_loop(0, ROOM, stage, 0)
            face_send(d).start()

    straight()
    for s in range(SPECIES):
        for e in range(2):
            @pl.when(inside(NEAR[2 + e]))
            def _():
                give(e, s).wait_recv()
                own = dense[safe[2 + e], s, pl.ds(pl.multiple_of(mine_first, HALF), HALF), :]
                sendz[e, s] = jnp.where(asked[2 + e], own, heldq[e, s])
                carry_send(e, s).start()

    def flag_round(n, held, following):
        for k, target in enumerate(ring[n]):
            copy = flag_copy(bases[n], k, target, held)
            copy.wait()
        total = flags[held]
        for k in range(len(ring[n])):
            total = jnp.maximum(total, flags[bases[n] + k])
        if following is None:
            flag_out[...] = total
        else:
            flags[following] = total
            for k, target in enumerate(ring[n + 1]):
                flag_copy(bases[n + 1], k, target, following).start()

    kept = []
    for t in range(KEEP):
        rel = src_s[0, t] - me * CAP
        kept.append(jnp.where((rel >= 0) & (rel < CAP), rel, 0))

    def ready(t, carry):
        slot = jnp.where(t == 0, kept[0], kept[1])
        prepare_patch(
            mobility, fermi_gain, rates, lambda s, rows: dense[slot, s, rows, :], coef.at[t], base.at[t])
        return carry
    flag_round(0, 0, 1)
    lax.fori_loop(0, KEEP, ready, 0)

    for d, step in enumerate(NEAR):
        @pl.when(inside(step))
        def _():
            face_wait(d).wait_recv()

    def ghost_place(slot, f):
        nb = nbr_s[slot, f]
        rel = nb - me * CAP
        here = (rel >= 0) & (rel < CAP)
        opposite_f = f + 1 - 2 * (f % 2)
        own = jnp.where(here, rel * 6 + opposite_f, slot * 6 + f)
        own = jnp.where((nb < 0) | here, own, 0)
        away = jnp.int32(-1)
        for d, step in enumerate(NEAR):
            rel = nb - device(step) * CAP
            there = (nb >= 0) & (rel >= 0) & (rel < CAP)
            code = jnp.where(there, rel * 6 + opposite_f, 0)
            away = jnp.where(there, d * ROOM + jnp.minimum(table_s[4, d, code], ROOM - 1), away)
        return own, away

    def ghost_value(slot, f):
        own, away = ghost_place(slot, f)
        other = jnp.maximum(away, 0)
        return jnp.where(away >= 0, landf[other // ROOM, other % ROOM], own_faces[own])

    for d, step in enumerate(NEAR):
        @pl.when(inside(step))
        def _():
            def stage(f, carry):
                sendg[d, f] = ghost_value(safe[d], f)
                return carry
            lax.fori_loop(0, 6, stage, 0)
            ghost_send(d).start()

    flag_round(1, 1, 2)

    def stay(t):
        slot = kept[t]

        def layer(f, carry):
            ghost[f] = ghost_value(slot, f)
            return carry
        lax.fori_loop(0, 6, layer, 0)
        sweep_patch(
            lambda s, rows: dense[slot, s, rows, :], lambda f, s, rows: ghost[f, s, rows, :],
            coef.at[t], base.at[t], ping, result.at[t], lambda s: None)
        pltpu.make_async_copy(result.at[t], swept.at[t], out_sem.at[t]).start()

    stay(0)
    for s in range(SPECIES):
        for e in range(2):
            @pl.when(inside(NEAR[2 + e]))
            def _():
                carry_wait(e, s).wait_recv()
                hand(e, s).start()
    stay(1)

    flag_round(2, 2, None)

    for d, step in enumerate(NEAR):
        @pl.when(inside(step))
        def _():
            face_send(d).wait_send()
            ghost_send(d).wait_send()
            for s in range(SPECIES):
                if d < 2:
                    patch_send(d, s).wait_send()
                    patch_wait(d, s).wait_recv()
                else:
                    give(d - 2, s).wait_send()
                    carry_send(d - 2, s).wait_send()
                    hand(d - 2, s).wait()
            ghost_wait(d).wait_recv()
    for t in range(KEEP):
        pltpu.make_async_copy(result.at[t], swept.at[t], out_sem.at[t]).wait()


def smooth_kernel(
    nx, ny,
    src_s, mobility, fermi_gain, rates, landp, landz, landq, landg, swept,
    out,
    cur, ghost, coef, base, ping, pong, blank, cur_sem, half_sem, ghost_sem, out_sem, zero_sem,
):
    gx, gy = lax.axis_index("gx"), lax.axis_index("gy")
    me = gx * ny + gy
    whence = []
    for t in range(KEEP):
        source = src_s[0, t]
        rel = source - me * CAP
        own = (rel >= 0) & (rel < CAP)
        came = jnp.int32(0)
        for d, step in enumerate(NEAR):
            away = source - (me + step[0] * ny + step[1]) * CAP
            came = jnp.where((away >= 0) & (away < CAP), d, came)
        whence.append((source, own, jnp.where(own, rel, 0), came))

    def fetch_own(t):
        return (pltpu.make_async_copy(swept.at[t], pong.at[t], cur_sem.at[t]),)

    core = gx % 2

    def fetch_moved(t):
        came = whence[t][3]
        e = jnp.maximum(came - 2, 0)
        straight = (
            pltpu.make_async_copy(landp.at[jnp.minimum(came, 1)], cur.at[t], cur_sem.at[t]),
        )
        halves = (
            pltpu.make_async_copy(landz.at[e], cur.at[t, :, pl.ds(pl.multiple_of(core * HALF, HALF), HALF), :], cur_sem.at[t]),
            pltpu.make_async_copy(landq.at[e], cur.at[t, :, pl.ds(pl.multiple_of((1 - core) * HALF, HALF), HALF), :], half_sem.at[t]),
        )
        layers = pltpu.make_async_copy(landg.at[came], ghost.at[t], ghost_sem.at[t])
        return straight, halves, layers

    def start_moved(t):
        straight, halves, layers = fetch_moved(t)
        layers.start()

        @pl.when(whence[t][3] < 2)
        def _():
            straight[0].start()

        @pl.when(whence[t][3] >= 2)
        def _():
            halves[0].start()
            halves[1].start()

    def wait_moved(t):
        straight, halves, layers = fetch_moved(t)
        layers.wait()

        @pl.when(whence[t][3] < 2)
        def _():
            straight[0].wait()

        @pl.when(whence[t][3] >= 2)
        def _():
            halves[0].wait()
            halves[1].wait()

    for t in range(KEEP):
        source, own, slot, came = whence[t]

        @pl.when((source >= 0) & own)
        def _():
            for copy in fetch_own(t):
                copy.start()

        @pl.when((source >= 0) & jnp.logical_not(own))
        def _():
            start_moved(t)

    blank[...] = jnp.zeros(blank.shape, jnp.float32)
    zeros = [
        pltpu.make_async_copy(blank, out.at[pl.ds(s, 1), pl.ds(KEEP, CAP - KEEP), :], zero_sem.at[s])
        for s in range(SPECIES)
    ]
    for copy in zeros:
        copy.start()
    def put_out(t, s):
        return pltpu.make_async_copy(
            pong.at[t, pl.ds(s, 1)].reshape(1, 1, B**3), out.at[pl.ds(s, 1), pl.ds(t, 1), :], out_sem.at[t, s])

    for t in range(KEEP):
        source, own, slot, came = whence[t]

        @pl.when(source < 0)
        def _():
            pong[t] = jnp.zeros((SPECIES, ROWS, 128), jnp.float32)
            for s in range(SPECIES):
                put_out(t, s).start()

        @pl.when((source >= 0) & own)
        def _():
            for copy in fetch_own(t):
                copy.wait()
            for s in range(SPECIES):
                put_out(t, s).start()

    for t in range(KEEP):
        source, own, slot, came = whence[t]

        @pl.when((source >= 0) & jnp.logical_not(own))
        def _():
            wait_moved(t)
            prepare_patch(mobility, fermi_gain, rates, lambda s, rows: cur[t, s, rows, :], coef, base)
            sweep_patch(
                lambda s, rows: cur[t, s, rows, :], lambda f, s, rows: ghost[t, f, s, rows, :], coef, base, ping, pong.at[t],
                lambda s: put_out(t, s).start())

    for copy in zeros:
        copy.wait()
    for t in range(KEEP):
        for s in range(SPECIES):
            put_out(t, s).wait()


def in_vmem():
    return pl.BlockSpec(memory_space=pltpu.VMEM)


def in_smem():
    return pl.BlockSpec(memory_space=pltpu.SMEM)


def anywhere():
    return pl.BlockSpec(memory_space=pl.ANY)


def exchange(nx, ny, conc, neighbours, source, mobility, fermi_gain, rates):
    f32, i32 = jnp.float32, jnp.int32
    dma = pltpu.SemaphoreType.DMA
    n_flags = 3 + nx - 1 + 6
    return pl.pallas_call(
        functools.partial(exchange_kernel, nx, ny),
        out_shape=(
            jax.ShapeDtypeStruct((2, SPECIES, ROWS, 128), f32),
            jax.ShapeDtypeStruct((2, SPECIES, HALF, 128), f32),
            jax.ShapeDtypeStruct((2, SPECIES, HALF, 128), f32),
            jax.ShapeDtypeStruct((4, 6, SPECIES, 8, 128), f32),
            jax.ShapeDtypeStruct((KEEP, SPECIES, ROWS, 128), f32),
            jax.ShapeDtypeStruct((8, 128), i32),
        ),
        in_specs=[anywhere()] + [in_smem()] * 5 + [in_vmem()] * 2,
        out_specs=(anywhere(),) * 5 + (in_vmem(),),
        scratch_shapes=[
            pltpu.VMEM((SPECIES, CAP, B**3), f32),
            pltpu.VMEM((CAP, SPECIES, ROWS, 128), f32),
            pltpu.VMEM((CAP * 6, SPECIES, 8, 128), f32),
            pltpu.VMEM((13, 8, 128), i32),
            pltpu.VMEM((5, 8, 128), i32),
            pltpu.SMEM((5, 8, 128), i32),
            pltpu.VMEM((2, SPECIES, ROWS, 128), f32),
            pltpu.VMEM((2, SPECIES, HALF, 128), f32),
            pltpu.VMEM((2, SPECIES, HALF, 128), f32),
            pltpu.VMEM((2, SPECIES, HALF, 128), f32),
            pltpu.VMEM((4, ROOM, SPECIES, 8, 128), f32),
            pltpu.VMEM((4, ROOM, SPECIES, 8, 128), f32),
            pltpu.VMEM((4, 6, SPECIES, 8, 128), f32),
            pltpu.VMEM((n_flags, 8, 128), i32),
            pltpu.VMEM((6, SPECIES, 8, 128), f32),
            pltpu.VMEM((KEEP, SPECIES, ROWS, 128), f32),
            pltpu.VMEM((KEEP, SPECIES, ROWS, 128), f32),
            pltpu.VMEM((ROWS, 128), f32),
            pltpu.VMEM((KEEP, SPECIES, ROWS, 128), f32),
            dma,
            dma((12,)), dma((12,)),
            dma,
            dma((2, SPECIES)), dma((2, SPECIES)), dma((2, SPECIES)), dma((2, SPECIES)),
            dma((2, SPECIES)), dma((2, SPECIES)), dma((2, SPECIES)), dma((2, SPECIES)), dma((4,)), dma((4,)), dma((4,)), dma((4,)),
            dma((n_flags,)), dma((n_flags,)),
            dma((KEEP,)),
        ],
        compiler_params=pltpu.CompilerParams(collective_id=0, has_side_effects=True, vmem_limit_bytes=40 * 2**20),
    )(conc, neighbours, source, mobility, fermi_gain, rates, neighbours, source)


def smooth(nx, ny, landp, landz, landq, landg, swept, source, mobility, fermi_gain, rates):
    f32 = jnp.float32
    dma = pltpu.SemaphoreType.DMA
    return pl.pallas_call(
        functools.partial(smooth_kernel, nx, ny),
        out_shape=jax.ShapeDtypeStruct((SPECIES, CAP, B**3), f32),
        in_specs=[in_smem()] * 4 + [anywhere()] * 5,
        out_specs=anywhere(),
        scratch_shapes=[
            pltpu.VMEM((KEEP, SPECIES, ROWS, 128), f32),
            pltpu.VMEM((KEEP, 6, SPECIES, 8, 128), f32),
            pltpu.VMEM((SPECIES, ROWS, 128), f32),
            pltpu.VMEM((SPECIES, ROWS, 128), f32),
            pltpu.VMEM((ROWS, 128), f32),
            pltpu.VMEM((KEEP, SPECIES, ROWS, 128), f32),
            pltpu.VMEM((1, CAP - KEEP, B**3), f32),
            dma((KEEP,)),
            dma((KEEP,)),
            dma((KEEP,)),
            dma((KEEP, SPECIES)),
            dma((SPECIES,)),
        ],
        compiler_params=pltpu.CompilerParams(vmem_limit_bytes=60 * 2**20),
    )(source, mobility, fermi_gain, rates, landp, landz, landq, landg, swept)


OPPOSITE = (1, 0, 3, 2, 5, 4)


def passed_along(x, axis, by):
    devices = lax.axis_size(axis)
    pairs = [(i, i + by) for i in range(devices) if 0 <= i + by < devices]
    return lax.ppermute(x, axis, pairs)


def with_halo(x, sides, width):
    edges = {}
    for axis, dim in sides:
        devices, length = (lax.axis_size(axis), x.shape[dim])
        up = [(i, (i + 1) % devices) for i in range(devices - 1)]
        last = lax.slice_in_dim(x, length - width, length, axis=dim)
        leading = lax.slice_in_dim(x, 0, width, axis=dim)
        edges[dim] = (
            lax.ppermute(last, axis, up),
            lax.ppermute(leading, axis, [(b, a) for a, b in up]),
        )
    done = []
    for _, dim in sides:
        low, high = edges[dim]
        around = [(width, width) if d in done else (0, 0) for d in range(x.ndim)]
        x = jnp.concatenate([jnp.pad(low, around), x, jnp.pad(high, around)], axis=dim)
        done.append(dim)
    return x


def faces_of(blocks):
    last = blocks.shape[-1] - 1
    return jnp.stack(
        [
            blocks[..., 0, :, :],
            blocks[..., last, :, :],
            blocks[..., :, 0, :],
            blocks[..., :, last, :],
            blocks[..., :, :, 0],
            blocks[..., :, :, last],
        ],
        axis=-4,
    )


def neighbour_sum(iterate, ghosts):
    lower_x = jnp.concatenate([ghosts[0][:, None], iterate[:, :-1]], axis=1)
    upper_x = jnp.concatenate([iterate[:, 1:], ghosts[1][:, None]], axis=1)
    lower_y = jnp.concatenate([ghosts[2][:, :, None], iterate[:, :, :-1]], axis=2)
    upper_y = jnp.concatenate([iterate[:, :, 1:], ghosts[3][:, :, None]], axis=2)
    lower_z = jnp.concatenate([ghosts[4][..., None], iterate[..., :-1]], axis=3)
    upper_z = jnp.concatenate([iterate[..., 1:], ghosts[5][..., None]], axis=3)
    return lower_x + upper_x + lower_y + upper_y + lower_z + upper_z


def smooth_plain(current, ghosts, mobility, fermi_gain, rates):
    dopant_sum = current[0] + current[3] + current[4]
    half_total = 0.5 * dopant_sum
    electrons = half_total + jnp.sqrt(half_total * half_total + 1.0)
    gain_column = fermi_gain[:, None, None, None]
    spread = (
        mobility[:, None, None, None] * (1.0 + gain_column * electrons[None]) / (1.0 + gain_column)
    )
    dopant, interstitial, vacancy, pair_inter, pair_vacancy = (
        current[0],
        current[1],
        current[2],
        current[3],
        current[4],
    )
    forming_ai = rates[0] * dopant * interstitial - rates[1] * pair_inter
    forming_av = rates[2] * dopant * vacancy - rates[3] * pair_vacancy
    recombine = rates[4] * (interstitial * vacancy - 1.0)
    source = jnp.stack(
        [
            dopant - forming_ai - forming_av,
            interstitial - forming_ai - recombine,
            vacancy - forming_av - recombine,
            pair_inter + forming_ai,
            pair_vacancy + forming_av,
        ],
        axis=0,
    )
    diagonal = 1.0 + 6.0 * spread
    iterate = current
    for repeat in range(SWEEPS):
        iterate = (source + spread * neighbour_sum(iterate, ghosts)) / diagonal
    return iterate


def smooth_all(current, ghosts, mobility, fermi_gain, rates):

    def per_patch(paired):
        return smooth_plain(paired[0], paired[1], mobility, fermi_gain, rates)

    return lax.map(per_patch, (current, ghosts))


def gather_ghosts(face_table, neighbours, column_index, row_index, rows_count, capacity):
    face_rows = face_table.reshape(9 * capacity * 6, SPECIES, B, B)
    safe_slot = jnp.maximum(neighbours, 0)
    source_device = safe_slot // capacity
    step_x = source_device // rows_count - column_index + 1
    step_y = source_device % rows_count - row_index + 1
    opposite = jnp.array(OPPOSITE, jnp.int32)
    face_ids = jnp.arange(6, dtype=jnp.int32)
    remote = ((step_x * 3 + step_y) * capacity + safe_slot % capacity) * 6 + opposite[None, :]
    local = (4 * capacity + jnp.arange(capacity, dtype=jnp.int32)[:, None]) * 6 + face_ids[None, :]
    picked = jnp.clip(jnp.where(neighbours >= 0, remote, local), 0, 9 * capacity * 6 - 1)
    one = functools.partial(lax.dynamic_index_in_dim, face_rows, axis=0, keepdims=False)
    ghosts = lax.map(one, picked.reshape(-1))
    return ghosts.reshape(picked.shape + face_rows.shape[1:])


def counted(hits):
    places = jnp.arange(hits.shape[0])
    before = places[None, :] <= places[:, None]
    return jnp.sum(jnp.where(before & hits[None, :], 1, 0), axis=1) - 1


def pick_rows(pulls, this_device, capacity, payload):
    wanted = (pulls >= 0) & (pulls // capacity == this_device)
    position = counted(wanted)
    chosen = wanted[None, :] & (position[None, :] == jnp.arange(MOVE, dtype=jnp.int32)[:, None])
    slot_list = jnp.sum(jnp.where(chosen, pulls % capacity, 0), axis=1)
    return payload[slot_list]


def place_rows(index, source_device, sender, start):
    from_sender = (source_device == sender) & (source_device >= 0)
    position = counted(from_sender)
    return jnp.where(from_sender, start + position, index)


def relocate(payload, source_slot, requests, this_device, rows_count, capacity):
    source_device = jnp.where(source_slot >= 0, source_slot // capacity, -1)
    index = jnp.where(
        (source_slot >= 0) & (source_device == this_device), source_slot % capacity, -1
    )
    pieces = [payload]
    start = capacity
    for offset in (1, -1):
        outgoing = pick_rows(requests[1 + offset, 1], this_device, capacity, payload)
        arrived = passed_along(outgoing, "gx", offset)
        index = place_rows(index, source_device, this_device - offset * rows_count, start)
        pieces.append(arrived)
        start = start + MOVE
    for offset in (1, -1):
        outgoing = pick_rows(requests[1, 1 + offset], this_device, capacity, payload)
        arrived = passed_along(outgoing, "gy", offset)
        index = place_rows(index, source_device, this_device - offset, start)
        pieces.append(arrived)
        start = start + MOVE
    candidates = jnp.concatenate(pieces, axis=0)
    gathered = candidates[jnp.maximum(index, 0)]
    return jnp.where((index >= 0)[:, None], gathered, jnp.zeros_like(gathered))


def general(concentration, neighbours, source_slot, mobility, fermi_gain, rates):
    capacity = concentration.shape[0]
    cells = concentration.shape[2]
    column_index = lax.axis_index("gx")
    row_index = lax.axis_index("gy")
    rows_count = lax.axis_size("gy")
    this_device = column_index * rows_count + row_index
    blocks = concentration.reshape(capacity, SPECIES, B, B, B)
    own_faces = faces_of(blocks).reshape(1, 1, capacity, 6, SPECIES, B * B)
    face_table = with_halo(own_faces, (("gx", 0), ("gy", 1)), 1)
    requests = with_halo(source_slot.reshape(1, 1, capacity), (("gx", 0), ("gy", 1)), 1)
    ghosts = gather_ghosts(face_table, neighbours, column_index, row_index, rows_count, capacity)
    working = KEEP - 1 + MOVE
    payload = jnp.concatenate(
        [
            concentration.reshape(capacity, SPECIES * cells),
            ghosts.reshape(capacity, 6 * SPECIES * B * B),
        ],
        axis=1,
    )
    arrived = relocate(payload, source_slot, requests, this_device, rows_count, capacity)[:working]
    current = arrived[:, : SPECIES * cells].reshape(working, SPECIES, B, B, B)
    layers = arrived[:, SPECIES * cells :].reshape(working, 6, SPECIES, B, B)
    swept = smooth_all(current, layers, mobility, fermi_gain, rates).reshape(
        working, SPECIES, cells
    )
    live_rows = (source_slot[:working] >= 0)[:, None, None]
    swept = jnp.where(live_rows, swept, jnp.zeros_like(swept))
    return jnp.concatenate(
        [swept, jnp.zeros((capacity - working, SPECIES, cells), jnp.float32)], axis=0
    )


def body(nx, ny, concentration, neighbours, source_slot, mobility, fermi_gain, rates):
    source = source_slot.reshape(1, CAP)
    conc = concentration.transpose(1, 0, 2)
    landp, landz, landq, landg, swept, flag = exchange(nx, ny, conc, neighbours, source, mobility, fermi_gain, rates)

    def common():
        return smooth(nx, ny, landp, landz, landq, landg, swept, source, mobility, fermi_gain, rates).transpose(1, 0, 2)

    def crowded():
        return general(concentration, neighbours, source_slot, mobility, fermi_gain, rates)

    return lax.cond(flag[0, 0] == 0, common, crowded)


def solution(mesh):
    placed = (P(("gx", "gy"), None, None), P(("gx", "gy"), None), P(("gx", "gy")), P(), P(), P())
    return jax.shard_map(
        functools.partial(body, mesh.shape["gx"], mesh.shape["gy"]),
        mesh=mesh, in_specs=placed, out_specs=P(("gx", "gy"), None, None), check_vma=False,
    )
```

```python
import functools

import jax
import jax.numpy as jnp
from jax import lax
from jax.experimental import pallas as pl
from jax.experimental.pallas import tpu as pltpu
from jax.sharding import PartitionSpec as P

B = 32
SPECIES = 5
SWEEPS = 3
KEEP = 2
MOVE = 1
CAP = 6
ROWS = 256
EARLY = 12
ROOM = 6
MESH = pl.DeviceIdType.MESH

NEAR = ((-1, 0), (1, 0), (0, -1), (0, 1))
FAR = ((-2, 0), (2, 0), (0, -2), (0, 2), (-1, -1), (-1, 1), (1, -1), (1, 1))
AROUND = NEAR + FAR
ORDER = (2, 3, 0, 1)
HALF = ROWS // 2
PLACE = {(0, 0): 0, **{step: i + 1 for i, step in enumerate(AROUND)}}


def iota(shape, dim):
    return lax.broadcasted_iota(jnp.int32, shape, dim)


def prepare_patch(mobility, fermi_gain, rates, cell, coef, base):
    scale = [mobility[s] / jnp.full((8, 128), 1.0 + fermi_gain[s]) for s in range(SPECIES)]

    def planes(xo, carry):
        for xi in range(8):
            plane = pl.ds(pl.multiple_of(xo * 64 + xi * 8, 8), 8)
            a, i, v, p, q = [cell(s, plane) for s in range(SPECIES)]
            half = 0.5 * (a + p + q)
            electrons = half + jnp.sqrt(half * half + 1.0)
            ai = rates[0] * a * i - rates[1] * p
            av = rates[2] * a * v - rates[3] * q
            re = rates[4] * (i * v - 1.0)
            sources = (a - ai - av, i - ai - re, v - av - re, p + ai, q + av)
            for s in range(SPECIES):
                spread = scale[s] * (1.0 + fermi_gain[s] * electrons)
                inverse = 1.0 / (1.0 + 6.0 * spread)
                coef[s, plane, :] = spread * inverse
                base[s, plane, :] = sources[s] * inverse
        return carry

    lax.fori_loop(0, 4, planes, 0)


def sweep_patch(cell, layer, coef, base, ping, result, finish):
    lane = iota((8, 128), 1)
    sub = iota((8, 128), 0)
    z = lane % 32
    first_y = (sub == 0) & (lane < 32)
    last_y = (sub == 7) & (lane >= 96)
    whole = pl.ds(0, 8)

    def ghosts(s):
        for x in range(B):
            plane = pl.ds(8 * x, 8)
            low = pltpu.roll(layer(4, s, whole), (128 - x) % 128, 1) if x else layer(4, s, whole)
            high = pltpu.roll(layer(5, s, whole), 31 - x, 1) if x < 31 else layer(5, s, whole)
            extra = jnp.where(z == 0, low, jnp.where(z == 31, high, 0.0))
            low = jnp.broadcast_to(layer(2, s, pl.ds(x % 8, 1)), (8, 128))
            high = jnp.broadcast_to(layer(3, s, pl.ds(x % 8, 1)), (8, 128))
            xo = x // 8
            low = pltpu.roll(low, 128 - 32 * xo, 1) if xo else low
            high = pltpu.roll(high, 96 - 32 * xo, 1) if xo < 3 else high
            extra = extra + jnp.where(first_y, low, jnp.where(last_y, high, 0.0))
            if x == 0:
                extra = extra + layer(0, s, whole)
            if x == B - 1:
                extra = extra + layer(1, s, whole)
            base[s, plane, :] = base[s, plane, :] + coef[s, plane, :] * extra

    def species(s, carry):
        def sweep(get, put):
            before = None
            here = get(0)
            for x in range(B):
                after = get(x + 1) if x + 1 < B else None
                total = jnp.where(z == 0, 0.0, pltpu.roll(here, 1, 1)) + jnp.where(z == 31, 0.0, pltpu.roll(here, 127, 1))
                down = pltpu.roll(here, 32, 1)
                down = jnp.where(lane >= 32, down, pltpu.roll(down, 1, 0))
                up = pltpu.roll(here, 96, 1)
                up = jnp.where(lane < 96, up, pltpu.roll(up, 7, 0))
                total = total + jnp.where(first_y, 0.0, down) + jnp.where(last_y, 0.0, up)
                if before is not None:
                    total = total + before
                if after is not None:
                    total = total + after
                put(x, base[s, 8 * x:8 * x + 8, :] + coef[s, 8 * x:8 * x + 8, :] * total)
                before, here = here, after

        def put_ping(x, value):
            ping[8 * x:8 * x + 8, :] = value

        def put_result(x, value):
            result[s, 8 * x:8 * x + 8, :] = value

        ghosts(s)
        sweep(lambda x: cell(s, pl.ds(8 * x, 8)), put_result)
        sweep(lambda x: result[s, 8 * x:8 * x + 8, :], put_ping)
        sweep(lambda x: ping[8 * x:8 * x + 8, :], put_result)
        finish(s)
        return carry

    lax.fori_loop(0, SPECIES, species, 0)


def exchange_kernel(
    nx, ny,
    conc, nbr_s, src_s, mobility, fermi_gain, rates, nbr_v, src_v,
    landp, landz, landq, landg, swept, flag_out,
    raw, dense, own_faces, meta, table, table_s, sendp, sendq, heldq, sendz, sendf, landf, sendg, flags, ghost, coef, base, ping, result,
    in_sem, meta_ss, meta_rs, tab_sem, p_ss, p_rs, q_ss, q_rs, z_ss, z_rs, h_ss, h_rs, f_ss, f_rs, g_ss, g_rs, fl_ss, fl_rs, out_sem,
):
    gx, gy = lax.axis_index("gx"), lax.axis_index("gy")
    me = gx * ny + gy

    def inside(step):
        x, y = gx + step[0], gy + step[1]
        return (x >= 0) & (x < nx) & (y >= 0) & (y < ny)

    def at(step):
        return (gx + step[0], gy + step[1])

    load = pltpu.make_async_copy(conc, raw, in_sem)
    load.start()

    row, col = gy // 4, gy % 4
    ring = (
        [(gx, row * 4 + (col + k) % 4) for k in range(1, 4)],
        [(gx, ((row + k) % 4) * 4 + col) for k in range(1, 4)],
        [((gx + k) % nx, gy) for k in range(1, nx)],
    )

    meta[...] = jnp.full(meta.shape, -1, jnp.int32)
    meta[0, 0:CAP, 0:6] = nbr_v[...]
    meta[0, CAP:CAP + 1, 0:CAP] = src_v[...]

    barrier = pltpu.get_barrier_semaphore()
    expected = nx - 1 + 6
    for step in AROUND:
        there = inside(step)
        expected = expected + there.astype(jnp.int32)

        @pl.when(there)
        def _():
            pl.semaphore_signal(barrier, inc=1, device_id=at(step), device_id_type=MESH)
    for group in ring:
        for target in group:
            pl.semaphore_signal(barrier, inc=1, device_id=target, device_id_type=MESH)
    load.wait()

    def spread_out(k, carry):
        s, x = k // B, k % B
        planes = raw[s, :, pl.ds(pl.multiple_of(x * 1024, 1024), 1024)].reshape(CAP, 8, 128)
        for q in range(CAP):
            dense[q, s, pl.ds(pl.multiple_of(x * 8, 8), 8), :] = planes[q]
        return carry

    lax.fori_loop(0, SPECIES * B, spread_out, 0)

    lane8 = iota((8, 128), 1)

    def faces(k, carry):
        q, s = k // SPECIES, k % SPECIES
        own_faces[q * 6 + 0, s] = dense[q, s, 0:8, :]
        own_faces[q * 6 + 1, s] = dense[q, s, ROWS - 8:ROWS, :]
        low = jnp.zeros((8, 128), jnp.float32)
        high = jnp.zeros((8, 128), jnp.float32)
        for b in range(4):
            first = dense[q, s, pl.ds(64 * b, 8, stride=8), :]
            final = dense[q, s, pl.ds(64 * b + 7, 8, stride=8), :]
            here = lane8 // 32 == b
            low = jnp.where(here, pltpu.roll(first, 32 * b, 1) if b else first, low)
            high = jnp.where(here, pltpu.roll(final, 32 * (b + 1), 1) if b < 3 else final, high)
        own_faces[q * 6 + 2, s] = low
        own_faces[q * 6 + 3, s] = high
        low = jnp.zeros((8, 128), jnp.float32)
        high = jnp.zeros((8, 128), jnp.float32)
        for x in range(B):
            turned = pltpu.roll(dense[q, s, 8 * x:8 * x + 8, :], x + 1, 1)
            high = jnp.where(lane8 % 32 == x, turned, high)
            low = jnp.where(lane8 % 32 == (x + 1) % 32, turned, low)
        own_faces[q * 6 + 4, s] = pltpu.roll(low, 127, 1)
        own_faces[q * 6 + 5, s] = pltpu.roll(high, 96, 1)
        return carry

    lax.fori_loop(0, EARLY, faces, 0)
    pl.semaphore_wait(barrier, expected)

    def opposite(i):
        return AROUND.index((-AROUND[i][0], -AROUND[i][1]))

    def meta_send(i):
        return pltpu.make_async_remote_copy(
            src_ref=meta.at[0], dst_ref=meta.at[1 + opposite(i)],
            send_sem=meta_ss.at[i], recv_sem=meta_rs.at[opposite(i)], device_id=at(AROUND[i]), device_id_type=MESH)

    for i, step in enumerate(AROUND):
        @pl.when(inside(step))
        def _():
            meta_send(i).start()

    lax.fori_loop(EARLY, CAP * SPECIES, faces, 0)

    for i, step in enumerate(AROUND):
        @pl.when(inside(step))
        def _():
            meta_send(i).wait_send()
            pltpu.make_async_remote_copy(
                src_ref=meta.at[0], dst_ref=meta.at[1 + i], send_sem=meta_ss.at[i], recv_sem=meta_rs.at[i],
                device_id=at(step), device_id_type=MESH).wait_recv()

    def device(step):
        return me + step[0] * ny + step[1]

    def sources(step):
        return meta[PLACE[step], CAP:CAP + 1, :]

    taken = []
    for d, step in enumerate(NEAR):
        rel = sources(step) - me * CAP
        slot = jnp.max(jnp.where((rel >= 0) & (rel < CAP), rel, -1))
        taken.append(slot)
    safe = [jnp.maximum(slot, 0) for slot in taken]
    asked = [slot >= 0 for slot in taken]

    def patch_send(d, s):
        return pltpu.make_async_remote_copy(
            src_ref=sendp.at[d, s], dst_ref=landp.at[d ^ 1, s], send_sem=p_ss.at[d, s], recv_sem=p_rs.at[d ^ 1, s],
            device_id=at(NEAR[d]), device_id_type=MESH)

    def patch_wait(d, s):
        return pltpu.make_async_remote_copy(
            src_ref=sendp.at[d, s], dst_ref=landp.at[d, s], send_sem=p_ss.at[d, s], recv_sem=p_rs.at[d, s],
            device_id=at(NEAR[d]), device_id_type=MESH)

    core = gx % 2
    twin = (gx + 1 - 2 * core, gy)
    mine_first, twin_first = core * HALF, (1 - core) * HALF

    def copy_along(src, dst, ss, rs, target):
        return pltpu.make_async_remote_copy(
            src_ref=src, dst_ref=dst, send_sem=ss, recv_sem=rs, device_id=target, device_id_type=MESH)

    def give(e, s):
        return copy_along(sendq.at[e, s], heldq.at[e, s], q_ss.at[e, s], q_rs.at[e, s], twin)

    def carry_send(e, s):
        return copy_along(sendz.at[e, s], landz.at[1 - e, s], z_ss.at[e, s], z_rs.at[1 - e, s], at(NEAR[2 + e]))

    def carry_wait(e, s):
        return copy_along(sendz.at[e, s], landz.at[e, s], z_ss.at[e, s], z_rs.at[e, s], at(NEAR[2 + e]))

    def hand(e, s):
        return copy_along(landz.at[e, s], landq.at[e, s], h_ss.at[e, s], h_rs.at[e, s], twin)

    for s in range(SPECIES):
        for e in range(2):
            @pl.when(inside(NEAR[2 + e]))
            def _():
                sendq[e, s] = dense[safe[2 + e], s, pl.ds(pl.multiple_of(twin_first, HALF), HALF), :]
                give(e, s).start()

    def straight():
        for d in range(2):
            @pl.when(inside(NEAR[d]))
            def _():
                for s in range(SPECIES):
                    sendp[d, s] = dense[safe[d], s]
                    patch_send(d, s).start()


    def face_send(d):
        return pltpu.make_async_remote_copy(
            src_ref=sendf.at[d], dst_ref=landf.at[d ^ 1], send_sem=f_ss.at[d], recv_sem=f_rs.at[d ^ 1],
            device_id=at(NEAR[d]), device_id_type=MESH)

    def face_wait(d):
        return pltpu.make_async_remote_copy(
            src_ref=sendf.at[d], dst_ref=landf.at[d], send_sem=f_ss.at[d], recv_sem=f_rs.at[d],
            device_id=at(NEAR[d]), device_id_type=MESH)

    def ghost_send(d):
        return pltpu.make_async_remote_copy(
            src_ref=sendg.at[d], dst_ref=landg.at[d ^ 1], send_sem=g_ss.at[d], recv_sem=g_rs.at[d ^ 1],
            device_id=at(NEAR[d]), device_id_type=MESH)

    def ghost_wait(d):
        return pltpu.make_async_remote_copy(
            src_ref=sendg.at[d], dst_ref=landg.at[d], send_sem=g_ss.at[d], recv_sem=g_rs.at[d],
            device_id=at(NEAR[d]), device_id_type=MESH)

    side = iota((8, 128), 1)
    far_side = side + 1 - 2 * (side % 2)
    slot_row = iota((8, 128), 0)
    lane1 = iota((1, 128), 1)

    def named(step):
        owner = device(step)
        hit = jnp.zeros((8, 128), jnp.bool_)
        for extra in ((0, 0),) + NEAR:
            hit = hit | (sources((step[0] + extra[0], step[1] + extra[1])) == owner * CAP + slot_row)
        return jnp.max(hit.astype(jnp.int32), axis=1, keepdims=True) > 0

    def wanted(step, of, names):
        rel = meta[PLACE[step]] - device(of) * CAP
        good = names & (rel >= 0) & (rel < CAP) & (slot_row < CAP) & (side < 6)
        code = jnp.where(good, rel * 6 + far_side, 127)
        hit = jnp.zeros((8, 128), jnp.bool_)
        for f in range(6):
            hit = hit | (code[:, f:f + 1] == side)
        mask = jnp.max(hit.astype(jnp.int32), axis=0, keepdims=True)
        mask = jnp.where(lane1 < 36, mask, 0)
        total = mask
        for k in (1, 2, 4, 8, 16, 32):
            total = total + jnp.where(lane1 >= k, pltpu.roll(total, k, 1), 0)
        return mask, total - mask

    mine = named((0, 0))
    over = jnp.zeros((8, 128), jnp.int32)
    for d, step in enumerate(NEAR):
        mask, rank = wanted(step, (0, 0), named(step))
        over = jnp.maximum(over, jnp.where((mask > 0) & (rank >= ROOM), 1, 0))
        chosen = jnp.where((mask > 0) & (rank == slot_row), side, 0)
        table[d] = jnp.broadcast_to(jnp.max(chosen, axis=1, keepdims=True), (8, 128))
        _, rank = wanted((0, 0), step, mine)
        table[4, d:d + 1, :] = rank
    over = jnp.broadcast_to(jnp.max(jnp.max(over, axis=1, keepdims=True), axis=0, keepdims=True), (8, 128))
    twin_base = (me + (1 - 2 * core) * ny) * CAP
    for e, dy in enumerate((-1, 1)):
        rel = sources((0, dy)) - me * CAP
        other = jnp.where(core == 0, sources((1, dy)), sources((-1, dy))) - twin_base
        both = jnp.where((rel >= 0) & (rel < CAP), 1, 0) * jnp.max(
            jnp.where((other >= 0) & (other < CAP), 1, 0), axis=1, keepdims=True)
        over = jnp.maximum(over, jnp.max(both, axis=1, keepdims=True))
    flags[0] = over
    to_scalars = pltpu.make_async_copy(table, table_s, tab_sem)
    to_scalars.start()

    def flag_copy(base, k, target, held):
        return pltpu.make_async_remote_copy(
            src_ref=flags.at[held], dst_ref=flags.at[base + k], send_sem=fl_ss.at[base + k],
            recv_sem=fl_rs.at[base + k], device_id=target, device_id_type=MESH)

    bases = (3, 6, 9)

    for k, target in enumerate(ring[0]):
        flag_copy(bases[0], k, target, 0).start()

    to_scalars.wait()
    for d in ORDER:
        @pl.when(inside(NEAR[d]))
        def _():
            def stage(p, carry):
                sendf[d, p] = own_faces[table_s[d, p, 0]]
                return carry
            lax.fori_loop(0, ROOM, stage, 0)
            face_send(d).start()

    straight()
    for s in range(SPECIES):
        for e in range(2):
            @pl.when(inside(NEAR[2 + e]))
            def _():
                give(e, s).wait_recv()
                own = dense[safe[2 + e], s, pl.ds(pl.multiple_of(mine_first, HALF), HALF), :]
                sendz[e, s] = jnp.where(asked[2 + e], own, heldq[e, s])
                carry_send(e, s).start()

    def flag_round(n, held, following):
        for k, target in enumerate(ring[n]):
            copy = flag_copy(bases[n], k, target, held)
            copy.wait()
        total = flags[held]
        for k in range(len(ring[n])):
            total = jnp.maximum(total, flags[bases[n] + k])
        if following is None:
            flag_out[...] = total
        else:
            flags[following] = total
            for k, target in enumerate(ring[n + 1]):
                flag_copy(bases[n + 1], k, target, following).start()

    kept = []
    for t in range(KEEP):
        rel = src_s[0, t] - me * CAP
        kept.append(jnp.where((rel >= 0) & (rel < CAP), rel, 0))

    def ready(t, carry):
        slot = jnp.where(t == 0, kept[0], kept[1])
        prepare_patch(
            mobility, fermi_gain, rates, lambda s, rows: dense[slot, s, rows, :], coef.at[t], base.at[t])
        return carry
    lax.fori_loop(0, KEEP, ready, 0)

    for d, step in enumerate(NEAR):
        @pl.when(inside(step))
        def _():
            face_wait(d).wait_recv()

    flag_round(0, 0, 1)

    def ghost_place(slot, f):
        nb = nbr_s[slot, f]
        rel = nb - me * CAP
        here = (rel >= 0) & (rel < CAP)
        opposite_f = f + 1 - 2 * (f % 2)
        own = jnp.where(here, rel * 6 + opposite_f, slot * 6 + f)
        own = jnp.where((nb < 0) | here, own, 0)
        away = jnp.int32(-1)
        for d, step in enumerate(NEAR):
            rel = nb - device(step) * CAP
            there = (nb >= 0) & (rel >= 0) & (rel < CAP)
            code = jnp.where(there, rel * 6 + opposite_f, 0)
            away = jnp.where(there, d * ROOM + jnp.minimum(table_s[4, d, code], ROOM - 1), away)
        return own, away

    def ghost_value(slot, f):
        own, away = ghost_place(slot, f)
        other = jnp.maximum(away, 0)
        return jnp.where(away >= 0, landf[other // ROOM, other % ROOM], own_faces[own])

    for d, step in enumerate(NEAR):
        @pl.when(inside(step))
        def _():
            def stage(f, carry):
                sendg[d, f] = ghost_value(safe[d], f)
                return carry
            lax.fori_loop(0, 6, stage, 0)
            ghost_send(d).start()

    def stay(t):
        slot = kept[t]

        def layer(f, carry):
            ghost[f] = ghost_value(slot, f)
            return carry
        lax.fori_loop(0, 6, layer, 0)
        sweep_patch(
            lambda s, rows: dense[slot, s, rows, :], lambda f, s, rows: ghost[f, s, rows, :],
            coef.at[t], base.at[t], ping, result.at[t], lambda s: None)
        pltpu.make_async_copy(result.at[t], swept.at[t], out_sem.at[t]).start()

    stay(0)
    flag_round(1, 1, 2)
    for s in range(SPECIES):
        for e in range(2):
            @pl.when(inside(NEAR[2 + e]))
            def _():
                carry_wait(e, s).wait_recv()
                hand(e, s).start()
    stay(1)

    flag_round(2, 2, None)

    for d, step in enumerate(NEAR):
        @pl.when(inside(step))
        def _():
            face_send(d).wait_send()
            ghost_send(d).wait_send()
            for s in range(SPECIES):
                if d < 2:
                    patch_send(d, s).wait_send()
                    patch_wait(d, s).wait_recv()
                else:
                    give(d - 2, s).wait_send()
                    carry_send(d - 2, s).wait_send()
                    hand(d - 2, s).wait()
            ghost_wait(d).wait_recv()
    for t in range(KEEP):
        pltpu.make_async_copy(result.at[t], swept.at[t], out_sem.at[t]).wait()


def smooth_kernel(
    nx, ny,
    src_s, mobility, fermi_gain, rates, landp, landz, landq, landg, swept,
    out,
    cur, ghost, coef, base, ping, pong, blank, cur_sem, half_sem, ghost_sem, out_sem, zero_sem,
):
    gx, gy = lax.axis_index("gx"), lax.axis_index("gy")
    me = gx * ny + gy
    whence = []
    for t in range(KEEP):
        source = src_s[0, t]
        rel = source - me * CAP
        own = (rel >= 0) & (rel < CAP)
        came = jnp.int32(0)
        for d, step in enumerate(NEAR):
            away = source - (me + step[0] * ny + step[1]) * CAP
            came = jnp.where((away >= 0) & (away < CAP), d, came)
        whence.append((source, own, jnp.where(own, rel, 0), came))

    def fetch_own(t):
        return (pltpu.make_async_copy(swept.at[t], pong.at[t], cur_sem.at[t]),)

    core = gx % 2

    def fetch_moved(t):
        came = whence[t][3]
        e = jnp.maximum(came - 2, 0)
        straight = (
            pltpu.make_async_copy(landp.at[jnp.minimum(came, 1)], cur.at[t], cur_sem.at[t]),
        )
        halves = (
            pltpu.make_async_copy(landz.at[e], cur.at[t, :, pl.ds(pl.multiple_of(core * HALF, HALF), HALF), :], cur_sem.at[t]),
            pltpu.make_async_copy(landq.at[e], cur.at[t, :, pl.ds(pl.multiple_of((1 - core) * HALF, HALF), HALF), :], half_sem.at[t]),
        )
        layers = pltpu.make_async_copy(landg.at[came], ghost.at[t], ghost_sem.at[t])
        return straight, halves, layers

    def start_moved(t):
        straight, halves, layers = fetch_moved(t)
        layers.start()

        @pl.when(whence[t][3] < 2)
        def _():
            straight[0].start()

        @pl.when(whence[t][3] >= 2)
        def _():
            halves[0].start()
            halves[1].start()

    def wait_moved(t):
        straight, halves, layers = fetch_moved(t)
        layers.wait()

        @pl.when(whence[t][3] < 2)
        def _():
            straight[0].wait()

        @pl.when(whence[t][3] >= 2)
        def _():
            halves[0].wait()
            halves[1].wait()

    for t in range(KEEP):
        source, own, slot, came = whence[t]

        @pl.when((source >= 0) & own)
        def _():
            for copy in fetch_own(t):
                copy.start()

        @pl.when((source >= 0) & jnp.logical_not(own))
        def _():
            start_moved(t)

    blank[...] = jnp.zeros(blank.shape, jnp.float32)
    zeros = [
        pltpu.make_async_copy(blank, out.at[pl.ds(s, 1), pl.ds(KEEP, CAP - KEEP), :], zero_sem.at[s])
        for s in range(SPECIES)
    ]
    for copy in zeros:
        copy.start()
    def put_out(t, s):
        return pltpu.make_async_copy(
            pong.at[t, pl.ds(s, 1)].reshape(1, 1, B**3), out.at[pl.ds(s, 1), pl.ds(t, 1), :], out_sem.at[t, s])

    for t in range(KEEP):
        source, own, slot, came = whence[t]

        @pl.when(source < 0)
        def _():
            pong[t] = jnp.zeros((SPECIES, ROWS, 128), jnp.float32)
            for s in range(SPECIES):
                put_out(t, s).start()

        @pl.when((source >= 0) & own)
        def _():
            for copy in fetch_own(t):
                copy.wait()
            for s in range(SPECIES):
                put_out(t, s).start()

    for t in range(KEEP):
        source, own, slot, came = whence[t]

        @pl.when((source >= 0) & jnp.logical_not(own))
        def _():
            wait_moved(t)
            prepare_patch(mobility, fermi_gain, rates, lambda s, rows: cur[t, s, rows, :], coef, base)
            sweep_patch(
                lambda s, rows: cur[t, s, rows, :], lambda f, s, rows: ghost[t, f, s, rows, :], coef, base, ping, pong.at[t],
                lambda s: put_out(t, s).start())

    for copy in zeros:
        copy.wait()
    for t in range(KEEP):
        for s in range(SPECIES):
            put_out(t, s).wait()


def in_vmem():
    return pl.BlockSpec(memory_space=pltpu.VMEM)


def in_smem():
    return pl.BlockSpec(memory_space=pltpu.SMEM)


def anywhere():
    return pl.BlockSpec(memory_space=pl.ANY)


def exchange(nx, ny, conc, neighbours, source, mobility, fermi_gain, rates):
    f32, i32 = jnp.float32, jnp.int32
    dma = pltpu.SemaphoreType.DMA
    n_flags = 3 + nx - 1 + 6
    return pl.pallas_call(
        functools.partial(exchange_kernel, nx, ny),
        out_shape=(
            jax.ShapeDtypeStruct((2, SPECIES, ROWS, 128), f32),
            jax.ShapeDtypeStruct((2, SPECIES, HALF, 128), f32),
            jax.ShapeDtypeStruct((2, SPECIES, HALF, 128), f32),
            jax.ShapeDtypeStruct((4, 6, SPECIES, 8, 128), f32),
            jax.ShapeDtypeStruct((KEEP, SPECIES, ROWS, 128), f32),
            jax.ShapeDtypeStruct((8, 128), i32),
        ),
        in_specs=[anywhere()] + [in_smem()] * 5 + [in_vmem()] * 2,
        out_specs=(anywhere(),) * 5 + (in_vmem(),),
        scratch_shapes=[
            pltpu.VMEM((SPECIES, CAP, B**3), f32),
            pltpu.VMEM((CAP, SPECIES, ROWS, 128), f32),
            pltpu.VMEM((CAP * 6, SPECIES, 8, 128), f32),
            pltpu.VMEM((13, 8, 128), i32),
            pltpu.VMEM((5, 8, 128), i32),
            pltpu.SMEM((5, 8, 128), i32),
            pltpu.VMEM((2, SPECIES, ROWS, 128), f32),
            pltpu.VMEM((2, SPECIES, HALF, 128), f32),
            pltpu.VMEM((2, SPECIES, HALF, 128), f32),
            pltpu.VMEM((2, SPECIES, HALF, 128), f32),
            pltpu.VMEM((4, ROOM, SPECIES, 8, 128), f32),
            pltpu.VMEM((4, ROOM, SPECIES, 8, 128), f32),
            pltpu.VMEM((4, 6, SPECIES, 8, 128), f32),
            pltpu.VMEM((n_flags, 8, 128), i32),
            pltpu.VMEM((6, SPECIES, 8, 128), f32),
            pltpu.VMEM((KEEP, SPECIES, ROWS, 128), f32),
            pltpu.VMEM((KEEP, SPECIES, ROWS, 128), f32),
            pltpu.VMEM((ROWS, 128), f32),
            pltpu.VMEM((KEEP, SPECIES, ROWS, 128), f32),
            dma,
            dma((12,)), dma((12,)),
            dma,
            dma((2, SPECIES)), dma((2, SPECIES)), dma((2, SPECIES)), dma((2, SPECIES)),
            dma((2, SPECIES)), dma((2, SPECIES)), dma((2, SPECIES)), dma((2, SPECIES)), dma((4,)), dma((4,)), dma((4,)), dma((4,)),
            dma((n_flags,)), dma((n_flags,)),
            dma((KEEP,)),
        ],
        compiler_params=pltpu.CompilerParams(collective_id=0, has_side_effects=True, vmem_limit_bytes=40 * 2**20),
    )(conc, neighbours, source, mobility, fermi_gain, rates, neighbours, source)


def smooth(nx, ny, landp, landz, landq, landg, swept, source, mobility, fermi_gain, rates):
    f32 = jnp.float32
    dma = pltpu.SemaphoreType.DMA
    return pl.pallas_call(
        functools.partial(smooth_kernel, nx, ny),
        out_shape=jax.ShapeDtypeStruct((SPECIES, CAP, B**3), f32),
        in_specs=[in_smem()] * 4 + [anywhere()] * 5,
        out_specs=anywhere(),
        scratch_shapes=[
            pltpu.VMEM((KEEP, SPECIES, ROWS, 128), f32),
            pltpu.VMEM((KEEP, 6, SPECIES, 8, 128), f32),
            pltpu.VMEM((SPECIES, ROWS, 128), f32),
            pltpu.VMEM((SPECIES, ROWS, 128), f32),
            pltpu.VMEM((ROWS, 128), f32),
            pltpu.VMEM((KEEP, SPECIES, ROWS, 128), f32),
            pltpu.VMEM((1, CAP - KEEP, B**3), f32),
            dma((KEEP,)),
            dma((KEEP,)),
            dma((KEEP,)),
            dma((KEEP, SPECIES)),
            dma((SPECIES,)),
        ],
        compiler_params=pltpu.CompilerParams(vmem_limit_bytes=60 * 2**20),
    )(source, mobility, fermi_gain, rates, landp, landz, landq, landg, swept)


OPPOSITE = (1, 0, 3, 2, 5, 4)


def passed_along(x, axis, by):
    devices = lax.axis_size(axis)
    pairs = [(i, i + by) for i in range(devices) if 0 <= i + by < devices]
    return lax.ppermute(x, axis, pairs)


def with_halo(x, sides, width):
    edges = {}
    for axis, dim in sides:
        devices, length = (lax.axis_size(axis), x.shape[dim])
        up = [(i, (i + 1) % devices) for i in range(devices - 1)]
        last = lax.slice_in_dim(x, length - width, length, axis=dim)
        leading = lax.slice_in_dim(x, 0, width, axis=dim)
        edges[dim] = (
            lax.ppermute(last, axis, up),
            lax.ppermute(leading, axis, [(b, a) for a, b in up]),
        )
    done = []
    for _, dim in sides:
        low, high = edges[dim]
        around = [(width, width) if d in done else (0, 0) for d in range(x.ndim)]
        x = jnp.concatenate([jnp.pad(low, around), x, jnp.pad(high, around)], axis=dim)
        done.append(dim)
    return x


def faces_of(blocks):
    last = blocks.shape[-1] - 1
    return jnp.stack(
        [
            blocks[..., 0, :, :],
            blocks[..., last, :, :],
            blocks[..., :, 0, :],
            blocks[..., :, last, :],
            blocks[..., :, :, 0],
            blocks[..., :, :, last],
        ],
        axis=-4,
    )


def neighbour_sum(iterate, ghosts):
    lower_x = jnp.concatenate([ghosts[0][:, None], iterate[:, :-1]], axis=1)
    upper_x = jnp.concatenate([iterate[:, 1:], ghosts[1][:, None]], axis=1)
    lower_y = jnp.concatenate([ghosts[2][:, :, None], iterate[:, :, :-1]], axis=2)
    upper_y = jnp.concatenate([iterate[:, :, 1:], ghosts[3][:, :, None]], axis=2)
    lower_z = jnp.concatenate([ghosts[4][..., None], iterate[..., :-1]], axis=3)
    upper_z = jnp.concatenate([iterate[..., 1:], ghosts[5][..., None]], axis=3)
    return lower_x + upper_x + lower_y + upper_y + lower_z + upper_z


def smooth_plain(current, ghosts, mobility, fermi_gain, rates):
    dopant_sum = current[0] + current[3] + current[4]
    half_total = 0.5 * dopant_sum
    electrons = half_total + jnp.sqrt(half_total * half_total + 1.0)
    gain_column = fermi_gain[:, None, None, None]
    spread = (
        mobility[:, None, None, None] * (1.0 + gain_column * electrons[None]) / (1.0 + gain_column)
    )
    dopant, interstitial, vacancy, pair_inter, pair_vacancy = (
        current[0],
        current[1],
        current[2],
        current[3],
        current[4],
    )
    forming_ai = rates[0] * dopant * interstitial - rates[1] * pair_inter
    forming_av = rates[2] * dopant * vacancy - rates[3] * pair_vacancy
    recombine = rates[4] * (interstitial * vacancy - 1.0)
    source = jnp.stack(
        [
            dopant - forming_ai - forming_av,
            interstitial - forming_ai - recombine,
            vacancy - forming_av - recombine,
            pair_inter + forming_ai,
            pair_vacancy + forming_av,
        ],
        axis=0,
    )
    diagonal = 1.0 + 6.0 * spread
    iterate = current
    for repeat in range(SWEEPS):
        iterate = (source + spread * neighbour_sum(iterate, ghosts)) / diagonal
    return iterate


def smooth_all(current, ghosts, mobility, fermi_gain, rates):

    def per_patch(paired):
        return smooth_plain(paired[0], paired[1], mobility, fermi_gain, rates)

    return lax.map(per_patch, (current, ghosts))


def gather_ghosts(face_table, neighbours, column_index, row_index, rows_count, capacity):
    face_rows = face_table.reshape(9 * capacity * 6, SPECIES, B, B)
    safe_slot = jnp.maximum(neighbours, 0)
    source_device = safe_slot // capacity
    step_x = source_device // rows_count - column_index + 1
    step_y = source_device % rows_count - row_index + 1
    opposite = jnp.array(OPPOSITE, jnp.int32)
    face_ids = jnp.arange(6, dtype=jnp.int32)
    remote = ((step_x * 3 + step_y) * capacity + safe_slot % capacity) * 6 + opposite[None, :]
    local = (4 * capacity + jnp.arange(capacity, dtype=jnp.int32)[:, None]) * 6 + face_ids[None, :]
    picked = jnp.clip(jnp.where(neighbours >= 0, remote, local), 0, 9 * capacity * 6 - 1)
    one = functools.partial(lax.dynamic_index_in_dim, face_rows, axis=0, keepdims=False)
    ghosts = lax.map(one, picked.reshape(-1))
    return ghosts.reshape(picked.shape + face_rows.shape[1:])


def counted(hits):
    places = jnp.arange(hits.shape[0])
    before = places[None, :] <= places[:, None]
    return jnp.sum(jnp.where(before & hits[None, :], 1, 0), axis=1) - 1


def pick_rows(pulls, this_device, capacity, payload):
    wanted = (pulls >= 0) & (pulls // capacity == this_device)
    position = counted(wanted)
    chosen = wanted[None, :] & (position[None, :] == jnp.arange(MOVE, dtype=jnp.int32)[:, None])
    slot_list = jnp.sum(jnp.where(chosen, pulls % capacity, 0), axis=1)
    return payload[slot_list]


def place_rows(index, source_device, sender, start):
    from_sender = (source_device == sender) & (source_device >= 0)
    position = counted(from_sender)
    return jnp.where(from_sender, start + position, index)


def relocate(payload, source_slot, requests, this_device, rows_count, capacity):
    source_device = jnp.where(source_slot >= 0, source_slot // capacity, -1)
    index = jnp.where(
        (source_slot >= 0) & (source_device == this_device), source_slot % capacity, -1
    )
    pieces = [payload]
    start = capacity
    for offset in (1, -1):
        outgoing = pick_rows(requests[1 + offset, 1], this_device, capacity, payload)
        arrived = passed_along(outgoing, "gx", offset)
        index = place_rows(index, source_device, this_device - offset * rows_count, start)
        pieces.append(arrived)
        start = start + MOVE
    for offset in (1, -1):
        outgoing = pick_rows(requests[1, 1 + offset], this_device, capacity, payload)
        arrived = passed_along(outgoing, "gy", offset)
        index = place_rows(index, source_device, this_device - offset, start)
        pieces.append(arrived)
        start = start + MOVE
    candidates = jnp.concatenate(pieces, axis=0)
    gathered = candidates[jnp.maximum(index, 0)]
    return jnp.where((index >= 0)[:, None], gathered, jnp.zeros_like(gathered))


def general(concentration, neighbours, source_slot, mobility, fermi_gain, rates):
    capacity = concentration.shape[0]
    cells = concentration.shape[2]
    column_index = lax.axis_index("gx")
    row_index = lax.axis_index("gy")
    rows_count = lax.axis_size("gy")
    this_device = column_index * rows_count + row_index
    blocks = concentration.reshape(capacity, SPECIES, B, B, B)
    own_faces = faces_of(blocks).reshape(1, 1, capacity, 6, SPECIES, B * B)
    face_table = with_halo(own_faces, (("gx", 0), ("gy", 1)), 1)
    requests = with_halo(source_slot.reshape(1, 1, capacity), (("gx", 0), ("gy", 1)), 1)
    ghosts = gather_ghosts(face_table, neighbours, column_index, row_index, rows_count, capacity)
    working = KEEP - 1 + MOVE
    payload = jnp.concatenate(
        [
            concentration.reshape(capacity, SPECIES * cells),
            ghosts.reshape(capacity, 6 * SPECIES * B * B),
        ],
        axis=1,
    )
    arrived = relocate(payload, source_slot, requests, this_device, rows_count, capacity)[:working]
    current = arrived[:, : SPECIES * cells].reshape(working, SPECIES, B, B, B)
    layers = arrived[:, SPECIES * cells :].reshape(working, 6, SPECIES, B, B)
    swept = smooth_all(current, layers, mobility, fermi_gain, rates).reshape(
        working, SPECIES, cells
    )
    live_rows = (source_slot[:working] >= 0)[:, None, None]
    swept = jnp.where(live_rows, swept, jnp.zeros_like(swept))
    return jnp.concatenate(
        [swept, jnp.zeros((capacity - working, SPECIES, cells), jnp.float32)], axis=0
    )


def body(nx, ny, concentration, neighbours, source_slot, mobility, fermi_gain, rates):
    source = source_slot.reshape(1, CAP)
    conc = concentration.transpose(1, 0, 2)
    landp, landz, landq, landg, swept, flag = exchange(nx, ny, conc, neighbours, source, mobility, fermi_gain, rates)

    def common():
        return smooth(nx, ny, landp, landz, landq, landg, swept, source, mobility, fermi_gain, rates).transpose(1, 0, 2)

    def crowded():
        return general(concentration, neighbours, source_slot, mobility, fermi_gain, rates)

    return lax.cond(flag[0, 0] == 0, common, crowded)


def solution(mesh):
    placed = (P(("gx", "gy"), None, None), P(("gx", "gy"), None), P(("gx", "gy")), P(), P(), P())
    return jax.shard_map(
        functools.partial(body, mesh.shape["gx"], mesh.shape["gy"]),
        mesh=mesh, in_specs=placed, out_specs=P(("gx", "gy"), None, None), check_vma=False,
    )
```
